128 devices in a mesh: pair: 8 (over z, y_lo), tile: 16 (over y_hi, x, core).
Axes of the slice: x: 4, y: 4 (y_hi: 2, y_lo: 2; y = y_hi * 2 + y_lo), z: 4, core: 2. Of those that a mesh axis runs over, the one named last changes fastest.
Arguments:
- phases: bfloat16 [1536, 131072], P(('pair', 'tile')), may hold values from -5 to 5
- pair_dates: int32 [1536, 2], replicated, may hold values from 0 to 303, as said below
- weights: float32 [2, 1536], replicated, may hold values from 0.25 to 4
- coords: int32 [2, 131072], P(None, ('pair', 'tile')), may hold values from 0 to 4095, as said below
Outputs:
- coefficients: float32 [32, 131072], P(None, ('pair', 'tile'))
- screens: float32 [304, 256], P('pair')
The draws below stay inside these ranges and needn't reach their ends.
Inputs may be any that keep to these rules, and one draw needn't show every extreme that they name: `pair_dates`: in every row the first date is earlier than the second, at most 15 dates before it. `coords`: pixel b * 1024 + j with j < 512 has its row among the 512 rows of band b // 16 and its column among the 256 columns of band b % 16; the other pixels lie anywhere in the frame.
All inputs are finite; a program needn't handle non-finite values.
Results may differ from the reference program's by a relative error of at most 0.006.
Values may be sent and summed in bfloat16 or wider, within the bound.
A program may use at most 128 MiB of HBM per device.

```python
import math
import jax
import jax.numpy as jnp
from jax import lax

K = 1536
DATES = 304
NB = 32
KNOTS = 16
FRAME = 4096
ITERS = 2
PIX_DEV = 1024
SCREEN = 256
NPIX = 131072
N_PAIR = 8
N_TILE = 16


def pixel_coords(key):
    position = jnp.arange(NPIX, dtype=jnp.int32)
    device_block = position // PIX_DEV
    within = position % PIX_DEV
    band_rows = FRAME // N_PAIR
    band_cols = FRAME // N_TILE
    row_start = device_block // N_TILE * band_rows
    col_start = device_block % N_TILE * band_cols
    key_list = jax.random.split(key, 4)
    local_rows = row_start + jax.random.randint(key_list[0], (NPIX,), 0, band_rows)
    local_cols = col_start + jax.random.randint(key_list[1], (NPIX,), 0, band_cols)
    spread_rows = jax.random.randint(key_list[2], (NPIX,), 0, FRAME)
    spread_cols = jax.random.randint(key_list[3], (NPIX,), 0, FRAME)
    nearby = within < PIX_DEV // 2
    pixel_rows = jnp.where(nearby, local_rows, spread_rows)
    pixel_cols = jnp.where(nearby, local_cols, spread_cols)
    pixel_rows = jnp.where(position == NPIX - 1, FRAME - 1, pixel_rows)
    pixel_cols = jnp.where(position == NPIX - 1, FRAME - 1, pixel_cols)
    pixel_rows = jnp.where(position == 0, 0, pixel_rows)
    pixel_cols = jnp.where(position == 0, 0, pixel_cols)
    return jnp.stack([pixel_rows, pixel_cols]).astype(jnp.int32)


def draw_coords(key, part):
    return pixel_coords(key)


def draw_phases(key, part):
    coords = pixel_coords(key)
    key = jax.random.fold_in(key, 11)
    key_list = jax.random.split(key, 6)
    row_frac = coords[0].astype(jnp.float32) / FRAME
    col_frac = coords[1].astype(jnp.float32) / FRAME
    amplitude = jax.random.uniform(key_list[0], (K, 1), jnp.float32, 0.5, 1.5)
    noise_part = 0.7 * jnp.clip(jax.random.normal(key_list[5], (K, NPIX), jnp.float32), -4.5, 4.5)
    freq_rows = jax.random.uniform(key_list[1], (K, 1), jnp.float32, -1.5, 1.5)
    freq_cols = jax.random.uniform(key_list[2], (K, 1), jnp.float32, -1.5, 1.5)
    shift = jax.random.uniform(key_list[3], (K, 1), jnp.float32, -math.pi, math.pi)
    smooth = amplitude * jnp.cos(2.0 * math.pi * (freq_rows * row_frac[None, :] + freq_cols * col_frac[None, :]) + shift)
    return (smooth + noise_part).astype(jnp.float32).astype(jnp.bfloat16)


def draw_pair_dates(key, part):
    key = jax.random.fold_in(key, 5)
    key_list = jax.random.split(key, 2)
    spacing = jax.random.randint(key_list[0], (K,), 1, 16)
    anchor = jax.random.randint(key_list[1], (K,), 0, DATES)
    earlier = anchor % (DATES - spacing)
    pair_index = jnp.arange(K, dtype=jnp.int32)
    earlier = jnp.where(pair_index == 0, DATES - 16, earlier)
    spacing = jnp.where(pair_index == 0, 15, spacing)
    earlier = jnp.where(pair_index == 1, 0, earlier)
    return jnp.stack([earlier, earlier + spacing], axis=1).astype(jnp.int32)


def setup_inputs(seed: int = 0) -> dict:
    keys = jax.random.split(jax.random.key(seed), 5)
    phases = draw_phases(jax.random.fold_in(keys[4], 71), 0)
    pair_dates = draw_pair_dates(jax.random.fold_in(keys[4], 71), 0)
    weights = jnp.clip(jnp.exp(jax.random.uniform(keys[2], (ITERS, K), jnp.float32, math.log(0.25), math.log(4.0))), 0.25, 4.0)
    coords = draw_coords(jax.random.fold_in(keys[4], 71), 0)
    return dict(phases=phases, pair_dates=pair_dates, weights=weights, coords=coords)


fit_ridge = 0.5
date_ridge = 1.0
knot_ridge = 1.0

def spline_rows(positions, basis_count):
    centers = jnp.arange(basis_count).astype(jnp.float32) - 1.0
    offset = jnp.abs(positions[None, :] - centers[:, None])
    near_part = 2.0 / 3.0 - offset * offset + 0.5 * offset * offset * offset
    remain = jnp.maximum(2.0 - offset, 0.0)
    return jnp.where(offset < 1.0, near_part, remain * remain * remain / 6.0)

def pair_setup(pair_dates, weights):
    date_axis = jnp.arange(DATES).astype(jnp.float32) * ((NB - 3.0) / (DATES - 1.0))
    temporal = spline_rows(date_axis, NB).T
    columns = jnp.arange(DATES).astype(jnp.int32)
    incidence = (columns[None, :] == pair_dates[:, 1:2]).astype(jnp.float32) - (columns[None, :] == pair_dates[:, 0:1]).astype(jnp.float32)
    design = jnp.dot(incidence, temporal, precision=lax.Precision.HIGHEST)
    fit_solves = []
    date_solves = []
    for iteration in range(ITERS):
        weight = weights[iteration]
        scaled = design * weight[:, None]
        normal = jnp.dot(design.T, scaled, precision=lax.Precision.HIGHEST) + fit_ridge * jnp.eye(NB, dtype=jnp.float32)
        factor = jnp.linalg.cholesky(normal)
        fit_solves.append(jax.scipy.linalg.cho_solve((factor, True), scaled.T).astype(jnp.bfloat16))
        weighted = incidence * weight[:, None]
        date_normal = jnp.dot(incidence.T, weighted, precision=lax.Precision.HIGHEST) + date_ridge * jnp.eye(DATES, dtype=jnp.float32)
        date_factor = jnp.linalg.cholesky(date_normal)
        date_solves.append(jax.scipy.linalg.cho_solve((date_factor, True), weighted.T).astype(jnp.bfloat16))
    return (design, fit_solves, date_solves)

def knot_basis(coords):
    scaled = coords.astype(jnp.float32) * ((KNOTS - 3.0) / FRAME)
    row_part = spline_rows(scaled[0], KNOTS)
    col_part = spline_rows(scaled[1], KNOTS)
    return (row_part[:, None, :] * col_part[None, :, :]).reshape(KNOTS * KNOTS, -1)

def fit_pass(corrected, fit_solve, date_solve, design):
    coeffs = jnp.dot(fit_solve.astype(jnp.float32), corrected.astype(jnp.float32), preferred_element_type=jnp.float32)
    fitted = jnp.dot(design, coeffs, precision=lax.Precision.HIGHEST)
    residual = (corrected.astype(jnp.float32) - fitted).astype(jnp.bfloat16)
    date_field = jnp.dot(date_solve.astype(jnp.float32), residual.astype(jnp.float32), preferred_element_type=jnp.float32).astype(jnp.bfloat16)
    return (coeffs, date_field)

def reference(phases, pair_dates, weights, coords):
    design, fit_solves, date_solves = pair_setup(pair_dates, weights)
    block_count = NPIX // PIX_DEV
    numbers = jnp.arange(block_count, dtype=jnp.int32)

    def gram_block(number):
        first_pixel = (number * PIX_DEV).astype(jnp.int32)
        knot_block = knot_basis(lax.dynamic_slice_in_dim(coords, first_pixel, PIX_DEV, 1))
        return jnp.dot(knot_block, knot_block.T, precision=lax.Precision.HIGHEST)
    gram_total = jnp.sum(lax.map(gram_block, numbers), axis=0) + knot_ridge * jnp.eye(SCREEN, dtype=jnp.float32)
    factor = jnp.linalg.cholesky(gram_total)
    screens = jnp.zeros((DATES, SCREEN), jnp.float32)
    coeff_blocks = None
    for iteration in range(ITERS):
        screen_bf = screens.astype(jnp.bfloat16)

        def pass_block(number):
            first_pixel = (number * PIX_DEV).astype(jnp.int32)
            knot_block = knot_basis(lax.dynamic_slice_in_dim(coords, first_pixel, PIX_DEV, 1)).astype(jnp.bfloat16)
            block_data = lax.dynamic_slice_in_dim(phases, first_pixel, PIX_DEV, 1)
            if iteration == 0:
                corrected = block_data
            else:
                screen_field = jnp.dot(screen_bf.astype(jnp.float32), knot_block.astype(jnp.float32), preferred_element_type=jnp.float32)
                shifts = jnp.take(screen_field, pair_dates[:, 1], axis=0) - jnp.take(screen_field, pair_dates[:, 0], axis=0)
                corrected = (block_data.astype(jnp.float32) - shifts).astype(jnp.bfloat16)
            coeffs, date_field = fit_pass(corrected, fit_solves[iteration], date_solves[iteration], design)
            partial_value = lax.dot_general(date_field.astype(jnp.float32), knot_block.astype(jnp.float32), (((1,), (1,)), ((), ())), preferred_element_type=jnp.float32)
            return (coeffs, partial_value)
        coeff_blocks, partials = lax.map(pass_block, numbers)
        totals = jnp.sum(partials, axis=0)
        screens = screens + jax.scipy.linalg.cho_solve((factor, True), totals.T).T
    coefficients = jnp.transpose(coeff_blocks, (1, 0, 2)).reshape(NB, NPIX)
    return (coefficients, screens)
```

```python
import functools

import jax
import jax.numpy as jnp
from jax import lax
from jax.experimental import pallas as pl
from jax.experimental.pallas import tpu as pltpu
from jax.sharding import PartitionSpec as P

MESH = pl.DeviceIdType.MESH
HI = lax.Precision.HIGHEST
F32, BF16 = jnp.float32, jnp.bfloat16
DATES, NB, KNOTS, FRAME, SCREEN = 304, 32, 16, 4096, 256
PAIRS, SLOTS, DEVICES, PIX = 12, 16, 128, 1024
N_TILE = 16
EVEN, ODD = 160, 144
KP = SLOTS * DEVICES
OWN = 40
VMEM_LIMIT = 60 * 1024 * 1024

def nn(a, b, precision=None):
    return lax.dot_general(a, b, (((1,), (0,)), ((), ())), precision=precision, preferred_element_type=F32)

def nt(a, b, precision=None):
    return lax.dot_general(a, b, (((1,), (1,)), ((), ())), precision=precision, preferred_element_type=F32)

def split2(x):
    hi = x.astype(BF16)
    return hi, (x - hi.astype(F32)).astype(BF16)

def spline(s):
    a = jnp.abs(s)
    r = jnp.maximum(2.0 - a, 0.0)
    q = jnp.maximum(1.0 - a, 0.0)
    return (r * r * r - 4.0 * (q * q * q)) * (1.0 / 6.0)

def date_of(r):
    rr = jnp.where(r < EVEN, r, r - EVEN)
    base = ((rr >> 4) << 5) + (rr & 15)
    return jnp.where(r < EVEN, base, base + 16)

def iota(shape, dim):
    return lax.broadcasted_iota(jnp.int32, shape, dim)

def block_inverse(c):
    n = c.shape[1]
    row = iota((1, n, n), 1)
    col = iota((1, n, n), 2)
    for j in range(n):
        prow = c[:, j:j + 1, :]
        pcol = c[:, :, j:j + 1]
        d = 1.0 / c[:, j:j + 1, j:j + 1]
        newrow = jnp.where(col[:, :1, :] == j, 1.0, prow) * d
        base = jnp.where(col == j, 0.0, c)
        c = jnp.where(row == j, newrow, base - pcol * newrow)
    return c

def newton(mats, floors, steps):
    xs, lows = [], []
    for m, floor in zip(mats, floors):
        n = m.shape[0]
        top = jnp.max(jnp.sum(jnp.abs(m), axis=1, keepdims=True), axis=0, keepdims=True)
        eye = (iota((n, n), 0) == iota((n, n), 1)).astype(F32)
        xs.append(eye * (2.0 / (top + floor)))
        lows.append(2.0 * floor / (top + floor))
    def body(_, carry):
        xs, lows = carry
        nx, nl = [], []
        ys = [nn(m, x, HI) for m, x in zip(mats, xs)]
        for x, y, low in zip(xs, ys, lows):
            n = x.shape[0]
            ab = low * (2.0 - low)
            k = 2.0 / (1.0 + ab)
            eye2 = jnp.where(iota((n, n), 0) == iota((n, n), 1), 2.0, 0.0)
            nx.append(nn(x, eye2 - y, HI) * k)
            nl.append(ab * k)
        return nx, nl
    xs, lows = lax.fori_loop(0, steps, body, (xs, lows))
    return xs

def own_dates(pair):
    row, col = iota((OWN, DATES), 0), iota((OWN, DATES), 1)
    return jnp.where((pair * 38 + row == date_of(col)) & (row < 38), 1.0, 0.0)

def setup_math(pd, w, pair):
    t = date_of(iota((DATES, KP), 0))
    at = (jnp.where(t == pd[1:2, :], 1.0, 0.0) - jnp.where(t == pd[0:1, :], 1.0, 0.0))
    at16 = at.astype(BF16)
    tt = date_of(iota((DATES, NB), 0)).astype(F32) * ((NB - 3.0) / (DATES - 1.0))
    temporal = spline(tt - (iota((DATES, NB), 1).astype(F32) - 1.0))
    t1 = temporal.T
    a = t1.astype(BF16); r = t1 - a.astype(F32)
    b = r.astype(BF16); c = (r - b.astype(F32)).astype(BF16)
    xt = nn(a, at16) + nn(b, at16) + nn(c, at16)
    xs, ys, es, ns = [], [], [], []
    pis = []
    eyeN = jnp.where(iota((DATES, DATES), 0) == iota((DATES, DATES), 1), 1.0, 0.0)
    fold = jnp.where((iota((EVEN, 16), 0) & 15) == iota((EVEN, 16), 1), 1.0, 0.0)
    blockmask = (iota((EVEN, EVEN), 0) >> 4) == (iota((EVEN, EVEN), 1) >> 4)
    comps = []
    fn = []
    for i in range(2):
        wi = w[i:i + 1, :]
        whi, wlo = split2(wi)
        n = nt((at * whi.astype(F32)).astype(BF16), at16) + nt((at * wlo.astype(F32)).astype(BF16), at16) + eyeN
        ns.append(n)
        p = n[:EVEN, :EVEN]
        comps.append(nn(jnp.where(blockmask, p, 0.0), fold, HI).reshape(10, 16, 16))
        fn.append(nt(xt * wi, xt, HI) + 0.5 * jnp.where(iota((NB, NB), 0) == iota((NB, NB), 1), 1.0, 0.0))
    inv = block_inverse(jnp.concatenate(comps, axis=0))
    schurs, yy = [], []
    for i in range(2):
        ci = inv[10 * i:10 * i + 10].reshape(EVEN, 16)
        pi = jnp.where(blockmask, nt(ci, fold, HI), 0.0)
        e = ns[i][:EVEN, EVEN:]
        y = nn(pi, e, HI)
        s = ns[i][EVEN:, EVEN:] - lax.dot_general(e, y, (((0,), (0,)), ((), ())), precision=HI, preferred_element_type=F32)
        pis.append(pi); yy.append(y); schurs.append(s)
    s0, s1, f0, f1 = newton([schurs[0], schurs[1], fn[0], fn[1]], [1.0, 1.0, 0.5, 0.5], 11)
    fs = [nn(f0, xt * w[0:1, :], HI).astype(BF16), nn(f1, xt * w[1:2, :], HI).astype(BF16)]
    out = []
    sel = own_dates(pair)
    ninv = []
    for i, si in enumerate((s0, s1)):
        ysi = nn(yy[i], si, HI)
        tl = pis[i] + nt(ysi, yy[i], HI)
        top = jnp.concatenate([tl, -ysi], axis=1)
        bot = jnp.concatenate([-ysi.T, si], axis=1)
        ninv.append(jnp.concatenate([top, bot], axis=0))
    def dsolve(m, wi):
        hi, lo = split2(m)
        return ((nn(hi, at16) + nn(lo, at16)) * wi).astype(BF16)
    d0 = dsolve(ninv[0], w[0:1, :])
    d1 = dsolve(nn(sel, ninv[1], HI), w[1:2, :])
    xhi, xlo = split2(xt)
    c0 = nt(d0, xhi) + nt(d0, xlo)
    c1 = nt(d1, xhi) + nt(d1, xlo)
    fa1 = nt(fs[1], at16)
    da1 = nt(d1, at16)
    lhs = jnp.concatenate([fs[0], fs[1], d0, d1], axis=0)
    return lhs, c0, c1, fa1, da1, sel

def tail_math(lhs, c0, c1, fa1, da1, sel, zall, g):
    (h,) = newton([g], [1.0], 12)
    zhi, zlo = split2(zall)
    lz = nn(lhs, zhi) + nn(lhs, zlo)
    f0z, f1z, d0z, d1z = lz[0:32], lz[32:64], lz[64:64 + DATES], lz[64 + DATES:]
    w0 = d0z - nn(c0, f0z, HI)
    s1 = nn(w0, h, HI)
    v = w0 - s1
    fz1 = f1z - nn(fa1, v, HI)
    dz1 = d1z - nn(da1, v, HI)
    w1 = dz1 - nn(c1, fz1, HI)
    s2 = nn(sel, s1, HI) + nn(w1, h, HI)
    e = nn(fa1, s1, HI)
    return e, s2


def setup_kernel(pd_ref, w_ref, lhs_ref, c0_ref, c1_ref, fa1_ref, da1_ref):
    lhs, c0, c1, fa1, da1, _ = setup_math(pd_ref[...], w_ref[...], lax.axis_index("pair"))
    lhs_ref[...] = lhs
    c0_ref[...] = c0
    c1_ref[...] = c1
    fa1_ref[...] = fa1
    da1_ref[...] = da1


def device_of(index):
    return (index // N_TILE, index % N_TILE)


def exchange_kernel(
    ph_ref, ck_ref, y_ref, z_ref, g_ref,
    ypad, cscr, bscr, lscr, zown, gown,
    c_send, c_recv, y_send, y_recv, z_send, z_recv, g_send, g_recv, own_sem,
):
    pair, tile = lax.axis_index("pair"), lax.axis_index("tile")
    me = pair * N_TILE + tile

    def peer(i):
        return lax.rem(me + i, DEVICES)

    barrier = pltpu.get_barrier_semaphore()

    def greet(i, _):
        pl.semaphore_signal(barrier, inc=1, device_id=device_of(peer(i)), device_id_type=MESH)
        return 0

    lax.fori_loop(1, DEVICES, greet, 0)
    pl.semaphore_wait(barrier, DEVICES - 1)

    def c_copy(other, slot):
        return pltpu.make_async_remote_copy(
            src_ref=cscr.at[slot], dst_ref=cscr.at[slot],
            send_sem=c_send.at[other], recv_sem=c_recv.at[slot],
            device_id=device_of(other), device_id_type=MESH,
        )

    def y_copy(other, slot):
        return pltpu.make_async_remote_copy(
            src_ref=ypad.at[other], dst_ref=y_ref.at[slot],
            send_sem=y_send.at[other], recv_sem=y_recv.at[slot],
            device_id=device_of(other), device_id_type=MESH,
        )

    def z_copy(other, slot):
        return pltpu.make_async_remote_copy(
            src_ref=zown, dst_ref=z_ref.at[slot],
            send_sem=z_send.at[other], recv_sem=z_recv.at[slot],
            device_id=device_of(other), device_id_type=MESH,
        )

    def g_copy(other, slot):
        return pltpu.make_async_remote_copy(
            src_ref=gown, dst_ref=g_ref.at[slot],
            send_sem=g_send.at[other], recv_sem=g_recv.at[slot],
            device_id=(pair, other), device_id_type=MESH,
        )

    cscr[me] = ck_ref[...]

    def c_start(i, _):
        c_copy(peer(i), me).start()
        return 0

    lax.fori_loop(1, DEVICES, c_start, 0)

    def y_pack(other):
        block = ph_ref[:, pl.ds(pl.multiple_of(other * PIX, PIX), PIX)]
        ypad[other] = jnp.concatenate([block, jnp.zeros((SLOTS - PAIRS, PIX), BF16)], axis=0)

    def y_start(i, _):
        other = peer(i)
        y_pack(other)
        y_copy(other, me).start()
        return 0

    lax.fori_loop(1, DEVICES, y_start, 0)
    y_pack(me)
    own = pltpu.make_async_copy(ypad.at[me], y_ref.at[me], own_sem)
    own.start()

    shift = tile.astype(F32) - 1.0
    centers = iota((KNOTS, 1), 0).astype(F32) - 1.0

    def build(slot_of, buf):
        lscr[buf, 0:16] = ypad[slot_of]
        for i in range(PIX // 128):
            lanes = pl.ds(i * 128, 128)
            code = cscr[slot_of, i:i + 1, :]
            row = (code >> 16).astype(F32) * ((KNOTS - 3.0) / FRAME)
            col = (code & 65535).astype(F32) * ((KNOTS - 3.0) / FRAME)
            rows = spline(row - centers)
            cols = spline(col - centers)
            for m in range(KNOTS):
                bscr[buf, m * KNOTS:(m + 1) * KNOTS, lanes] = (rows[m:m + 1, :] * cols).astype(BF16)
            mine = spline(row - shift) * cols
            hi, lo = split2(mine)
            lscr[buf, 16:32, lanes] = hi
            lscr[buf, 32:48, lanes] = lo

    def c_wait(i):
        other = peer(i)
        c_copy(other, other).wait_recv()

    def product(buf):
        return nt(lscr[buf], bscr[buf])

    build(me, 0)

    def pass_body(k, acc):
        c_wait(2 * k + 1)
        c_wait(2 * k + 2)
        build(peer(2 * k + 1), 1)
        acc = acc + product(0)
        build(peer(2 * k + 2), 0)
        return acc + product(1)

    acc = lax.fori_loop(0, DEVICES // 2 - 1, pass_body, jnp.zeros((48, SCREEN), F32))
    c_wait(DEVICES - 1)
    build(peer(DEVICES - 1), 1)
    acc = acc + product(0)
    acc = acc + product(1)

    zown[...] = acc[0:16]
    gown[...] = acc[16:48]

    def z_start(i, _):
        z_copy(peer(i), me).start()
        return 0

    lax.fori_loop(1, DEVICES, z_start, 0)

    def g_start(i, _):
        g_copy(lax.rem(tile + i, N_TILE), tile).start()
        return 0

    lax.fori_loop(1, N_TILE, g_start, 0)
    z_ref[me] = acc[0:16]
    g_ref[tile] = acc[16:48]

    def g_wait(i, _):
        other = lax.rem(tile + i, N_TILE)
        g_copy(other, other).wait_recv()
        g_copy(other, tile).wait_send()
        return 0

    lax.fori_loop(1, N_TILE, g_wait, 0)

    def z_wait(i, _):
        other = peer(i)
        z_copy(other, other).wait_recv()
        z_copy(other, me).wait_send()
        c_copy(other, me).wait_send()
        return 0

    lax.fori_loop(1, DEVICES, z_wait, 0)

    def y_wait(i, _):
        other = peer(i)
        y_copy(other, other).wait_recv()
        y_copy(other, me).wait_send()
        return 0

    lax.fori_loop(1, DEVICES, y_wait, 0)
    own.wait()


def final_kernel(lhs_ref, c0_ref, c1_ref, fa1_ref, da1_ref, z_ref, g_ref, y_ref, ck_ref, co_ref, sc_ref, bscr):
    pair = lax.axis_index("pair")
    first = jnp.concatenate([g_ref[j, 0:16] for j in range(KNOTS)], axis=0)
    second = jnp.concatenate([g_ref[j, 16:32] for j in range(KNOTS)], axis=0)
    eye = jnp.where(iota((SCREEN, SCREEN), 0) == iota((SCREEN, SCREEN), 1), 1.0, 0.0)
    gram = first + second + second.T + eye
    sel = own_dates(pair)
    e, s2 = tail_math(
        lhs_ref[...], c0_ref[...], c1_ref[...], fa1_ref[...], da1_ref[...], sel,
        z_ref[...].reshape(KP, SCREEN), gram,
    )
    sc_ref[...] = s2[0:38]
    centers = iota((KNOTS, 1), 0).astype(F32) - 1.0
    for i in range(PIX // 128):
        lanes = pl.ds(i * 128, 128)
        code = ck_ref[i:i + 1, :]
        row = (code >> 16).astype(F32) * ((KNOTS - 3.0) / FRAME)
        col = (code & 65535).astype(F32) * ((KNOTS - 3.0) / FRAME)
        rows = spline(row - centers)
        cols = spline(col - centers)
        for m in range(KNOTS):
            bscr[m * KNOTS:(m + 1) * KNOTS, lanes] = (rows[m:m + 1, :] * cols).astype(BF16)
    ehi, elo = split2(e)
    screen_part = nn(ehi, bscr[...]) + nn(elo, bscr[...])
    fit = nn(lhs_ref[32:64, :], y_ref[...].reshape(KP, PIX))
    co_ref[...] = fit - screen_part


def local(phases, pair_dates, weights, coords):
    pd = jnp.pad(pair_dates.reshape(DEVICES, PAIRS, 2), ((0, 0), (0, SLOTS - PAIRS), (0, 0)), constant_values=-1)
    pd = pd.reshape(KP, 2).T
    w = jnp.pad(weights.reshape(2, DEVICES, PAIRS), ((0, 0), (0, 0), (0, SLOTS - PAIRS))).reshape(2, KP)
    codes = (coords[0] * 65536 + coords[1]).reshape(PIX // 128, 128)
    vmem = pl.BlockSpec(memory_space=pltpu.VMEM)
    anyspace = pl.BlockSpec(memory_space=pl.ANY)
    shape = jax.ShapeDtypeStruct
    lhs, c0, c1, fa1, da1 = pl.pallas_call(
        setup_kernel,
        out_shape=[
            shape((2 * NB + DATES + OWN, KP), BF16), shape((DATES, NB), F32), shape((OWN, NB), F32),
            shape((NB, DATES), F32), shape((OWN, DATES), F32),
        ],
        in_specs=[vmem] * 2,
        out_specs=[vmem] * 5,
        compiler_params=pltpu.CompilerParams(vmem_limit_bytes=VMEM_LIMIT),
        name="setup",
    )(pd, w)
    dma = pltpu.SemaphoreType.DMA
    y, z, g = pl.pallas_call(
        exchange_kernel,
        out_shape=[
            shape((DEVICES, SLOTS, PIX), BF16), shape((DEVICES, SLOTS, SCREEN), F32),
            shape((N_TILE, 32, SCREEN), F32),
        ],
        in_specs=[vmem] * 2,
        out_specs=[anyspace, vmem, vmem],
        scratch_shapes=[
            pltpu.VMEM((DEVICES, SLOTS, PIX), BF16),
            pltpu.VMEM((DEVICES, PIX // 128, 128), jnp.int32),
            pltpu.VMEM((2, SCREEN, PIX), BF16),
            pltpu.VMEM((2, 48, PIX), BF16),
            pltpu.VMEM((SLOTS, SCREEN), F32),
            pltpu.VMEM((32, SCREEN), F32),
            dma((DEVICES,)), dma((DEVICES,)), dma((DEVICES,)), dma((DEVICES,)),
            dma((DEVICES,)), dma((DEVICES,)), dma((N_TILE,)), dma((N_TILE,)), dma,
        ],
        compiler_params=pltpu.CompilerParams(
            collective_id=0, has_side_effects=True, vmem_limit_bytes=VMEM_LIMIT
        ),
        name="exchange",
    )(phases, codes)
    co, sc = pl.pallas_call(
        final_kernel,
        out_shape=[shape((NB, PIX), F32), shape((38, SCREEN), F32)],
        in_specs=[vmem] * 9,
        out_specs=[vmem] * 2,
        scratch_shapes=[pltpu.VMEM((SCREEN, PIX), BF16)],
        compiler_params=pltpu.CompilerParams(vmem_limit_bytes=VMEM_LIMIT),
        name="final",
    )(lhs, c0, c1, fa1, da1, z, g, y, codes)
    return co, sc


def solution(mesh):
    return jax.shard_map(
        local,
        mesh=mesh,
        in_specs=(P(("pair", "tile"), None), P(), P(), P(None, ("pair", "tile"))),
        out_specs=(P(None, ("pair", "tile")), P("pair", None)),
        check_vma=False,
    )
```

```python
import functools

import jax
import jax.numpy as jnp
from jax import lax
from jax.experimental import pallas as pl
from jax.experimental.pallas import tpu as pltpu
from jax.sharding import PartitionSpec as P

MESH = pl.DeviceIdType.MESH
HI = lax.Precision.HIGHEST
F32, BF16 = jnp.float32, jnp.bfloat16
DATES, NB, KNOTS, FRAME, SCREEN = 304, 32, 16, 4096, 256
PAIRS, SLOTS, DEVICES, PIX = 12, 16, 128, 1024
N_TILE = 16
EVEN, ODD = 160, 144
KP = SLOTS * DEVICES
OWN = 40
N_PAIR = 8
F0_AT, F1_AT, D1_AT, ROWS = 384, 416, 448, 512
VMEM_LIMIT = 60 * 1024 * 1024

def nn(a, b, precision=None):
    return lax.dot_general(a, b, (((1,), (0,)), ((), ())), precision=precision, preferred_element_type=F32)

def nt(a, b, precision=None):
    return lax.dot_general(a, b, (((1,), (1,)), ((), ())), precision=precision, preferred_element_type=F32)

def tn(a, b, precision=None):
    return lax.dot_general(a, b, (((0,), (0,)), ((), ())), precision=precision, preferred_element_type=F32)

def split2(x):
    hi = x.astype(BF16)
    return hi, (x - hi.astype(F32)).astype(BF16)

def spline(s):
    a = jnp.abs(s)
    r = jnp.maximum(2.0 - a, 0.0)
    q = jnp.maximum(1.0 - a, 0.0)
    return (r * r * r - 4.0 * (q * q * q)) * (1.0 / 6.0)

def date_of(r):
    rr = jnp.where(r < EVEN, r, r - EVEN)
    base = ((rr >> 4) << 5) + (rr & 15)
    return jnp.where(r < EVEN, base, base + 16)

def iota(shape, dim):
    return lax.broadcasted_iota(jnp.int32, shape, dim)

def block_inverse(c):
    n = c.shape[1]
    row = iota((1, n, n), 1)
    col = iota((1, n, n), 2)
    for j in range(n):
        prow = c[:, j:j + 1, :]
        pcol = c[:, :, j:j + 1]
        d = 1.0 / c[:, j:j + 1, j:j + 1]
        newrow = jnp.where(col[:, :1, :] == j, 1.0, prow) * d
        base = jnp.where(col == j, 0.0, c)
        c = jnp.where(row == j, newrow, base - pcol * newrow)
    return c

def product3(a, b):
    (ah, al), (bh, bl) = a, b
    return nn(ah, bh) + (nn(ah, bl) + nn(al, bh))

def newton(mats, floors, steps):
    xs, lows, parts, eyes = [], [], [], []
    for m, floor in zip(mats, floors):
        n = m.shape[0]
        top = jnp.max(jnp.sum(jnp.abs(m), axis=1, keepdims=True), axis=0, keepdims=True)
        diagonal = iota((n, n), 0) == iota((n, n), 1)
        xs.append(jnp.where(diagonal, 2.0 / (top + floor), 0.0))
        lows.append(2.0 * floor / (top + floor))
        parts.append(split2(m))
        eyes.append(jnp.where(diagonal, 2.0, 0.0))
    def body(_, carry):
        xs, lows = carry
        nx, nl = [], []
        halves = [split2(x) for x in xs]
        ys = [product3(m, x) for m, x in zip(parts, halves)]
        for x, y, eye, low in zip(halves, ys, eyes, lows):
            ab = low * (2.0 - low)
            k = 2.0 / (1.0 + ab)
            nx.append(product3(x, split2(eye - y)) * k)
            nl.append(ab * k)
        return nx, nl
    xs, lows = lax.fori_loop(0, steps, body, (xs, lows))
    out = []
    for m, x, eye in zip(mats, xs, eyes):
        out.append(nn(x, eye - nn(m, x, HI), HI))
    return out

def own_dates(pair):
    row, col = iota((OWN, DATES), 0), iota((OWN, DATES), 1)
    return jnp.where((pair * 38 + row == date_of(col)) & (row < 38), 1.0, 0.0)

def incidence_rows(pd):
    t = date_of(iota((DATES, KP), 0))
    later = jnp.where(t == pd[1:2, :], 1.0, 0.0)
    return later - jnp.where(t == pd[0:1, :], 1.0, 0.0)

def design_rows(at16):
    tt = date_of(iota((DATES, NB), 0)).astype(F32) * ((NB - 3.0) / (DATES - 1.0))
    t1 = spline(tt - (iota((DATES, NB), 1).astype(F32) - 1.0)).T
    a = t1.astype(BF16)
    r = t1 - a.astype(F32)
    b, c = split2(r)
    return nn(a, at16) + nn(b, at16) + nn(c, at16)

def normal_parts(at, at16, xt, w):
    eye = jnp.where(iota((DATES, DATES), 0) == iota((DATES, DATES), 1), 1.0, 0.0)
    fold = jnp.where((iota((EVEN, 16), 0) & 15) == iota((EVEN, 16), 1), 1.0, 0.0)
    mask = (iota((EVEN, EVEN), 0) >> 4) == (iota((EVEN, EVEN), 1) >> 4)
    ns, comps, fits = [], [], []
    for i in range(2):
        wi = w[i:i + 1, :]
        hi, lo = split2(wi)
        n = nt((at * hi.astype(F32)).astype(BF16), at16) + nt((at * lo.astype(F32)).astype(BF16), at16) + eye
        ns.append(n)
        comps.append(nn(jnp.where(mask, n[:EVEN, :EVEN], 0.0), fold, HI).reshape(10, 16, 16))
        fits.append(nt(xt * wi, xt, HI) + jnp.where(iota((NB, NB), 0) == iota((NB, NB), 1), 0.5, 0.0))
    inv = block_inverse(jnp.concatenate(comps, axis=0))
    firsts, links, schurs = [], [], []
    for i in range(2):
        compact = inv[10 * i:10 * i + 10].reshape(EVEN, 16)
        first = jnp.where(mask, nt(compact, fold, HI), 0.0)
        e = ns[i][:EVEN, EVEN:]
        y = nn(first, e, HI)
        schurs.append(ns[i][EVEN:, EVEN:] - tn(e, y, HI))
        firsts.append(first)
        links.append(y)
    return firsts, links, schurs, fits

def full_inverse(first, link, last):
    right = nn(link, last, HI)
    top = jnp.concatenate([first + nt(right, link, HI), -right], axis=1)
    bottom = jnp.concatenate([-right.T, last], axis=1)
    return jnp.concatenate([top, bottom], axis=0)

def date_solve(inverse, at16, wi):
    hi, lo = split2(inverse)
    return ((nn(hi, at16) + nn(lo, at16)) * wi).astype(BF16)

def knot_rows(code, centers):
    scale = (KNOTS - 3.0) / FRAME
    rows = spline((code >> 16).astype(F32) * scale - centers)
    cols = spline((code & 65535).astype(F32) * scale - centers)
    return rows, cols


def mega_kernel(
    ph_ref, ck_ref, pd_ref, w_ref, co_ref, sc_ref,
    cg, sb, rb, bhi, blo_ref, ybuf, gs, gr, gg, zs, zr, zg, wg, cp, cr, lhs,
    c_send, c_recv, y_send, y_recv, gs_send, gs_recv, gg_send, gg_recv,
    zs_send, zs_recv, zg_send, zg_recv, w_send, w_recv, f_send, f_recv,
):
    pair, tile = lax.axis_index("pair"), lax.axis_index("tile")

    def tile_peer(i):
        return lax.rem(tile + i, N_TILE)

    def pair_peer(i):
        return lax.rem(pair + i, N_PAIR)

    def loop(lo, hi, f):
        def body(i, carry):
            f(i)
            return carry
        lax.fori_loop(lo, hi, body, 0)

    def to_tile(src, dst, send, recv, other, slot):
        return pltpu.make_async_remote_copy(
            src_ref=src, dst_ref=dst.at[slot], send_sem=send.at[other], recv_sem=recv.at[slot],
            device_id=(pair, other), device_id_type=MESH,
        )

    def to_pair(src, dst, send, recv, other, slot):
        return pltpu.make_async_remote_copy(
            src_ref=src, dst_ref=dst.at[slot], send_sem=send.at[other], recv_sem=recv.at[slot],
            device_id=(other, tile), device_id_type=MESH,
        )

    def c_copy(other, slot):
        return to_pair(cg.at[pair], cg, c_send, c_recv, other, slot)

    def y_copy(other, slot):
        return to_tile(sb.at[other], rb, y_send, y_recv, other, slot)

    def gs_copy(other, slot):
        return to_tile(gs.at[other], gr, gs_send, gs_recv, other, slot)

    def gg_copy(other, slot):
        return to_tile(gg.at[tile], gg, gg_send, gg_recv, other, slot)

    def zs_copy(other, slot):
        return to_tile(zs.at[other], zr, zs_send, zs_recv, other, slot)

    def zg_copy(other, slot):
        return to_pair(zg.at[pair], zg, zg_send, zg_recv, other, slot)

    def w_copy(other, slot):
        return to_tile(wg.at[tile], wg, w_send, w_recv, other, slot)

    def f_copy(other, slot):
        return to_pair(cp.at[other], cr, f_send, f_recv, other, slot)

    def start_tile(copy):
        loop(1, N_TILE, lambda i: copy(tile_peer(i), tile).start())

    def start_pair(copy):
        loop(1, N_PAIR, lambda i: copy(pair_peer(i), pair).start())

    def wait_tile(copy):
        loop(1, N_TILE, lambda i: copy(tile_peer(i), tile_peer(i)).wait_recv())

    def wait_pair(copy):
        loop(1, N_PAIR, lambda i: copy(pair_peer(i), pair_peer(i)).wait_recv())

    barrier = pltpu.get_barrier_semaphore()
    loop(1, N_TILE, lambda i: pl.semaphore_signal(
        barrier, inc=1, device_id=(pair, tile_peer(i)), device_id_type=MESH))
    loop(1, N_PAIR, lambda i: pl.semaphore_signal(
        barrier, inc=1, device_id=(pair_peer(i), tile), device_id_type=MESH))
    pl.semaphore_wait(barrier, N_TILE + N_PAIR - 2)

    cg[pair] = ck_ref[...]
    start_pair(c_copy)

    def pack(other, dst):
        blocks = []
        for p in range(N_PAIR):
            first = pl.multiple_of((p * N_TILE + other) * PIX, PIX)
            blocks.append(ph_ref[:, pl.ds(first, PIX)].astype(F32))
        for a in range(4):
            two = jnp.concatenate([blocks[2 * a][0:8], blocks[2 * a + 1][0:8]], axis=0)
            dst[a] = two.astype(BF16)
        for a in range(2):
            four = jnp.concatenate([blocks[4 * a + q][8:12] for q in range(4)], axis=0)
            dst[4 + a] = four.astype(BF16)

    def y_start(i):
        other = tile_peer(i)
        pack(other, sb.at[other])
        y_copy(other, tile).start()

    loop(1, N_TILE, y_start)
    pack(tile, rb.at[tile])

    wait_pair(c_copy)
    centers = iota((KNOTS, 1), 0).astype(F32) - 1.0

    def knots(p, carry):
        g1, g2 = carry
        for i in range(PIX // 128):
            rows, cols = knot_rows(cg[p, i:i + 1, :], centers)
            lanes = pl.ds(i * 128, 128)
            for m in range(KNOTS):
                hi, lo = split2(rows[m:m + 1, :] * cols)
                bhi[p, m * KNOTS:(m + 1) * KNOTS, lanes] = hi
                blo_ref[m * KNOTS:(m + 1) * KNOTS, lanes] = lo
        hi = bhi[p]
        return g1 + nt(hi, hi), g2 + nt(hi, blo_ref[...])

    zero = jnp.zeros((SCREEN, SCREEN), F32)
    g1, g2 = lax.fori_loop(0, N_PAIR, knots, (zero, zero))
    gpart = (g1 + g2 + g2.T).reshape(N_TILE, KNOTS, SCREEN)
    gs[...] = gpart
    start_tile(gs_copy)
    gr[tile] = gs[tile]

    w = w_ref[...]
    at = incidence_rows(pd_ref[...])
    at16 = at.astype(BF16)
    xt = design_rows(at16)
    firsts, links, schurs, fits = normal_parts(at, at16, xt, w)

    wait_tile(gs_copy)
    gsum = gr[0]
    for t in range(1, N_TILE):
        gsum = gsum + gr[t]
    gg[tile] = gsum
    start_tile(gg_copy)
    wait_tile(gg_copy)
    gram = gg[...].reshape(SCREEN, SCREEN)
    gram = gram + jnp.where(iota((SCREEN, SCREEN), 0) == iota((SCREEN, SCREEN), 1), 1.0, 0.0)
    h, last0, last1, f0, f1 = newton([gram] + schurs + fits, [1.0, 1.0, 1.0, 0.5, 0.5], 11)
    sel = own_dates(pair)
    fit0 = nn(f0, xt * w[0:1, :], HI).astype(BF16)
    fit1 = nn(f1, xt * w[1:2, :], HI).astype(BF16)
    d0 = date_solve(full_inverse(firsts[0], links[0], last0), at16, w[0:1, :])
    d1 = date_solve(nn(sel, full_inverse(firsts[1], links[1], last1), HI), at16, w[1:2, :])
    lhs[0:DATES] = d0
    lhs[DATES:F0_AT] = jnp.zeros((F0_AT - DATES, KP), BF16)
    lhs[F0_AT:D1_AT] = jnp.concatenate([fit0, fit1], axis=0)
    lhs[D1_AT:ROWS] = jnp.concatenate([d1, jnp.zeros((ROWS - D1_AT - OWN, KP), BF16)], axis=0)
    xhi, xlo = split2(xt)
    c0 = nt(d0, xhi) + nt(d0, xlo)
    c1 = nt(d1, xhi) + nt(d1, xlo)
    fa1 = nt(fit1, at16)
    da1 = nt(d1, at16)

    def unpack(t):
        rest = [rb[t, 4 + a].astype(F32) for a in range(2)]
        for a in range(4):
            two = rb[t, a].astype(F32)
            for b in range(2):
                p = 2 * a + b
                low = rest[p // 4][4 * (p % 4):4 * (p % 4) + 4]
                block = jnp.concatenate([two[8 * b:8 * b + 8], low, jnp.zeros((4, PIX), F32)], axis=0)
                rows = pl.ds(pl.multiple_of(t * SLOTS, SLOTS), SLOTS)
                ybuf[p, rows, :] = block.astype(BF16)

    unpack(tile)

    def y_arrive(i):
        other = tile_peer(i)
        y_copy(other, other).wait_recv()
        unpack(other)

    loop(1, N_TILE, y_arrive)
    fit_own = lhs[F1_AT:D1_AT, pl.ds(pl.multiple_of(pair * SCREEN, SCREEN), SCREEN)]

    def z_body(p, acc):
        y = ybuf[p]
        cp[p] = nn(fit_own, y)
        return acc + nt(bhi[p], y)

    zt = lax.fori_loop(0, N_PAIR, z_body, zero)
    zs[...] = zt.reshape(N_TILE, KNOTS, SCREEN)
    start_tile(zs_copy)
    start_pair(f_copy)
    zr[tile] = zs[tile]
    cr[pair] = cp[pair]
    wait_tile(zs_copy)
    zsum = zr[0]
    for t in range(1, N_TILE):
        zsum = zsum + zr[t]
    zg[pair] = zsum
    start_pair(zg_copy)
    wait_pair(zg_copy)
    zrow = jnp.concatenate([zg[p] for p in range(N_PAIR)], axis=1)
    zhi, zlo = split2(zrow)
    both = nt(jnp.concatenate([zhi, zlo], axis=0), lhs[...])
    wg[tile] = both[0:KNOTS] + both[KNOTS:2 * KNOTS]
    start_tile(w_copy)
    wait_tile(w_copy)

    wt = wg[...].reshape(SCREEN, ROWS)
    w0 = wt[:, 0:DATES] - nt(wt[:, F0_AT:F1_AT], c0, HI)
    s1 = nn(h, w0, HI)
    e = nt(s1, fa1, HI).T
    v = w0 - s1
    fz1 = wt[:, F1_AT:D1_AT] - nt(v, fa1, HI)
    dz1 = wt[:, D1_AT:D1_AT + OWN] - nt(v, da1, HI)
    s2 = nt(s1, sel, HI) + nn(h, dz1 - nt(fz1, c1, HI), HI)
    sc_ref[...] = s2.T[0:38]
    wait_pair(f_copy)
    ehi, elo = split2(e)
    own_knots = bhi[pair]
    total = cr[0]
    for p in range(1, N_PAIR):
        total = total + cr[p]
    co_ref[...] = total - (nn(ehi, own_knots) + nn(elo, own_knots))

    def drain_tile(i):
        other = tile_peer(i)
        for copy in (y_copy, gs_copy, gg_copy, zs_copy, w_copy):
            copy(other, tile).wait_send()

    loop(1, N_TILE, drain_tile)

    def drain_pair(i):
        other = pair_peer(i)
        for copy in (c_copy, zg_copy, f_copy):
            copy(other, pair).wait_send()

    loop(1, N_PAIR, drain_pair)


def local(phases, pair_dates, weights, coords):
    pd = jnp.pad(pair_dates.reshape(DEVICES, PAIRS, 2), ((0, 0), (0, SLOTS - PAIRS), (0, 0)), constant_values=-1)
    pd = pd.reshape(KP, 2).T
    w = jnp.pad(weights.reshape(2, DEVICES, PAIRS), ((0, 0), (0, 0), (0, SLOTS - PAIRS))).reshape(2, KP)
    codes = (coords[0] * 65536 + coords[1]).reshape(PIX // 128, 128)
    vmem = pl.BlockSpec(memory_space=pltpu.VMEM)
    shape = jax.ShapeDtypeStruct
    dma = pltpu.SemaphoreType.DMA
    tiles, pairs = dma((N_TILE,)), dma((N_PAIR,))
    return pl.pallas_call(
        mega_kernel,
        out_shape=[shape((NB, PIX), F32), shape((38, SCREEN), F32)],
        in_specs=[vmem] * 4,
        out_specs=[vmem] * 2,
        scratch_shapes=[
            pltpu.VMEM((N_PAIR, PIX // 128, 128), jnp.int32),
            pltpu.VMEM((N_TILE, 6, SLOTS, PIX), BF16),
            pltpu.VMEM((N_TILE, 6, SLOTS, PIX), BF16),
            pltpu.VMEM((N_PAIR, SCREEN, PIX), BF16),
            pltpu.VMEM((SCREEN, PIX), BF16),
            pltpu.VMEM((N_PAIR, SCREEN, PIX), BF16),
            pltpu.VMEM((N_TILE, KNOTS, SCREEN), F32),
            pltpu.VMEM((N_TILE, KNOTS, SCREEN), F32),
            pltpu.VMEM((N_TILE, KNOTS, SCREEN), F32),
            pltpu.VMEM((N_TILE, KNOTS, SCREEN), F32),
            pltpu.VMEM((N_TILE, KNOTS, SCREEN), F32),
            pltpu.VMEM((N_PAIR, KNOTS, SCREEN), F32),
            pltpu.VMEM((N_TILE, KNOTS, ROWS), F32),
            pltpu.VMEM((N_PAIR, NB, PIX), F32),
            pltpu.VMEM((N_PAIR, NB, PIX), F32),
            pltpu.VMEM((ROWS, KP), BF16),
            pairs, pairs, tiles, tiles, tiles, tiles, tiles, tiles,
            tiles, tiles, pairs, pairs, tiles, tiles, pairs, pairs,
        ],
        compiler_params=pltpu.CompilerParams(
            collective_id=0, has_side_effects=True, vmem_limit_bytes=VMEM_LIMIT
        ),
        name="mega",
    )(phases, codes, pd, w)


def solution(mesh):
    return jax.shard_map(
        local,
        mesh=mesh,
        in_specs=(P(("pair", "tile"), None), P(), P(), P(None, ("pair", "tile"))),
        out_specs=(P(None, ("pair", "tile")), P("pair", None)),
        check_vma=False,
    )
```

```python
import functools

import jax
import jax.numpy as jnp
from jax import lax
from jax.experimental import pallas as pl
from jax.experimental.pallas import tpu as pltpu
from jax.sharding import PartitionSpec as P

MESH = pl.DeviceIdType.MESH
HI = lax.Precision.HIGHEST
F32, BF16 = jnp.float32, jnp.bfloat16
DATES, NB, KNOTS, FRAME, SCREEN = 304, 32, 16, 4096, 256
PAIRS, SLOTS, DEVICES, PIX = 12, 16, 128, 1024
N_TILE = 16
EVEN, ODD = 160, 144
KP = PAIRS * DEVICES
GROUP = PAIRS * N_TILE
OWN = 40
N_PAIR = 8
F0_AT, F1_AT, D1_AT, ROWS = 384, 416, 448, 512
VMEM_LIMIT = 60 * 1024 * 1024

def nn(a, b, precision=None):
    return lax.dot_general(a, b, (((1,), (0,)), ((), ())), precision=precision, preferred_element_type=F32)

def nt(a, b, precision=None):
    return lax.dot_general(a, b, (((1,), (1,)), ((), ())), precision=precision, preferred_element_type=F32)

def tn(a, b, precision=None):
    return lax.dot_general(a, b, (((0,), (0,)), ((), ())), precision=precision, preferred_element_type=F32)

def split2(x):
    hi = x.astype(BF16)
    return hi, (x - hi.astype(F32)).astype(BF16)

def spline(s):
    a = jnp.abs(s)
    r = jnp.maximum(2.0 - a, 0.0)
    q = jnp.maximum(1.0 - a, 0.0)
    return (r * r * r - 4.0 * (q * q * q)) * (1.0 / 6.0)

def date_of(r):
    rr = jnp.where(r < EVEN, r, r - EVEN)
    base = ((rr >> 4) << 5) + (rr & 15)
    return jnp.where(r < EVEN, base, base + 16)

def iota(shape, dim):
    return lax.broadcasted_iota(jnp.int32, shape, dim)

def block_inverse(c):
    n = c.shape[1]
    row = iota((1, n, n), 1)
    col = iota((1, n, n), 2)
    for j in range(n):
        prow = c[:, j:j + 1, :]
        pcol = c[:, :, j:j + 1]
        d = 1.0 / c[:, j:j + 1, j:j + 1]
        newrow = jnp.where(col[:, :1, :] == j, 1.0, prow) * d
        base = jnp.where(col == j, 0.0, c)
        c = jnp.where(row == j, newrow, base - pcol * newrow)
    return c

def product3(a, b):
    (ah, al), (bh, bl) = a, b
    return nn(ah, bh) + (nn(ah, bl) + nn(al, bh))

def p3(a, b):
    return product3(split2(a), split2(b))

def p3t(a, b):
    (ah, al), (bh, bl) = split2(a), split2(b)
    return nt(ah, bh) + (nt(ah, bl) + nt(al, bh))

def newton_start(mats, floors):
    xs, lows = [], []
    for m, floor in zip(mats, floors):
        n = m.shape[0]
        top = jnp.max(jnp.sum(jnp.abs(m), axis=1, keepdims=True), axis=0, keepdims=True)
        c = 2.0 / (top + floor)
        low = c * floor
        ab = low * (2.0 - low)
        k = 2.0 / (1.0 + ab)
        diagonal = iota((n, n), 0) == iota((n, n), 1)
        xs.append((jnp.where(diagonal, 2.0, 0.0) - m * c) * (c * k))
        lows.append(ab * k)
    return xs, lows

def newton_steps(mats, state, steps):
    parts = [split2(m) for m in mats]
    def body(_, carry):
        xs, lows = carry
        nx, nl = [], []
        halves = [split2(x) for x in xs]
        ys = [product3(m, x) for m, x in zip(parts, halves)]
        for x, y, low in zip(halves, ys, lows):
            n = y.shape[0]
            ab = low * (2.0 - low)
            k = 2.0 / (1.0 + ab)
            eye = jnp.where(iota((n, n), 0) == iota((n, n), 1), 2.0, 0.0)
            nx.append(product3(x, split2(eye - y)) * k)
            nl.append(ab * k)
        return nx, nl
    return lax.fori_loop(0, steps, body, state)

def newton_end(mats, state):
    out = []
    for m, x in zip(mats, state[0]):
        n = m.shape[0]
        eye = jnp.where(iota((n, n), 0) == iota((n, n), 1), 2.0, 0.0)
        out.append(nn(x, eye - nn(m, x, HI), HI))
    return out

def own_dates(pair):
    row, col = iota((OWN, DATES), 0), iota((OWN, DATES), 1)
    return jnp.where((pair * 38 + row == date_of(col)) & (row < 38), 1.0, 0.0)

def incidence_rows(pd):
    unit = jnp.where(iota((8, 2), 0) == iota((8, 2), 1), 1.0, 0.0)
    row = nt(unit, pd.astype(F32), HI).astype(jnp.int32)
    t = date_of(iota((DATES, KP), 0))
    later = jnp.where(t == row[1:2, :], 1.0, 0.0)
    return later - jnp.where(t == row[0:1, :], 1.0, 0.0)

def design_rows(at16):
    tt = date_of(iota((DATES, NB), 0)).astype(F32) * ((NB - 3.0) / (DATES - 1.0))
    t1 = spline(tt - (iota((DATES, NB), 1).astype(F32) - 1.0)).T
    a = t1.astype(BF16)
    r = t1 - a.astype(F32)
    b, c = split2(r)
    return nn(a, at16) + nn(b, at16) + nn(c, at16)

def normal_parts(at, at16, xt, w):
    eye = jnp.where(iota((DATES, DATES), 0) == iota((DATES, DATES), 1), 1.0, 0.0)
    fold = jnp.where((iota((EVEN, 16), 0) & 15) == iota((EVEN, 16), 1), 1.0, 0.0)
    mask = (iota((EVEN, EVEN), 0) >> 4) == (iota((EVEN, EVEN), 1) >> 4)
    ns, comps, fits = [], [], []
    for i in range(2):
        wi = w[i:i + 1, :]
        hi, lo = split2(wi)
        n = nt((at * hi.astype(F32)).astype(BF16), at16) + nt((at * lo.astype(F32)).astype(BF16), at16) + eye
        ns.append(n)
        comps.append(nn(jnp.where(mask, n[:EVEN, :EVEN], 0.0), fold, HI).reshape(10, 16, 16))
        fits.append(nt(xt * wi, xt, HI) + jnp.where(iota((NB, NB), 0) == iota((NB, NB), 1), 0.5, 0.0))
    inv = block_inverse(jnp.concatenate(comps, axis=0))
    firsts, links, schurs = [], [], []
    for i in range(2):
        compact = inv[10 * i:10 * i + 10].reshape(EVEN, 16)
        first = jnp.where(mask, nt(compact, fold, HI), 0.0)
        e = ns[i][:EVEN, EVEN:]
        y = nn(first, e, HI)
        schurs.append(ns[i][EVEN:, EVEN:] - tn(e, y, HI))
        firsts.append(first)
        links.append(y)
    return firsts, links, schurs, fits

def full_inverse(first, link, last):
    right = p3(link, last)
    top = jnp.concatenate([first + p3t(right, link), -right], axis=1)
    bottom = jnp.concatenate([-right.T, last], axis=1)
    return jnp.concatenate([top, bottom], axis=0)

def date_solve(inverse, at16, wi):
    hi, lo = split2(inverse)
    return ((nn(hi, at16) + nn(lo, at16)) * wi).astype(BF16)

def spread_own(pair):
    row, col = iota((KP, SCREEN), 0), iota((KP, SCREEN), 1)
    inside = (col & 15) < PAIRS
    return jnp.where((row == GROUP * pair + PAIRS * (col >> 4) + (col & 15)) & inside, 1.0, 0.0).astype(BF16)

def squeeze():
    row, col = iota((SCREEN, SCREEN), 0), iota((SCREEN, SCREEN), 1)
    inside = (row & 15) < PAIRS
    return jnp.where((col == PAIRS * (row >> 4) + (row & 15)) & inside, 1.0, 0.0).astype(BF16)

def knot_rows(code, centers):
    scale = (KNOTS - 3.0) / FRAME
    rows = spline((code >> 16).astype(F32) * scale - centers)
    cols = spline((code & 65535).astype(F32) * scale - centers)
    return rows, cols


def mega_kernel(
    ph_ref, ck_ref, pd_ref, w_ref, co_ref, sc_ref,
    cg, sb, rb, bhi, blo_ref, ybuf, gs, gr, gg, zs, zr, zg, wg, cp, cr, lhs,
    c_send, c_recv, y_send, y_recv, gs_send, gs_recv, gg_send, gg_recv,
    zs_send, zs_recv, zg_send, zg_recv, w_send, w_recv, f_send, f_recv,
):
    pair, tile = lax.axis_index("pair"), lax.axis_index("tile")

    def tile_peer(i):
        return lax.rem(tile + i, N_TILE)

    def pair_peer(i):
        return lax.rem(pair + i, N_PAIR)

    def loop(lo, hi, f):
        def body(i, carry):
            f(i)
            return carry
        lax.fori_loop(lo, hi, body, 0)

    def to_tile(src, dst, send, recv, other, slot):
        return pltpu.make_async_remote_copy(
            src_ref=src, dst_ref=dst.at[slot], send_sem=send.at[other], recv_sem=recv.at[slot],
            device_id=(pair, other), device_id_type=MESH,
        )

    def to_pair(src, dst, send, recv, other, slot):
        return pltpu.make_async_remote_copy(
            src_ref=src, dst_ref=dst.at[slot], send_sem=send.at[other], recv_sem=recv.at[slot],
            device_id=(other, tile), device_id_type=MESH,
        )

    def c_copy(other, slot):
        return to_pair(cg.at[pair], cg, c_send, c_recv, other, slot)

    def y_copy(other, slot, part):
        return pltpu.make_async_remote_copy(
            src_ref=sb.at[other, part], dst_ref=rb.at[slot, part],
            send_sem=y_send.at[other, part], recv_sem=y_recv.at[slot, part],
            device_id=(pair, other), device_id_type=MESH,
        )

    def gs_copy(other, slot):
        return to_tile(gs.at[other], gr, gs_send, gs_recv, other, slot)

    def gg_copy(other, slot):
        return to_tile(gg.at[tile], gg, gg_send, gg_recv, other, slot)

    def zs_copy(other, slot):
        return to_tile(zs.at[other], zr, zs_send, zs_recv, other, slot)

    def zg_copy(other, slot):
        return to_pair(zg.at[pair], zg, zg_send, zg_recv, other, slot)

    def w_copy(other, slot):
        return to_tile(wg.at[tile], wg, w_send, w_recv, other, slot)

    def f_copy(other, slot):
        return to_pair(cp.at[other], cr, f_send, f_recv, other, slot)

    def start_tile(copy):
        loop(1, N_TILE, lambda i: copy(tile_peer(i), tile).start())

    def start_pair(copy):
        loop(1, N_PAIR, lambda i: copy(pair_peer(i), pair).start())

    def wait_tile(copy):
        loop(1, N_TILE, lambda i: copy(tile_peer(i), tile_peer(i)).wait_recv())

    def wait_pair(copy):
        loop(1, N_PAIR, lambda i: copy(pair_peer(i), pair_peer(i)).wait_recv())

    barrier = pltpu.get_barrier_semaphore()
    loop(1, N_TILE, lambda i: pl.semaphore_signal(
        barrier, inc=1, device_id=(pair, tile_peer(i)), device_id_type=MESH))
    loop(1, N_PAIR, lambda i: pl.semaphore_signal(
        barrier, inc=1, device_id=(pair_peer(i), tile), device_id_type=MESH))
    pl.semaphore_wait(barrier, N_TILE + N_PAIR - 2)

    code = ck_ref[0:1, :] * 65536 + ck_ref[1:2, :]
    cg[pair] = jnp.concatenate([code[:, i * 128:(i + 1) * 128] for i in range(PIX // 128)], axis=0)
    start_pair(c_copy)

    def pack(other, dst):
        blocks = []
        for p in range(N_PAIR):
            first = pl.multiple_of((p * N_TILE + other) * PIX, PIX)
            blocks.append(ph_ref[:, pl.ds(first, PIX)].astype(F32))
        for a in range(4):
            two = jnp.concatenate([blocks[2 * a][0:8], blocks[2 * a + 1][0:8]], axis=0)
            dst[a] = two.astype(BF16)
        for a in range(2):
            four = jnp.concatenate([blocks[4 * a + q][8:12] for q in range(4)], axis=0)
            dst[4 + a] = four.astype(BF16)

    def y_start(i):
        other = tile_peer(i)
        pack(other, sb.at[other])

    loop(1, N_TILE, y_start)
    for part in range(6):
        loop(1, N_TILE, lambda i, part=part: y_copy(tile_peer(i), tile, part).start())
    pack(tile, rb.at[tile])

    wait_pair(c_copy)
    centers = iota((KNOTS, 1), 0).astype(F32) - 1.0

    def knots(p, carry):
        g1, g2 = carry
        for i in range(PIX // 128):
            rows, cols = knot_rows(cg[p, i:i + 1, :], centers)
            lanes = pl.ds(i * 128, 128)
            for m in range(KNOTS):
                hi, lo = split2(rows[m:m + 1, :] * cols)
                bhi[p, m * KNOTS:(m + 1) * KNOTS, lanes] = hi
                blo_ref[m * KNOTS:(m + 1) * KNOTS, lanes] = lo
        hi = bhi[p]
        return g1 + nt(hi, hi), g2 + nt(hi, blo_ref[...])

    zero = jnp.zeros((SCREEN, SCREEN), F32)
    g1, g2 = lax.fori_loop(0, N_PAIR, knots, (zero, zero))
    gpart = (g1 + g2 + g2.T).reshape(N_TILE, KNOTS, SCREEN)
    gs[...] = gpart
    start_tile(gs_copy)
    gr[tile] = gs[tile]

    w = w_ref[...]
    at = incidence_rows(pd_ref[...])
    at16 = at.astype(BF16)
    xt = design_rows(at16)
    firsts, links, schurs, fits = normal_parts(at, at16, xt, w)

    lasts = newton_start(schurs + fits, [1.0, 1.0, 0.5, 0.5])
    lasts = newton_steps(schurs + fits, lasts, 8)
    last0, last1, f0, f1 = newton_end(schurs + fits, lasts)
    sel = own_dates(pair)
    fit0 = (p3(f0, xt) * w[0:1, :]).astype(BF16)
    fit1 = (p3(f1, xt) * w[1:2, :]).astype(BF16)
    d0 = date_solve(full_inverse(firsts[0], links[0], last0), at16, w[0:1, :])
    d1 = date_solve(p3(sel, full_inverse(firsts[1], links[1], last1)), at16, w[1:2, :])
    lhs[0:DATES] = d0
    lhs[DATES:F0_AT] = jnp.zeros((F0_AT - DATES, KP), BF16)
    lhs[F0_AT:D1_AT] = jnp.concatenate([fit0, fit1], axis=0)
    lhs[D1_AT:ROWS] = jnp.concatenate([d1, jnp.zeros((ROWS - D1_AT - OWN, KP), BF16)], axis=0)
    xhi, xlo = split2(xt)
    c0 = nt(d0, xhi) + nt(d0, xlo)
    c1 = nt(d1, xhi) + nt(d1, xlo)
    ends = jnp.concatenate([nt(fit1, at16), nt(d1, at16), sel], axis=0)
    fit_own = nn(fit1, spread_own(pair)).astype(BF16)

    wait_tile(gs_copy)
    gsum = gr[0]
    for t in range(1, N_TILE):
        gsum = gsum + gr[t]
    gg[tile] = gsum
    start_tile(gg_copy)

    def unpack(t):
        rest = [rb[t, 4 + a].astype(F32) for a in range(2)]
        for a in range(4):
            two = rb[t, a].astype(F32)
            for b in range(2):
                p = 2 * a + b
                low = rest[p // 4][4 * (p % 4):4 * (p % 4) + 4]
                block = jnp.concatenate([two[8 * b:8 * b + 8], low, jnp.zeros((4, PIX), F32)], axis=0)
                rows = pl.ds(pl.multiple_of(t * SLOTS, SLOTS), SLOTS)
                ybuf[p, rows, :] = block.astype(BF16)

    unpack(tile)

    def y_arrive(i):
        other = tile_peer(i)
        for part in range(6):
            y_copy(other, other, part).wait_recv()
        unpack(other)

    loop(1, N_TILE, y_arrive)
    def z_body(p, acc):
        y = ybuf[p]
        cp[p] = nn(fit_own, y)
        return acc + nt(bhi[p], y)

    zt = lax.fori_loop(0, N_PAIR, z_body, zero)
    zs[...] = zt.reshape(N_TILE, KNOTS, SCREEN)
    start_tile(zs_copy)
    start_pair(f_copy)
    zr[tile] = zs[tile]
    cr[pair] = cp[pair]
    wait_tile(gg_copy)
    gram = gg[...].reshape(SCREEN, SCREEN)
    gram = gram + jnp.where(iota((SCREEN, SCREEN), 0) == iota((SCREEN, SCREEN), 1), 1.0, 0.0)
    state = newton_start([gram], [1.0])
    state = newton_steps([gram], state, 3)
    wait_tile(zs_copy)
    zsum = zr[0]
    for t in range(1, N_TILE):
        zsum = zsum + zr[t]
    zhi, zlo = split2(zsum)
    zg[pair] = nn(jnp.concatenate([zhi, zlo], axis=0), squeeze()).astype(BF16)
    start_pair(zg_copy)
    state = newton_steps([gram], state, 3)
    wait_pair(zg_copy)
    zrow = jnp.concatenate([zg[p].astype(F32)[:, 0:GROUP] for p in range(N_PAIR)], axis=1).astype(BF16)
    both = nt(zrow, lhs[...])
    wg[tile] = both[0:KNOTS] + both[KNOTS:2 * KNOTS]
    start_tile(w_copy)
    state = newton_steps([gram], state, 3)
    (h,) = newton_end([gram], state)
    wait_pair(f_copy)
    total = cr[0]
    for p in range(1, N_PAIR):
        total = total + cr[p]
    wait_tile(w_copy)

    wt = wg[...].reshape(SCREEN, ROWS)
    w0 = wt[:, 0:DATES] - p3t(wt[:, F0_AT:F1_AT], c0)
    s1 = p3(h, w0)
    q0 = p3t(w0, ends[0:NB + OWN])
    q1 = p3t(s1, ends)
    ehi, elo = split2(q1[:, 0:NB].T)
    own_knots = bhi[pair]
    co_ref[...] = total - (nn(ehi, own_knots) + nn(elo, own_knots))
    step = wt[:, F1_AT:D1_AT + OWN] - (q0 - q1[:, 0:NB + OWN])
    change = step[:, NB:] - p3t(step[:, 0:NB], c1)
    s2 = q1[:, NB + OWN:] + p3(h, change)
    sc_ref[...] = s2.T[0:38]

    def drain_tile(i):
        other = tile_peer(i)
        for part in range(6):
            y_copy(other, tile, part).wait_send()
        for copy in (gs_copy, gg_copy, zs_copy, w_copy):
            copy(other, tile).wait_send()

    loop(1, N_TILE, drain_tile)

    def drain_pair(i):
        other = pair_peer(i)
        for copy in (c_copy, zg_copy, f_copy):
            copy(other, pair).wait_send()

    loop(1, N_PAIR, drain_pair)


def local(phases, pair_dates, weights, coords):
    vmem = pl.BlockSpec(memory_space=pltpu.VMEM)
    shape = jax.ShapeDtypeStruct
    dma = pltpu.SemaphoreType.DMA
    tiles, pairs, parts = dma((N_TILE,)), dma((N_PAIR,)), dma((N_TILE, 6))
    return pl.pallas_call(
        mega_kernel,
        out_shape=[shape((NB, PIX), F32), shape((38, SCREEN), F32)],
        in_specs=[vmem] * 4,
        out_specs=[vmem] * 2,
        scratch_shapes=[
            pltpu.VMEM((N_PAIR, PIX // 128, 128), jnp.int32),
            pltpu.VMEM((N_TILE, 6, SLOTS, PIX), BF16),
            pltpu.VMEM((N_TILE, 6, SLOTS, PIX), BF16),
            pltpu.VMEM((N_PAIR, SCREEN, PIX), BF16),
            pltpu.VMEM((SCREEN, PIX), BF16),
            pltpu.VMEM((N_PAIR, SCREEN, PIX), BF16),
            pltpu.VMEM((N_TILE, KNOTS, SCREEN), F32),
            pltpu.VMEM((N_TILE, KNOTS, SCREEN), F32),
            pltpu.VMEM((N_TILE, KNOTS, SCREEN), F32),
            pltpu.VMEM((N_TILE, KNOTS, SCREEN), F32),
            pltpu.VMEM((N_TILE, KNOTS, SCREEN), F32),
            pltpu.VMEM((N_PAIR, 2 * KNOTS, SCREEN), BF16),
            pltpu.VMEM((N_TILE, KNOTS, ROWS), F32),
            pltpu.VMEM((N_PAIR, NB, PIX), F32),
            pltpu.VMEM((N_PAIR, NB, PIX), F32),
            pltpu.VMEM((ROWS, KP), BF16),
            pairs, pairs, parts, parts, tiles, tiles, tiles, tiles,
            tiles, tiles, pairs, pairs, tiles, tiles, pairs, pairs,
        ],
        compiler_params=pltpu.CompilerParams(
            collective_id=0, has_side_effects=True, vmem_limit_bytes=VMEM_LIMIT
        ),
        name="mega",
    )(phases, coords, pair_dates, weights)


def solution(mesh):
    return jax.shard_map(
        local,
        mesh=mesh,
        in_specs=(P(("pair", "tile"), None), P(), P(), P(None, ("pair", "tile"))),
        out_specs=(P(None, ("pair", "tile")), P("pair", None)),
        check_vma=False,
    )
```

```python
import functools

import jax
import jax.numpy as jnp
from jax import lax
from jax.experimental import pallas as pl
from jax.experimental.pallas import tpu as pltpu
from jax.sharding import PartitionSpec as P

MESH = pl.DeviceIdType.MESH
HI = lax.Precision.HIGHEST
F32, BF16 = jnp.float32, jnp.bfloat16
DATES, NB, KNOTS, FRAME, SCREEN = 304, 32, 16, 4096, 256
PAIRS, SLOTS, DEVICES, PIX = 12, 16, 128, 1024
NPIX = DEVICES * PIX
N_TILE = 16
EVEN, ODD = 160, 144
KP = PAIRS * DEVICES
GROUP = PAIRS * N_TILE
OWN = 40
N_PAIR = 8
NEAR = 160
F0_AT, F1_AT, D1_AT, ROWS = 384, 416, 448, 608
HALF = PIX // 2
PARTS = 1
VMEM_LIMIT = 60 * 1024 * 1024

def nn(a, b, precision=None):
    return lax.dot_general(a, b, (((1,), (0,)), ((), ())), precision=precision, preferred_element_type=F32)

def nt(a, b, precision=None):
    return lax.dot_general(a, b, (((1,), (1,)), ((), ())), precision=precision, preferred_element_type=F32)

def tn(a, b, precision=None):
    return lax.dot_general(a, b, (((0,), (0,)), ((), ())), precision=precision, preferred_element_type=F32)

def split2(x):
    hi = x.astype(BF16)
    return hi, (x - hi.astype(F32)).astype(BF16)

def spline(s):
    a = jnp.abs(s)
    r = jnp.maximum(2.0 - a, 0.0)
    q = jnp.maximum(1.0 - a, 0.0)
    return (r * r * r - 4.0 * (q * q * q)) * (1.0 / 6.0)

def date_of(r):
    rr = jnp.where(r < EVEN, r, r - EVEN)
    base = ((rr >> 4) << 5) + (rr & 15)
    return jnp.where(r < EVEN, base, base + 16)

def iota(shape, dim):
    return lax.broadcasted_iota(jnp.int32, shape, dim)

def block_inverse(c):
    n = c.shape[1]
    row = iota((1, n, n), 1)
    col = iota((1, n, n), 2)
    for j in range(n):
        prow = c[:, j:j + 1, :]
        pcol = c[:, :, j:j + 1]
        d = 1.0 / c[:, j:j + 1, j:j + 1]
        newrow = jnp.where(col[:, :1, :] == j, 1.0, prow) * d
        base = jnp.where(col == j, 0.0, c)
        c = jnp.where(row == j, newrow, base - pcol * newrow)
    return c

def product3(a, b):
    (ah, al), (bh, bl) = a, b
    return nn(ah, bh) + (nn(ah, bl) + nn(al, bh))

def p3(a, b):
    return product3(split2(a), split2(b))

def p3t(a, b):
    (ah, al), (bh, bl) = split2(a), split2(b)
    return nt(ah, bh) + (nt(ah, bl) + nt(al, bh))

def newton_start(mats, floors):
    xs, lows = [], []
    for m, floor in zip(mats, floors):
        n = m.shape[0]
        top = jnp.max(jnp.sum(jnp.abs(m), axis=1, keepdims=True), axis=0, keepdims=True)
        c = 2.0 / (top + floor)
        low = c * floor
        ab = low * (2.0 - low)
        k = 2.0 / (1.0 + ab)
        diagonal = iota((n, n), 0) == iota((n, n), 1)
        xs.append((jnp.where(diagonal, 2.0, 0.0) - m * c) * (c * k))
        lows.append(ab * k)
    return xs, lows

def newton_steps(mats, state, steps):
    parts = [split2(m) for m in mats]
    def body(_, carry):
        xs, lows = carry
        nx, nl = [], []
        halves = [split2(x) for x in xs]
        ys = [product3(m, x) for m, x in zip(parts, halves)]
        for x, y, low in zip(halves, ys, lows):
            n = y.shape[0]
            ab = low * (2.0 - low)
            k = 2.0 / (1.0 + ab)
            eye = jnp.where(iota((n, n), 0) == iota((n, n), 1), 2.0, 0.0)
            nx.append(product3(x, split2(eye - y)) * k)
            nl.append(ab * k)
        return nx, nl
    return lax.fori_loop(0, steps, body, state)

def newton_end(mats, state):
    out = []
    for m, x in zip(mats, state[0]):
        n = m.shape[0]
        eye = jnp.where(iota((n, n), 0) == iota((n, n), 1), 2.0, 0.0)
        out.append(nn(x, eye - nn(m, x, HI), HI))
    return out

def near_dates(quarter):
    row, col = iota((NEAR, DATES), 0), iota((NEAR, DATES), 1)
    q = jnp.where(row >= 2 * OWN, jnp.where(row >= 3 * OWN, 3, 2), jnp.where(row >= OWN, 1, 0))
    i = row - OWN * q
    return jnp.where((38 * (4 * quarter + q) + i == date_of(col)) & (i < 38), 1.0, 0.0)

def by_group(x):
    lane = iota((8, KP), 1)
    t = (lane * 21846) >> 18
    delta = ((t >> 4) & 3) - ((t >> 2) & 3)
    out = x
    for d in (-3, -2, -1, 1, 2, 3):
        out = jnp.where(delta == d, pltpu.roll(x, (144 * d) % KP, 1), out)
    return out

def incidence_rows(pd):
    t = date_of(iota((DATES, KP), 0))
    later = jnp.where(t == pd[1:2, :], 1.0, 0.0)
    return later - jnp.where(t == pd[0:1, :], 1.0, 0.0)

def design_rows(at16):
    tt = date_of(iota((DATES, NB), 0)).astype(F32) * ((NB - 3.0) / (DATES - 1.0))
    t1 = spline(tt - (iota((DATES, NB), 1).astype(F32) - 1.0)).T
    a = t1.astype(BF16)
    r = t1 - a.astype(F32)
    b, c = split2(r)
    return nn(a, at16) + nn(b, at16) + nn(c, at16)

def normal_parts(at, at16, xt, w):
    eye = jnp.where(iota((DATES, DATES), 0) == iota((DATES, DATES), 1), 1.0, 0.0)
    fold = jnp.where((iota((EVEN, 16), 0) & 15) == iota((EVEN, 16), 1), 1.0, 0.0)
    mask = (iota((EVEN, EVEN), 0) >> 4) == (iota((EVEN, EVEN), 1) >> 4)
    ns, comps, fits = [], [], []
    for i in range(2):
        wi = w[i:i + 1, :]
        hi, lo = split2(wi)
        n = nt((at * hi.astype(F32)).astype(BF16), at16) + nt((at * lo.astype(F32)).astype(BF16), at16) + eye
        ns.append(n)
        comps.append(nn(jnp.where(mask, n[:EVEN, :EVEN], 0.0), fold, HI).reshape(10, 16, 16))
        fits.append(nt(xt * wi, xt, HI) + jnp.where(iota((NB, NB), 0) == iota((NB, NB), 1), 0.5, 0.0))
    inv = block_inverse(jnp.concatenate(comps, axis=0))
    firsts, links, schurs = [], [], []
    for i in range(2):
        compact = inv[10 * i:10 * i + 10].reshape(EVEN, 16)
        first = jnp.where(mask, nt(compact, fold, HI), 0.0)
        e = ns[i][:EVEN, EVEN:]
        y = nn(first, e, HI)
        schurs.append(ns[i][EVEN:, EVEN:] - tn(e, y, HI))
        firsts.append(first)
        links.append(y)
    return firsts, links, schurs, fits

def full_inverse(first, link, last):
    right = p3(link, last)
    top = jnp.concatenate([first + p3t(right, link), -right], axis=1)
    bottom = jnp.concatenate([-right.T, last], axis=1)
    return jnp.concatenate([top, bottom], axis=0)

def date_solve(inverse, at16, wi):
    hi, lo = split2(inverse)
    return ((nn(hi, at16) + nn(lo, at16)) * wi).astype(BF16)

def spread_own(group_of_residue):
    row, col = iota((KP, SCREEN), 0), iota((KP, SCREEN), 1)
    group = group_of_residue(iota((1, SCREEN), 1) >> 4)
    inside = (col & 15) < PAIRS
    return jnp.where((row == GROUP * group + PAIRS * (col >> 4) + (col & 15)) & inside, 1.0, 0.0).astype(BF16)

def squeeze():
    row, col = iota((SCREEN, SCREEN), 0), iota((SCREEN, SCREEN), 1)
    inside = (row & 15) < PAIRS
    return jnp.where((col == PAIRS * (row >> 4) + (row & 15)) & inside, 1.0, 0.0).astype(BF16)

def knot_rows(code, centers):
    scale = (KNOTS - 3.0) / FRAME
    rows = spline((code >> 16).astype(F32) * scale - centers)
    cols = spline((code & 65535).astype(F32) * scale - centers)
    return rows, cols


def mega_kernel(
    ph_hbm, ck_ref, pd_ref, w_ref, co_ref, sc_ref,
    ph_ref, ph_sem, cg, sb, rb, bhi, blo_ref, ybuf, gs, gr, gg, zs, zr, zg, wq, wg, cp, cr, lhs,
    c_send, c_recv, y_send, y_recv, gs_send, gs_recv, gg_send, gg_recv,
    zs_send, zs_recv, zg_send, zg_recv, w_send, w_recv, f_send, f_recv,
):
    pair, tile = lax.axis_index("pair"), lax.axis_index("tile")
    zh, zl, yl = pair // 4, (pair // 2) % 2, pair % 2
    yh, xh, xl, core = tile // 8, (tile // 4) % 2, (tile // 2) % 2, tile % 2
    me = zl * 8 + yl * 4 + xl * 2 + core
    group = zh * 4 + yh * 2 + xh

    def place(a, r):
        p = (a // 4) * 4 + (r // 8) * 2 + (r // 4) % 2
        return p, ((a // 2) % 2) * 8 + (a % 2) * 4 + r % 4

    def group_at(r, half):
        if half == 0:
            return group
        return (
            ((zh + zl + r // 8) % 2) * 4 + ((yh + yl + (r // 4) % 2) % 2) * 2 + (xh + xl + (r // 2) % 2) % 2
        )

    def residue_peer(i):
        t = me + i
        return jnp.where(t >= N_TILE, t - N_TILE, t)

    def class_peer(i):
        t = group + i
        return jnp.where(t >= N_PAIR, t - N_PAIR, t)

    def loop(lo, hi, f):
        def body(i, carry):
            f(i)
            return carry
        lax.fori_loop(lo, hi, body, 0)

    def to_residue(src, dst, send, recv, other, half=0):
        return pltpu.make_async_remote_copy(
            src_ref=src, dst_ref=dst, send_sem=send, recv_sem=recv,
            device_id=place(group_at(other, half), other), device_id_type=MESH,
        )

    def to_class(src, dst, send, recv, other, slot):
        return pltpu.make_async_remote_copy(
            src_ref=src, dst_ref=dst.at[slot], send_sem=send.at[other], recv_sem=recv.at[slot],
            device_id=place(other, me), device_id_type=MESH,
        )

    def c_copy(other, slot):
        return to_class(cg.at[group], cg, c_send, c_recv, other, slot)

    def y_copy(other, slot, half, part):
        rows = pl.ds(6 * part, 6)
        return to_residue(
            sb.at[half, other, rows], rb.at[half, slot, rows],
            y_send.at[half, other, part], y_recv.at[half, slot, part], other, half,
        )

    def gs_copy(other, slot):
        return to_residue(gs.at[other], gr.at[slot], gs_send.at[other], gs_recv.at[slot], other)

    def gg_copy(other, slot):
        return to_residue(gg.at[me], gg.at[slot], gg_send.at[other], gg_recv.at[slot], other)

    def zs_copy(other, slot, half):
        return to_residue(
            zs.at[half, other], zr.at[half, slot], zs_send.at[half, other], zs_recv.at[half, slot], other, half
        )

    def zg_copy(other, slot):
        return to_class(zg.at[group], zg, zg_send, zg_recv, other, slot)

    def w_copy(other, slot):
        return to_residue(wq.at[other // 4], wg.at[slot], w_send.at[other], w_recv.at[slot], other)

    def f_copy(other, slot, half):
        return to_class(cp.at[half, other], cr.at[half], f_send.at[half], f_recv.at[half], other, slot)

    def start_residue(copy, *more):
        loop(1, N_TILE, lambda i: copy(residue_peer(i), me, *more).start())

    def wait_residue(copy, *more):
        loop(1, N_TILE, lambda i: copy(residue_peer(i), residue_peer(i), *more).wait_recv())

    def start_class(copy, *more):
        loop(1, N_PAIR, lambda i: copy(class_peer(i), group, *more).start())

    def wait_class(copy, *more):
        loop(1, N_PAIR, lambda i: copy(class_peer(i), class_peer(i), *more).wait_recv())

    load = pltpu.make_async_copy(ph_hbm, ph_ref, ph_sem)
    load.start()
    barrier = pltpu.get_barrier_semaphore()

    def greet(where):
        pl.semaphore_signal(barrier, inc=1, device_id=where, device_id_type=MESH)

    for half in range(2):
        loop(1, N_TILE, lambda i, half=half: greet(place(group_at(residue_peer(i), half), residue_peer(i))))
    loop(1, N_PAIR, lambda i: greet(place(class_peer(i), me)))

    rows = jnp.concatenate([pd_ref[...].astype(F32), w_ref[...], jnp.zeros((4, KP), F32)], axis=0)
    rows = by_group(rows)
    w = rows[2:4, :]
    at = incidence_rows(rows[0:2, :].astype(jnp.int32))
    at16 = at.astype(BF16)
    xt = design_rows(at16)
    firsts, links, schurs, fits = normal_parts(at, at16, xt, w)
    pl.semaphore_wait(barrier, 2 * N_TILE + N_PAIR - 3)

    code = ck_ref[0:1, :] * 65536 + ck_ref[1:2, :]
    cg[group] = jnp.concatenate([code[:, i * 128:(i + 1) * 128] for i in range(PIX // 128)], axis=0)
    start_class(c_copy)

    load.wait()

    def pack(other, half, dst):
        blocks = []
        for a in range(N_PAIR):
            p, t = place(a, other)
            first = pl.multiple_of((p * N_TILE + t) * PIX + half * HALF, HALF)
            blocks.append(ph_ref[:, pl.ds(first, HALF)].astype(F32))
        for a in range(4):
            two = jnp.concatenate([blocks[2 * a][0:8], blocks[2 * a + 1][0:8]], axis=0)
            dst[a] = two.astype(BF16)
        for a in range(2):
            four = jnp.concatenate([blocks[4 * a + q][8:12] for q in range(4)], axis=0)
            dst[4 + a] = four.astype(BF16)

    def y_start(i, half):
        other = residue_peer(i)
        pack(other, half, sb.at[half, other])
        for part in range(PARTS):
            y_copy(other, me, half, part).start()

    for half in range(2):
        loop(1, N_TILE, lambda i, half=half: y_start(i, half))
    for half in range(2):
        pack(me, half, rb.at[half, me])

    lasts = newton_start(schurs + fits, [1.0, 1.0, 0.5, 0.5])
    lasts = newton_steps(schurs + fits, lasts, 8)
    last0, last1, f0, f1 = newton_end(schurs + fits, lasts)

    wait_class(c_copy)
    centers = iota((KNOTS, 1), 0).astype(F32) - 1.0

    def knots(p, carry):
        g1, g2 = carry
        for i in range(PIX // 128):
            rows, cols = knot_rows(cg[p, i:i + 1, :], centers)
            lanes = pl.ds(i * 128, 128)
            for m in range(KNOTS):
                hi, lo = split2(rows[m:m + 1, :] * cols)
                bhi[p, m * KNOTS:(m + 1) * KNOTS, lanes] = hi
                blo_ref[m * KNOTS:(m + 1) * KNOTS, lanes] = lo
        hi = bhi[p]
        return g1 + nt(hi, hi), g2 + nt(hi, blo_ref[...])

    zero = jnp.zeros((SCREEN, SCREEN), F32)
    g1, g2 = lax.fori_loop(0, N_PAIR, knots, (zero, zero))
    gs[...] = (g1 + g2 + g2.T).reshape(N_TILE, KNOTS, SCREEN)
    start_residue(gs_copy)
    gr[me] = gs[me]

    sel = near_dates(zh)
    fit0 = (p3(f0, xt) * w[0:1, :]).astype(BF16)
    fit1 = (p3(f1, xt) * w[1:2, :]).astype(BF16)
    d0 = date_solve(full_inverse(firsts[0], links[0], last0), at16, w[0:1, :])
    d1 = date_solve(p3(sel, full_inverse(firsts[1], links[1], last1)), at16, w[1:2, :])
    lhs[0:DATES] = d0
    lhs[DATES:F0_AT] = jnp.zeros((F0_AT - DATES, KP), BF16)
    lhs[F0_AT:D1_AT] = jnp.concatenate([fit0, fit1], axis=0)
    lhs[D1_AT:ROWS] = d1
    xhi, xlo = split2(xt)
    c0 = nt(d0, xhi) + nt(d0, xlo)
    c1 = nt(d1, xhi) + nt(d1, xlo)
    ends = jnp.concatenate([nt(fit1, at16), nt(d1, at16), sel], axis=0)
    fit_own = [nn(fit1, spread_own(functools.partial(group_at, half=half))).astype(BF16) for half in range(2)]

    wait_residue(gs_copy)
    gsum = gr[0]
    for t in range(1, N_TILE):
        gsum = gsum + gr[t]
    gg[me] = gsum
    start_residue(gg_copy)

    def unpack(t, half):
        rest = [rb[half, t, 4 + a].astype(F32) for a in range(2)]
        for a in range(4):
            two = rb[half, t, a].astype(F32)
            for b in range(2):
                p = 2 * a + b
                low = rest[p // 4][4 * (p % 4):4 * (p % 4) + 4]
                block = jnp.concatenate([two[8 * b:8 * b + 8], low, jnp.zeros((4, HALF), F32)], axis=0)
                ybuf[half, p, pl.ds(pl.multiple_of(t * SLOTS, SLOTS), SLOTS), :] = block.astype(BF16)

    def y_arrive(i, half):
        other = residue_peer(i)
        for part in range(PARTS):
            y_copy(other, other, half, part).wait_recv()
        unpack(other, half)

    def z_body(p, acc, half):
        y = ybuf[half, p]
        cp[half, p] = nn(fit_own[half], y).astype(BF16)
        return acc + nt(bhi[p, :, half * HALF:(half + 1) * HALF], y)

    for half in range(2):
        unpack(me, half)
        loop(1, N_TILE, lambda i, half=half: y_arrive(i, half))
        zt = lax.fori_loop(0, N_PAIR, functools.partial(z_body, half=half), zero)
        zs[half] = zt.reshape(N_TILE, KNOTS, SCREEN)
        start_residue(zs_copy, half)
        zr[half, me] = zs[half, me]
        cr[half, group] = cp[half, group]
    wait_residue(gg_copy)
    gram = gg[...].reshape(SCREEN, SCREEN)
    gram = gram + jnp.where(iota((SCREEN, SCREEN), 0) == iota((SCREEN, SCREEN), 1), 1.0, 0.0)
    state = newton_start([gram], [1.0])
    state = newton_steps([gram], state, 3)
    sums = []
    for half in range(2):
        wait_residue(zs_copy, half)
        zsum = zr[half, 0]
        for t in range(1, N_TILE):
            zsum = zsum + zr[half, t]
        sums.extend(split2(zsum))
    zg[group] = nn(jnp.concatenate(sums, axis=0), squeeze()).astype(BF16)
    start_class(zg_copy)
    for half in range(2):
        start_class(f_copy, half)
    state = newton_steps([gram], state, 3)
    wait_class(zg_copy)
    octant = iota((1, SCREEN), 1)
    octant = jnp.where(octant < GROUP, (octant * 10923) >> 18, -1)
    across = []
    for a in range(N_PAIR):
        b = ((zl + a // 4) % 2) * 4 + ((yl + (a // 2) % 2) % 2) * 2 + (xl + a % 2) % 2
        both = zg[b].astype(F32)
        across.append(both[2 * KNOTS:3 * KNOTS] + both[3 * KNOTS:4 * KNOTS])
    zrow = []
    for a in range(N_PAIR):
        both = zg[a].astype(F32)
        here = both[0:KNOTS] + both[KNOTS:2 * KNOTS]
        for m in range(N_PAIR):
            here = here + jnp.where(octant == m, across[a ^ m], 0.0)
        zrow.append(here[:, 0:GROUP])
    zhi, zlo = split2(jnp.concatenate(zrow, axis=1))
    both = nt(jnp.concatenate([zhi, zlo], axis=0), lhs[...])
    wt = both[0:KNOTS] + both[KNOTS:2 * KNOTS]
    w0 = wt[:, 0:DATES] - p3t(wt[:, F0_AT:F1_AT], c0)
    q = p3t(w0, ends)
    for n in range(4):
        lo = n * OWN
        wq[n] = jnp.concatenate([
            q[:, 0:NB], q[:, NB + lo:NB + lo + OWN], q[:, NB + NEAR + lo:NB + NEAR + lo + OWN],
            jnp.zeros((KNOTS, 128 - NB - 2 * OWN), F32),
            wt[:, F1_AT:D1_AT], wt[:, D1_AT + lo:D1_AT + lo + OWN], jnp.zeros((KNOTS, 128 - NB - OWN), F32),
        ], axis=1)
    start_residue(w_copy)
    wg[me] = wq[me // 4]
    state = newton_steps([gram], state, 3)
    (h,) = newton_end([gram], state)
    mine = zl * 2 + yl
    c1_own = c1[0:OWN]
    for n in range(1, 4):
        c1_own = jnp.where(mine == n, c1[n * OWN:(n + 1) * OWN], c1_own)
    totals = []
    for half in range(2):
        wait_class(f_copy, half)
        total = cr[half, 0].astype(F32)
        for p in range(1, N_PAIR):
            total = total + cr[half, p].astype(F32)
        totals.append(total)
    total = jnp.concatenate(totals, axis=1)
    wait_residue(w_copy)

    wt = wg[...].reshape(SCREEN, 2 * 128)
    q0 = wt[:, 0:128]
    q1 = p3(h, q0)
    ehi, elo = split2(q1[:, 0:NB].T)
    own_knots = bhi[group]
    co_ref[...] = total - (nn(ehi, own_knots) + nn(elo, own_knots))
    step = wt[:, 128:128 + NB + OWN] - (q0[:, 0:NB + OWN] - q1[:, 0:NB + OWN])
    change = step[:, NB:] - p3t(step[:, 0:NB], c1_own)
    s2 = q1[:, NB + OWN:NB + 2 * OWN] + p3(h, change)
    sc_ref[...] = s2.T[0:38]

    def drain_residue(i):
        other = residue_peer(i)
        for half in range(2):
            for part in range(PARTS):
                y_copy(other, me, half, part).wait_send()
            zs_copy(other, me, half).wait_send()
        for copy in (gs_copy, gg_copy, w_copy):
            copy(other, me).wait_send()

    loop(1, N_TILE, drain_residue)

    def drain_class(i):
        other = class_peer(i)
        for copy in (c_copy, zg_copy):
            copy(other, group).wait_send()
        for half in range(2):
            f_copy(other, group, half).wait_send()

    loop(1, N_PAIR, drain_class)


def local(phases, pair_dates, weights, coords):
    vmem = pl.BlockSpec(memory_space=pltpu.VMEM)
    shape = jax.ShapeDtypeStruct
    dma = pltpu.SemaphoreType.DMA
    tiles, pairs = dma((N_TILE,)), dma((N_PAIR,))
    twos, halves, parts = dma((2, N_PAIR)), dma((2, N_TILE)), dma((2, N_TILE, PARTS))
    return pl.pallas_call(
        mega_kernel,
        out_shape=[shape((NB, PIX), F32), shape((38, SCREEN), F32)],
        in_specs=[pl.BlockSpec(memory_space=pl.ANY)] + [vmem] * 3,
        out_specs=[vmem] * 2,
        scratch_shapes=[
            pltpu.VMEM((PAIRS, NPIX), BF16),
            dma,
            pltpu.VMEM((N_PAIR, PIX // 128, 128), jnp.int32),
            pltpu.VMEM((2, N_TILE, 6, SLOTS, HALF), BF16),
            pltpu.VMEM((2, N_TILE, 6, SLOTS, HALF), BF16),
            pltpu.VMEM((N_PAIR, SCREEN, PIX), BF16),
            pltpu.VMEM((SCREEN, PIX), BF16),
            pltpu.VMEM((2, N_PAIR, SCREEN, HALF), BF16),
            pltpu.VMEM((N_TILE, KNOTS, SCREEN), F32),
            pltpu.VMEM((N_TILE, KNOTS, SCREEN), F32),
            pltpu.VMEM((N_TILE, KNOTS, SCREEN), F32),
            pltpu.VMEM((2, N_TILE, KNOTS, SCREEN), F32),
            pltpu.VMEM((2, N_TILE, KNOTS, SCREEN), F32),
            pltpu.VMEM((N_PAIR, 4 * KNOTS, SCREEN), BF16),
            pltpu.VMEM((4, KNOTS, 2 * 128), F32),
            pltpu.VMEM((N_TILE, KNOTS, 2 * 128), F32),
            pltpu.VMEM((2, N_PAIR, NB, HALF), BF16),
            pltpu.VMEM((2, N_PAIR, NB, HALF), BF16),
            pltpu.VMEM((ROWS, KP), BF16),
            pairs, pairs, parts, parts, tiles, tiles, tiles, tiles,
            halves, halves, pairs, pairs, tiles, tiles, twos, twos,
        ],
        compiler_params=pltpu.CompilerParams(
            collective_id=0, has_side_effects=True, vmem_limit_bytes=VMEM_LIMIT
        ),
        name="mega",
    )(phases, coords, pair_dates.T, weights)


def solution(mesh):
    return jax.shard_map(
        local,
        mesh=mesh,
        in_specs=(P(("pair", "tile"), None), P(), P(), P(None, ("pair", "tile"))),
        out_specs=(P(None, ("pair", "tile")), P("pair", None)),
        check_vma=False,
    )
```

```python
import functools

import jax
import jax.numpy as jnp
from jax import lax
from jax.experimental import pallas as pl
from jax.experimental.pallas import tpu as pltpu
from jax.sharding import PartitionSpec as P

MESH = pl.DeviceIdType.MESH
HI = lax.Precision.HIGHEST
F32, BF16 = jnp.float32, jnp.bfloat16
DATES, NB, KNOTS, FRAME, SCREEN = 304, 32, 16, 4096, 256
PAIRS, SLOTS, DEVICES, PIX = 12, 16, 128, 1024
NPIX = DEVICES * PIX
N_TILE = 16
EVEN, ODD = 160, 144
KP = PAIRS * DEVICES
GROUP = PAIRS * N_TILE
OWN = 40
N_PAIR = 8
NEAR = 160
F0_AT, F1_AT, D1_AT, ROWS = 384, 416, 448, 608
HALF = PIX // 2
PARTS = 1
VMEM_LIMIT = 60 * 1024 * 1024

def nn(a, b, precision=None):
    return lax.dot_general(a, b, (((1,), (0,)), ((), ())), precision=precision, preferred_element_type=F32)

def nt(a, b, precision=None):
    return lax.dot_general(a, b, (((1,), (1,)), ((), ())), precision=precision, preferred_element_type=F32)

def tn(a, b, precision=None):
    return lax.dot_general(a, b, (((0,), (0,)), ((), ())), precision=precision, preferred_element_type=F32)

def split2(x):
    hi = x.astype(BF16)
    return hi, (x - hi.astype(F32)).astype(BF16)

def spline(s):
    a = jnp.abs(s)
    r = jnp.maximum(2.0 - a, 0.0)
    q = jnp.maximum(1.0 - a, 0.0)
    return (r * r * r - 4.0 * (q * q * q)) * (1.0 / 6.0)

def date_of(r):
    rr = jnp.where(r < EVEN, r, r - EVEN)
    base = ((rr >> 4) << 5) + (rr & 15)
    return jnp.where(r < EVEN, base, base + 16)

def iota(shape, dim):
    return lax.broadcasted_iota(jnp.int32, shape, dim)

def block_inverse(c):
    n = c.shape[1]
    row = iota((1, n, n), 1)
    col = iota((1, n, n), 2)
    for j in range(n):
        prow = c[:, j:j + 1, :]
        pcol = c[:, :, j:j + 1]
        d = 1.0 / c[:, j:j + 1, j:j + 1]
        newrow = jnp.where(col[:, :1, :] == j, 1.0, prow) * d
        base = jnp.where(col == j, 0.0, c)
        c = jnp.where(row == j, newrow, base - pcol * newrow)
    return c

def product3(a, b):
    (ah, al), (bh, bl) = a, b
    return nn(ah, bh) + (nn(ah, bl) + nn(al, bh))

def p3(a, b):
    return product3(split2(a), split2(b))

def p3t(a, b):
    (ah, al), (bh, bl) = split2(a), split2(b)
    return nt(ah, bh) + (nt(ah, bl) + nt(al, bh))

def newton_start(mats, floors):
    xs, lows = [], []
    for m, floor in zip(mats, floors):
        n = m.shape[0]
        top = jnp.max(jnp.sum(jnp.abs(m), axis=1, keepdims=True), axis=0, keepdims=True)
        c = 2.0 / (top + floor)
        low = c * floor
        ab = low * (2.0 - low)
        k = 2.0 / (1.0 + ab)
        diagonal = iota((n, n), 0) == iota((n, n), 1)
        xs.append((jnp.where(diagonal, 2.0, 0.0) - m * c) * (c * k))
        lows.append(ab * k)
    return xs, lows

def newton_steps(mats, state, steps):
    parts = [split2(m) for m in mats]
    def body(_, carry):
        xs, lows = carry
        nx, nl = [], []
        halves = [split2(x) for x in xs]
        ys = [product3(m, x) for m, x in zip(parts, halves)]
        for x, y, low in zip(halves, ys, lows):
            n = y.shape[0]
            ab = low * (2.0 - low)
            k = 2.0 / (1.0 + ab)
            eye = jnp.where(iota((n, n), 0) == iota((n, n), 1), 2.0, 0.0)
            nx.append(product3(x, split2(eye - y)) * k)
            nl.append(ab * k)
        return nx, nl
    return lax.fori_loop(0, steps, body, state)

def newton_end(mats, state):
    out = []
    for m, x in zip(mats, state[0]):
        n = m.shape[0]
        eye = jnp.where(iota((n, n), 0) == iota((n, n), 1), 2.0, 0.0)
        out.append(nn(x, eye - nn(m, x, HI), HI))
    return out

def near_dates(quarter):
    row, col = iota((NEAR, DATES), 0), iota((NEAR, DATES), 1)
    q = jnp.where(row >= 2 * OWN, jnp.where(row >= 3 * OWN, 3, 2), jnp.where(row >= OWN, 1, 0))
    i = row - OWN * q
    return jnp.where((38 * (4 * quarter + q) + i == date_of(col)) & (i < 38), 1.0, 0.0)

def by_group(x):
    lane = iota((8, KP), 1)
    t = (lane * 21846) >> 18
    delta = ((t >> 4) & 3) - ((t >> 2) & 3)
    out = x
    for d in (-3, -2, -1, 1, 2, 3):
        out = jnp.where(delta == d, pltpu.roll(x, (144 * d) % KP, 1), out)
    return out

def incidence_rows(pd):
    t = date_of(iota((DATES, KP), 0))
    later = jnp.where(t == pd[1:2, :], 1.0, 0.0)
    return later - jnp.where(t == pd[0:1, :], 1.0, 0.0)

def design_rows(at16):
    tt = date_of(iota((DATES, NB), 0)).astype(F32) * ((NB - 3.0) / (DATES - 1.0))
    t1 = spline(tt - (iota((DATES, NB), 1).astype(F32) - 1.0)).T
    a = t1.astype(BF16)
    r = t1 - a.astype(F32)
    b, c = split2(r)
    return nn(a, at16) + nn(b, at16) + nn(c, at16)

def normal_parts(at, at16, xt, w):
    eye = jnp.where(iota((DATES, DATES), 0) == iota((DATES, DATES), 1), 1.0, 0.0)
    fold = jnp.where((iota((EVEN, 16), 0) & 15) == iota((EVEN, 16), 1), 1.0, 0.0)
    mask = (iota((EVEN, EVEN), 0) >> 4) == (iota((EVEN, EVEN), 1) >> 4)
    ns, comps, fits = [], [], []
    for i in range(2):
        wi = w[i:i + 1, :]
        hi, lo = split2(wi)
        n = nt((at * hi.astype(F32)).astype(BF16), at16) + nt((at * lo.astype(F32)).astype(BF16), at16) + eye
        ns.append(n)
        comps.append(nn(jnp.where(mask, n[:EVEN, :EVEN], 0.0), fold, HI).reshape(10, 16, 16))
        fits.append(nt(xt * wi, xt, HI) + jnp.where(iota((NB, NB), 0) == iota((NB, NB), 1), 0.5, 0.0))
    return ns, comps, fits

def eliminate_even(ns, comps):
    fold = jnp.where((iota((EVEN, 16), 0) & 15) == iota((EVEN, 16), 1), 1.0, 0.0)
    mask = (iota((EVEN, EVEN), 0) >> 4) == (iota((EVEN, EVEN), 1) >> 4)
    inv = block_inverse(jnp.concatenate(comps, axis=0))
    firsts, links, schurs = [], [], []
    for i in range(2):
        compact = inv[10 * i:10 * i + 10].reshape(EVEN, 16)
        first = jnp.where(mask, nt(compact, fold, HI), 0.0)
        e = ns[i][:EVEN, EVEN:]
        y = nn(first, e, HI)
        schurs.append(ns[i][EVEN:, EVEN:] - tn(e, y, HI))
        firsts.append(first)
        links.append(y)
    return firsts, links, schurs

def full_inverse(first, link, last):
    right = p3(link, last)
    top = jnp.concatenate([first + p3t(right, link), -right], axis=1)
    bottom = jnp.concatenate([-right.T, last], axis=1)
    return jnp.concatenate([top, bottom], axis=0)

def date_solve(inverse, at16, wi):
    hi, lo = split2(inverse)
    return ((nn(hi, at16) + nn(lo, at16)) * wi).astype(BF16)

def spread_own(group_of_residue):
    row, col = iota((KP, SCREEN), 0), iota((KP, SCREEN), 1)
    group = group_of_residue(iota((1, SCREEN), 1) >> 4)
    inside = (col & 15) < PAIRS
    return jnp.where((row == GROUP * group + PAIRS * (col >> 4) + (col & 15)) & inside, 1.0, 0.0).astype(BF16)

def squeeze():
    row, col = iota((SCREEN, SCREEN), 0), iota((SCREEN, SCREEN), 1)
    inside = (row & 15) < PAIRS
    return jnp.where((col == PAIRS * (row >> 4) + (row & 15)) & inside, 1.0, 0.0).astype(BF16)

def knot_rows(code, centers):
    scale = (KNOTS - 3.0) / FRAME
    rows = spline((code >> 16).astype(F32) * scale - centers)
    cols = spline((code & 65535).astype(F32) * scale - centers)
    return rows, cols


def mega_kernel(
    ph_hbm, ck_ref, pd_ref, w_ref, wt_ref, h_ref, total_ref, kn_ref, c1_ref,
    ph_ref, ph_sem, cg, sb, rb, bhi, blo_ref, ybuf, gs, gr, gg, zs, zr, zg, wq, wg, cp, cr, lhs,
    c_send, c_recv, y_send, y_recv, gs_send, gs_recv, gg_send, gg_recv,
    zs_send, zs_recv, zg_send, zg_recv, w_send, w_recv, f_send, f_recv,
):
    pair, tile = lax.axis_index("pair"), lax.axis_index("tile")
    zh, zl, yl = pair >> 2, (pair >> 1) & 1, pair & 1
    yh, xh, xl, core = tile >> 3, (tile >> 2) & 1, (tile >> 1) & 1, tile & 1
    me = zl * 8 + yl * 4 + xl * 2 + core
    group = zh * 4 + yh * 2 + xh

    def place(a, r):
        return (a >> 2) * 4 + (r >> 2), ((a >> 1) & 1) * 8 + (a & 1) * 4 + (r & 3)

    def group_at(r, half):
        if half == 0:
            return group
        return (
            ((zh + zl + (r >> 3)) & 1) * 4 + ((yh + yl + (r >> 2)) & 1) * 2 + ((xh + xl + (r >> 1)) & 1)
        )

    def residue_peer(i):
        t = me + i
        return jnp.where(t >= N_TILE, t - N_TILE, t)

    def class_peer(i):
        t = group + i
        return jnp.where(t >= N_PAIR, t - N_PAIR, t)

    def loop(lo, hi, f):
        def body(i, carry):
            f(i)
            return carry
        lax.fori_loop(lo, hi, body, 0)

    def to_residue(src, dst, send, recv, other, half=0):
        return pltpu.make_async_remote_copy(
            src_ref=src, dst_ref=dst, send_sem=send, recv_sem=recv,
            device_id=place(group_at(other, half), other), device_id_type=MESH,
        )

    def to_class(src, dst, send, recv, other, slot):
        return pltpu.make_async_remote_copy(
            src_ref=src, dst_ref=dst.at[slot], send_sem=send.at[other], recv_sem=recv.at[slot],
            device_id=place(other, me), device_id_type=MESH,
        )

    def c_copy(other, slot):
        return to_class(cg.at[group], cg, c_send, c_recv, other, slot)

    def y_copy(other, slot, half, part):
        rows = pl.ds(6 * part, 6)
        return to_residue(
            sb.at[half, other, rows], rb.at[half, slot, rows],
            y_send.at[half, other, part], y_recv.at[half, slot, part], other, half,
        )

    def gs_copy(other, slot):
        return to_residue(gs.at[other], gr.at[slot], gs_send.at[other], gs_recv.at[slot], other)

    def gg_copy(other, slot):
        return to_residue(gg.at[me], gg.at[slot], gg_send.at[other], gg_recv.at[slot], other)

    def zs_copy(other, slot, half):
        return to_residue(
            zs.at[half, other], zr.at[half, slot], zs_send.at[half, other], zs_recv.at[half, slot], other, half
        )

    def zg_copy(other, slot):
        return to_class(zg.at[group], zg, zg_send, zg_recv, other, slot)

    def w_copy(other, slot):
        return to_residue(wq.at[other // 4], wg.at[slot], w_send.at[other], w_recv.at[slot], other)

    def f_copy(other, slot, half):
        return to_class(cp.at[half, other], cr.at[half], f_send.at[half], f_recv.at[half], other, slot)

    def start_residue(copy, *more):
        loop(1, N_TILE, lambda i: copy(residue_peer(i), me, *more).start())

    def wait_residue(copy, *more):
        loop(1, N_TILE, lambda i: copy(residue_peer(i), residue_peer(i), *more).wait_recv())

    def start_class(copy, *more):
        loop(1, N_PAIR, lambda i: copy(class_peer(i), group, *more).start())

    def wait_class(copy, *more):
        loop(1, N_PAIR, lambda i: copy(class_peer(i), class_peer(i), *more).wait_recv())

    load = pltpu.make_async_copy(ph_hbm, ph_ref, ph_sem)
    load.start()
    barrier = pltpu.get_barrier_semaphore()

    def greet(where):
        pl.semaphore_signal(barrier, inc=1, device_id=where, device_id_type=MESH)

    for half in range(2):
        loop(1, N_TILE, lambda i, half=half: greet(place(group_at(residue_peer(i), half), residue_peer(i))))
    loop(1, N_PAIR, lambda i: greet(place(class_peer(i), me)))

    rows = jnp.concatenate([pd_ref[...].astype(F32), w_ref[...], jnp.zeros((4, KP), F32)], axis=0)
    rows = by_group(rows)
    w = rows[2:4, :]
    at = incidence_rows(rows[0:2, :].astype(jnp.int32))
    at16 = at.astype(BF16)
    xt = design_rows(at16)
    normals, evens, fits = normal_parts(at, at16, xt, w)
    pl.semaphore_wait(barrier, 2 * N_TILE + N_PAIR - 3)

    code = ck_ref[0:1, :] * 65536 + ck_ref[1:2, :]
    cg[group] = jnp.concatenate([code[:, i * 128:(i + 1) * 128] for i in range(PIX // 128)], axis=0)
    start_class(c_copy)

    load.wait()

    def pack(other, half, dst):
        blocks = []
        for a in range(N_PAIR):
            p, t = place(a, other)
            first = pl.multiple_of((p * N_TILE + t) * PIX + half * HALF, HALF)
            blocks.append(ph_ref[:, pl.ds(first, HALF)].astype(F32))
        for a in range(4):
            two = jnp.concatenate([blocks[2 * a][0:8], blocks[2 * a + 1][0:8]], axis=0)
            dst[a] = two.astype(BF16)
        for a in range(2):
            four = jnp.concatenate([blocks[4 * a + q][8:12] for q in range(4)], axis=0)
            dst[4 + a] = four.astype(BF16)

    def y_start(i, half):
        other = residue_peer(i)
        pack(other, half, sb.at[half, other])
        for part in range(PARTS):
            y_copy(other, me, half, part).start()

    for half in range(2):
        loop(1, N_TILE, lambda i, half=half: y_start(i, half))
    for half in range(2):
        pack(me, half, rb.at[half, me])

    firsts, links, schurs = eliminate_even(normals, evens)
    lasts = newton_start(schurs + fits, [1.0, 1.0, 0.5, 0.5])
    lasts = newton_steps(schurs + fits, lasts, 8)
    last0, last1, f0, f1 = newton_end(schurs + fits, lasts)

    wait_class(c_copy)
    centers = iota((KNOTS, 1), 0).astype(F32) - 1.0

    def knots(p, carry):
        g1, g2 = carry
        for i in range(PIX // 128):
            rows, cols = knot_rows(cg[p, i:i + 1, :], centers)
            lanes = pl.ds(i * 128, 128)
            for m in range(KNOTS):
                hi, lo = split2(rows[m:m + 1, :] * cols)
                bhi[p, m * KNOTS:(m + 1) * KNOTS, lanes] = hi
                blo_ref[m * KNOTS:(m + 1) * KNOTS, lanes] = lo
        hi = bhi[p]
        return g1 + nt(hi, hi), g2 + nt(hi, blo_ref[...])

    zero = jnp.zeros((SCREEN, SCREEN), F32)
    g1, g2 = lax.fori_loop(0, N_PAIR, knots, (zero, zero))
    gs[...] = (g1 + g2 + g2.T).reshape(N_TILE, KNOTS, SCREEN)
    start_residue(gs_copy)
    gr[me] = gs[me]

    sel = near_dates(zh)
    fit0 = (p3(f0, xt) * w[0:1, :]).astype(BF16)
    fit1 = (p3(f1, xt) * w[1:2, :]).astype(BF16)
    d0 = date_solve(full_inverse(firsts[0], links[0], last0), at16, w[0:1, :])
    d1 = date_solve(p3(sel, full_inverse(firsts[1], links[1], last1)), at16, w[1:2, :])
    lhs[0:DATES] = d0
    lhs[DATES:F0_AT] = jnp.zeros((F0_AT - DATES, KP), BF16)
    lhs[F0_AT:D1_AT] = jnp.concatenate([fit0, fit1], axis=0)
    lhs[D1_AT:ROWS] = d1
    xhi, xlo = split2(xt)
    c0 = nt(d0, xhi) + nt(d0, xlo)
    c1 = nt(d1, xhi) + nt(d1, xlo)
    ends = jnp.concatenate([nt(fit1, at16), nt(d1, at16), sel], axis=0)
    fit_own = [nn(fit1, spread_own(functools.partial(group_at, half=half))).astype(BF16) for half in range(2)]

    wait_residue(gs_copy)
    gsum = gr[0]
    for t in range(1, N_TILE):
        gsum = gsum + gr[t]
    gg[me] = gsum
    start_residue(gg_copy)

    def unpack(t, half):
        rest = [rb[half, t, 4 + a].astype(F32) for a in range(2)]
        for a in range(4):
            two = rb[half, t, a].astype(F32)
            for b in range(2):
                p = 2 * a + b
                low = rest[p // 4][4 * (p % 4):4 * (p % 4) + 4]
                block = jnp.concatenate([two[8 * b:8 * b + 8], low, jnp.zeros((4, HALF), F32)], axis=0)
                ybuf[half, p, pl.ds(pl.multiple_of(t * SLOTS, SLOTS), SLOTS), :] = block.astype(BF16)

    def y_arrive(i, half):
        other = residue_peer(i)
        for part in range(PARTS):
            y_copy(other, other, half, part).wait_recv()
        unpack(other, half)

    def z_body(p, acc, half):
        y = ybuf[half, p]
        cp[half, p] = nn(fit_own[half], y).astype(BF16)
        return acc + nt(bhi[p, :, half * HALF:(half + 1) * HALF], y)

    for half in range(2):
        unpack(me, half)
        loop(1, N_TILE, lambda i, half=half: y_arrive(N_TILE - i, half))
        zt = lax.fori_loop(0, N_PAIR, functools.partial(z_body, half=half), zero)
        zs[half] = zt.reshape(N_TILE, KNOTS, SCREEN)
        start_residue(zs_copy, half)
        zr[half, me] = zs[half, me]
        cr[half, group] = cp[half, group]
    wait_residue(gg_copy)
    gram = gg[...].reshape(SCREEN, SCREEN)
    gram = gram + jnp.where(iota((SCREEN, SCREEN), 0) == iota((SCREEN, SCREEN), 1), 1.0, 0.0)
    state = newton_start([gram], [1.0])
    state = newton_steps([gram], state, 3)
    sums = []
    for half in range(2):
        wait_residue(zs_copy, half)
        zsum = zr[half, 0]
        for t in range(1, N_TILE):
            zsum = zsum + zr[half, t]
        sums.extend(split2(zsum))
    zg[group] = nn(jnp.concatenate(sums, axis=0), squeeze()).astype(BF16)
    start_class(zg_copy)
    for half in range(2):
        start_class(f_copy, half)
    state = newton_steps([gram], state, 3)
    wait_class(zg_copy)
    octant = iota((1, SCREEN), 1)
    octant = jnp.where(octant < GROUP, (octant * 10923) >> 18, -1)
    across = []
    for a in range(N_PAIR):
        b = ((zl + a // 4) % 2) * 4 + ((yl + (a // 2) % 2) % 2) * 2 + (xl + a % 2) % 2
        both = zg[b].astype(F32)
        across.append(both[2 * KNOTS:3 * KNOTS] + both[3 * KNOTS:4 * KNOTS])
    zrow = []
    for a in range(N_PAIR):
        both = zg[a].astype(F32)
        here = both[0:KNOTS] + both[KNOTS:2 * KNOTS]
        for m in range(N_PAIR):
            here = here + jnp.where(octant == m, across[a ^ m], 0.0)
        zrow.append(here[:, 0:GROUP])
    zhi, zlo = split2(jnp.concatenate(zrow, axis=1))
    both = nt(jnp.concatenate([zhi, zlo], axis=0), lhs[...])
    wt = both[0:KNOTS] + both[KNOTS:2 * KNOTS]
    w0 = wt[:, 0:DATES] - p3t(wt[:, F0_AT:F1_AT], c0)
    q = p3t(w0, ends)
    for n in range(4):
        lo = n * OWN
        wq[n] = jnp.concatenate([
            q[:, 0:NB], q[:, NB + lo:NB + lo + OWN], q[:, NB + NEAR + lo:NB + NEAR + lo + OWN],
            jnp.zeros((KNOTS, 128 - NB - 2 * OWN), F32),
            wt[:, F1_AT:D1_AT], wt[:, D1_AT + lo:D1_AT + lo + OWN], jnp.zeros((KNOTS, 128 - NB - OWN), F32),
        ], axis=1)
    start_residue(w_copy)
    wg[me] = wq[me // 4]
    state = newton_steps([gram], state, 3)
    (h,) = newton_end([gram], state)
    mine = zl * 2 + yl
    c1_own = c1[0:OWN]
    for n in range(1, 4):
        c1_own = jnp.where(mine == n, c1[n * OWN:(n + 1) * OWN], c1_own)
    totals = []
    for half in range(2):
        wait_class(f_copy, half)
        total = cr[half, 0].astype(F32)
        for p in range(1, N_PAIR):
            total = total + cr[half, p].astype(F32)
        totals.append(total)
    total = jnp.concatenate(totals, axis=1)
    wait_residue(w_copy)

    wt_ref[...] = wg[...].reshape(SCREEN, 2 * 128)
    h_ref[...] = h
    total_ref[...] = total
    kn_ref[...] = bhi[group]
    c1_ref[...] = c1_own

    def drain_residue(i):
        other = residue_peer(i)
        for half in range(2):
            for part in range(PARTS):
                y_copy(other, me, half, part).wait_send()
            zs_copy(other, me, half).wait_send()
        for copy in (gs_copy, gg_copy, w_copy):
            copy(other, me).wait_send()

    loop(1, N_TILE, drain_residue)

    def drain_class(i):
        other = class_peer(i)
        for copy in (c_copy, zg_copy):
            copy(other, group).wait_send()
        for half in range(2):
            f_copy(other, group, half).wait_send()

    loop(1, N_PAIR, drain_class)


def tail_kernel(wt_ref, h_ref, total_ref, kn_ref, c1_ref, co_ref, sc_ref):
    wt, h = wt_ref[...], h_ref[...]
    q0 = wt[:, 0:128]
    q1 = p3(h, q0)
    ehi, elo = split2(q1[:, 0:NB].T)
    knots = kn_ref[...]
    co_ref[...] = total_ref[...] - (nn(ehi, knots) + nn(elo, knots))
    step = wt[:, 128:128 + NB + OWN] - (q0[:, 0:NB + OWN] - q1[:, 0:NB + OWN])
    change = step[:, NB:] - p3t(step[:, 0:NB], c1_ref[...])
    s2 = q1[:, NB + OWN:NB + 2 * OWN] + p3(h, change)
    sc_ref[...] = s2.T[0:38]


def local(phases, pair_dates, weights, coords):
    vmem = pl.BlockSpec(memory_space=pltpu.VMEM)
    shape = jax.ShapeDtypeStruct
    dma = pltpu.SemaphoreType.DMA
    tiles, pairs = dma((N_TILE,)), dma((N_PAIR,))
    twos, halves, parts = dma((2, N_PAIR)), dma((2, N_TILE)), dma((2, N_TILE, PARTS))
    parts_out = pl.pallas_call(
        mega_kernel,
        out_shape=[
            shape((SCREEN, 2 * 128), F32), shape((SCREEN, SCREEN), F32), shape((NB, PIX), F32),
            shape((SCREEN, PIX), BF16), shape((OWN, NB), F32),
        ],
        in_specs=[pl.BlockSpec(memory_space=pl.ANY)] + [vmem] * 3,
        out_specs=[vmem] * 5,
        scratch_shapes=[
            pltpu.VMEM((PAIRS, NPIX), BF16),
            dma,
            pltpu.VMEM((N_PAIR, PIX // 128, 128), jnp.int32),
            pltpu.VMEM((2, N_TILE, 6, SLOTS, HALF), BF16),
            pltpu.VMEM((2, N_TILE, 6, SLOTS, HALF), BF16),
            pltpu.VMEM((N_PAIR, SCREEN, PIX), BF16),
            pltpu.VMEM((SCREEN, PIX), BF16),
            pltpu.VMEM((2, N_PAIR, SCREEN, HALF), BF16),
            pltpu.VMEM((N_TILE, KNOTS, SCREEN), F32),
            pltpu.VMEM((N_TILE, KNOTS, SCREEN), F32),
            pltpu.VMEM((N_TILE, KNOTS, SCREEN), F32),
            pltpu.VMEM((2, N_TILE, KNOTS, SCREEN), F32),
            pltpu.VMEM((2, N_TILE, KNOTS, SCREEN), F32),
            pltpu.VMEM((N_PAIR, 4 * KNOTS, SCREEN), BF16),
            pltpu.VMEM((4, KNOTS, 2 * 128), F32),
            pltpu.VMEM((N_TILE, KNOTS, 2 * 128), F32),
            pltpu.VMEM((2, N_PAIR, NB, HALF), BF16),
            pltpu.VMEM((2, N_PAIR, NB, HALF), BF16),
            pltpu.VMEM((ROWS, KP), BF16),
            pairs, pairs, parts, parts, tiles, tiles, tiles, tiles,
            halves, halves, pairs, pairs, tiles, tiles, twos, twos,
        ],
        compiler_params=pltpu.CompilerParams(
            collective_id=0, has_side_effects=True, vmem_limit_bytes=VMEM_LIMIT
        ),
        name="mega",
    )(phases, coords, pair_dates.T, weights)
    return pl.pallas_call(
        tail_kernel,
        out_shape=[shape((NB, PIX), F32), shape((38, SCREEN), F32)],
        in_specs=[vmem] * 5,
        out_specs=[vmem] * 2,
        compiler_params=pltpu.CompilerParams(vmem_limit_bytes=VMEM_LIMIT),
        name="tail",
    )(*parts_out)


def solution(mesh):
    return jax.shard_map(
        local,
        mesh=mesh,
        in_specs=(P(("pair", "tile"), None), P(), P(), P(None, ("pair", "tile"))),
        out_specs=(P(None, ("pair", "tile")), P("pair", None)),
        check_vma=False,
    )
```

```python
import functools

import jax
import jax.numpy as jnp
from jax import lax
from jax.experimental import pallas as pl
from jax.experimental.pallas import tpu as pltpu
from jax.sharding import PartitionSpec as P

MESH = pl.DeviceIdType.MESH
HI = lax.Precision.HIGHEST
F32, BF16 = jnp.float32, jnp.bfloat16
DATES, NB, KNOTS, FRAME, SCREEN = 304, 32, 16, 4096, 256
PAIRS, SLOTS, DEVICES, PIX = 12, 16, 128, 1024
NPIX = DEVICES * PIX
N_TILE = 16
EVEN, ODD = 160, 144
KP = PAIRS * DEVICES
GROUP = PAIRS * N_TILE
OWN = 40
N_PAIR = 8
NEAR = 160
F0_AT, F1_AT, D1_AT, ROWS = 384, 416, 448, 608
HALF = PIX // 2
PARTS = 1
VMEM_LIMIT = 60 * 1024 * 1024

def nn(a, b, precision=None):
    return lax.dot_general(a, b, (((1,), (0,)), ((), ())), precision=precision, preferred_element_type=F32)

def nt(a, b, precision=None):
    return lax.dot_general(a, b, (((1,), (1,)), ((), ())), precision=precision, preferred_element_type=F32)

def tn(a, b, precision=None):
    return lax.dot_general(a, b, (((0,), (0,)), ((), ())), precision=precision, preferred_element_type=F32)

def split2(x):
    hi = x.astype(BF16)
    return hi, (x - hi.astype(F32)).astype(BF16)

def spline(s):
    a = jnp.abs(s)
    r = jnp.maximum(2.0 - a, 0.0)
    q = jnp.maximum(1.0 - a, 0.0)
    return (r * r * r - 4.0 * (q * q * q)) * (1.0 / 6.0)

def date_of(r):
    rr = jnp.where(r < EVEN, r, r - EVEN)
    base = ((rr >> 4) << 5) + (rr & 15)
    return jnp.where(r < EVEN, base, base + 16)

def iota(shape, dim):
    return lax.broadcasted_iota(jnp.int32, shape, dim)

def block_inverse(c):
    n = c.shape[1]
    row = iota((1, n, n), 1)
    col = iota((1, n, n), 2)
    for j in range(n):
        prow = c[:, j:j + 1, :]
        pcol = c[:, :, j:j + 1]
        d = 1.0 / c[:, j:j + 1, j:j + 1]
        newrow = jnp.where(col[:, :1, :] == j, 1.0, prow) * d
        base = jnp.where(col == j, 0.0, c)
        c = jnp.where(row == j, newrow, base - pcol * newrow)
    return c

def product3(a, b):
    (ah, al), (bh, bl) = a, b
    return nn(ah, bh) + (nn(ah, bl) + nn(al, bh))

def p3(a, b):
    return product3(split2(a), split2(b))

def p3t(a, b):
    (ah, al), (bh, bl) = split2(a), split2(b)
    return nt(ah, bh) + (nt(ah, bl) + nt(al, bh))

def newton_start(mats, floors):
    xs, lows = [], []
    for m, floor in zip(mats, floors):
        n = m.shape[0]
        top = jnp.max(jnp.sum(jnp.abs(m), axis=1, keepdims=True), axis=0, keepdims=True)
        c = 2.0 / (top + floor)
        low = c * floor
        ab = low * (2.0 - low)
        k = 2.0 / (1.0 + ab)
        diagonal = iota((n, n), 0) == iota((n, n), 1)
        xs.append((jnp.where(diagonal, 2.0, 0.0) - m * c) * (c * k))
        lows.append(ab * k)
    return xs, lows

def newton_steps(mats, state, steps):
    parts = [split2(m) for m in mats]
    def body(_, carry):
        xs, lows = carry
        nx, nl = [], []
        halves = [split2(x) for x in xs]
        ys = [product3(m, x) for m, x in zip(parts, halves)]
        for x, y, low in zip(halves, ys, lows):
            n = y.shape[0]
            ab = low * (2.0 - low)
            k = 2.0 / (1.0 + ab)
            eye = jnp.where(iota((n, n), 0) == iota((n, n), 1), 2.0, 0.0)
            nx.append(product3(x, split2(eye - y)) * k)
            nl.append(ab * k)
        return nx, nl
    return lax.fori_loop(0, steps, body, state)

def newton_end(mats, state):
    out = []
    for m, x in zip(mats, state[0]):
        n = m.shape[0]
        eye = jnp.where(iota((n, n), 0) == iota((n, n), 1), 2.0, 0.0)
        out.append(nn(x, eye - nn(m, x, HI), HI))
    return out

def near_dates(quarter):
    row, col = iota((NEAR, DATES), 0), iota((NEAR, DATES), 1)
    q = jnp.where(row >= 2 * OWN, jnp.where(row >= 3 * OWN, 3, 2), jnp.where(row >= OWN, 1, 0))
    i = row - OWN * q
    return jnp.where((38 * (4 * quarter + q) + i == date_of(col)) & (i < 38), 1.0, 0.0)

def by_group(x):
    lane = iota((8, KP), 1)
    t = (lane * 21846) >> 18
    delta = ((t >> 4) & 3) - ((t >> 2) & 3)
    out = x
    for d in (-3, -2, -1, 1, 2, 3):
        out = jnp.where(delta == d, pltpu.roll(x, (144 * d) % KP, 1), out)
    return out

def incidence_rows(pd):
    t = date_of(iota((DATES, KP), 0))
    later = jnp.where(t == pd[1:2, :], 1.0, 0.0)
    return later - jnp.where(t == pd[0:1, :], 1.0, 0.0)

def design_rows(at16):
    tt = date_of(iota((DATES, NB), 0)).astype(F32) * ((NB - 3.0) / (DATES - 1.0))
    t1 = spline(tt - (iota((DATES, NB), 1).astype(F32) - 1.0)).T
    a = t1.astype(BF16)
    r = t1 - a.astype(F32)
    b, c = split2(r)
    return nn(a, at16) + nn(b, at16) + nn(c, at16)

def normal_parts(at, at16, xt, w):
    eye = jnp.where(iota((DATES, DATES), 0) == iota((DATES, DATES), 1), 1.0, 0.0)
    fold = jnp.where((iota((EVEN, 16), 0) & 15) == iota((EVEN, 16), 1), 1.0, 0.0)
    mask = (iota((EVEN, EVEN), 0) >> 4) == (iota((EVEN, EVEN), 1) >> 4)
    ns, comps, fits = [], [], []
    for i in range(2):
        wi = w[i:i + 1, :]
        hi, lo = split2(wi)
        n = nt((at * hi.astype(F32)).astype(BF16), at16) + nt((at * lo.astype(F32)).astype(BF16), at16) + eye
        ns.append(n)
        comps.append(nn(jnp.where(mask, n[:EVEN, :EVEN], 0.0), fold, HI).reshape(10, 16, 16))
        fits.append(nt(xt * wi, xt, HI) + jnp.where(iota((NB, NB), 0) == iota((NB, NB), 1), 0.5, 0.0))
    return ns, comps, fits

def eliminate_even(ns, comps):
    fold = jnp.where((iota((EVEN, 16), 0) & 15) == iota((EVEN, 16), 1), 1.0, 0.0)
    mask = (iota((EVEN, EVEN), 0) >> 4) == (iota((EVEN, EVEN), 1) >> 4)
    inv = block_inverse(jnp.concatenate(comps, axis=0))
    firsts, links, schurs = [], [], []
    for i in range(2):
        compact = inv[10 * i:10 * i + 10].reshape(EVEN, 16)
        first = jnp.where(mask, nt(compact, fold, HI), 0.0)
        e = ns[i][:EVEN, EVEN:]
        y = nn(first, e, HI)
        schurs.append(ns[i][EVEN:, EVEN:] - tn(e, y, HI))
        firsts.append(first)
        links.append(y)
    return firsts, links, schurs

def full_inverse(first, link, last):
    right = p3(link, last)
    top = jnp.concatenate([first + p3t(right, link), -right], axis=1)
    bottom = jnp.concatenate([-right.T, last], axis=1)
    return jnp.concatenate([top, bottom], axis=0)

def date_solve(inverse, at16, wi):
    hi, lo = split2(inverse)
    return ((nn(hi, at16) + nn(lo, at16)) * wi).astype(BF16)

def spread_own(group_of_residue):
    row, col = iota((KP, SCREEN), 0), iota((KP, SCREEN), 1)
    group = group_of_residue(iota((1, SCREEN), 1) >> 4)
    inside = (col & 15) < PAIRS
    return jnp.where((row == GROUP * group + PAIRS * (col >> 4) + (col & 15)) & inside, 1.0, 0.0).astype(BF16)

def squeeze():
    row, col = iota((SCREEN, SCREEN), 0), iota((SCREEN, SCREEN), 1)
    inside = (row & 15) < PAIRS
    return jnp.where((col == PAIRS * (row >> 4) + (row & 15)) & inside, 1.0, 0.0).astype(BF16)

def knot_rows(code, centers):
    scale = (KNOTS - 3.0) / FRAME
    rows = spline((code >> 16).astype(F32) * scale - centers)
    cols = spline((code & 65535).astype(F32) * scale - centers)
    return rows, cols


def mega_kernel(
    ph_hbm, ck_ref, pd_ref, w_ref, wt_ref, h_ref, total_ref, kn_ref, c1_ref,
    ph_ref, ph_sem, cg, sb, rb, bhi, blo_ref, ybuf, gs, gr, gg, zs, zr, zg, wq, wg, cp, cr, lhs,
    c_send, c_recv, y_send, y_recv, gs_send, gs_recv, gg_send, gg_recv,
    zs_send, zs_recv, zg_send, zg_recv, w_send, w_recv, f_send, f_recv,
):
    pair, tile = lax.axis_index("pair"), lax.axis_index("tile")
    zh, zl, yl = pair >> 2, (pair >> 1) & 1, pair & 1
    yh, xh, xl, core = tile >> 3, (tile >> 2) & 1, (tile >> 1) & 1, tile & 1
    me = zl * 8 + yl * 4 + xl * 2 + core
    group = zh * 4 + yh * 2 + xh

    def place(a, r):
        return (a >> 2) * 4 + (r >> 2), ((a >> 1) & 1) * 8 + (a & 1) * 4 + (r & 3)

    def group_at(r, half):
        if half == 0:
            return group
        return (
            ((zh + zl + (r >> 3)) & 1) * 4 + ((yh + yl + (r >> 2)) & 1) * 2 + ((xh + xl + (r >> 1)) & 1)
        )

    def residue_peer(i):
        t = me + i
        return jnp.where(t >= N_TILE, t - N_TILE, t)

    def class_peer(i):
        t = group + i
        return jnp.where(t >= N_PAIR, t - N_PAIR, t)

    def residue_far(i):
        k = N_TILE - i
        return (
            ((zl + (k >> 3)) & 1) * 8 + ((yl + (k >> 2)) & 1) * 4 + ((xl + (k >> 1)) & 1) * 2 + ((core + k) & 1)
        )

    def class_far(i):
        k = N_PAIR - i
        return ((zh + (k >> 2)) & 1) * 4 + ((yh + (k >> 1)) & 1) * 2 + ((xh + k) & 1)

    def loop(lo, hi, f):
        def body(i, carry):
            f(i)
            return carry
        lax.fori_loop(lo, hi, body, 0)

    def to_residue(src, dst, send, recv, other, half=0):
        return pltpu.make_async_remote_copy(
            src_ref=src, dst_ref=dst, send_sem=send, recv_sem=recv,
            device_id=place(group_at(other, half), other), device_id_type=MESH,
        )

    def to_class(src, dst, send, recv, other, slot):
        return pltpu.make_async_remote_copy(
            src_ref=src, dst_ref=dst.at[slot], send_sem=send.at[other], recv_sem=recv.at[slot],
            device_id=place(other, me), device_id_type=MESH,
        )

    def c_copy(other, slot):
        return to_class(cg.at[group], cg, c_send, c_recv, other, slot)

    def y_copy(other, slot, half, part):
        rows = pl.ds(6 * part, 6)
        return to_residue(
            sb.at[half, other, rows], rb.at[half, slot, rows],
            y_send.at[half, other, part], y_recv.at[half, slot, part], other, half,
        )

    def gs_copy(other, slot):
        return to_residue(gs.at[other], gr.at[slot], gs_send.at[other], gs_recv.at[slot], other)

    def gg_copy(other, slot):
        return to_residue(gg.at[me], gg.at[slot], gg_send.at[other], gg_recv.at[slot], other)

    def zs_copy(other, slot, half):
        return to_residue(
            zs.at[half, other], zr.at[half, slot], zs_send.at[half, other], zs_recv.at[half, slot], other, half
        )

    def zg_copy(other, slot):
        return to_class(zg.at[group], zg, zg_send, zg_recv, other, slot)

    def w_copy(other, slot):
        return to_residue(wq.at[other // 4], wg.at[slot], w_send.at[other], w_recv.at[slot], other)

    def f_copy(other, slot, half):
        return to_class(cp.at[half, other], cr.at[half], f_send.at[half], f_recv.at[half], other, slot)

    def start_residue(copy, *more):
        loop(1, N_TILE, lambda i: copy(residue_far(i), me, *more).start())

    def wait_residue(copy, *more):
        loop(1, N_TILE, lambda i: copy(residue_peer(i), residue_peer(i), *more).wait_recv())

    def sent_residue(copy, *more):
        loop(1, N_TILE, lambda i: copy(residue_peer(i), me, *more).wait_send())

    def sent_class(copy, *more):
        loop(1, N_PAIR, lambda i: copy(class_peer(i), group, *more).wait_send())

    def start_class(copy, *more):
        loop(1, N_PAIR, lambda i: copy(class_far(i), group, *more).start())

    def wait_class(copy, *more):
        loop(1, N_PAIR, lambda i: copy(class_peer(i), class_peer(i), *more).wait_recv())

    load = pltpu.make_async_copy(ph_hbm, ph_ref, ph_sem)
    load.start()
    barrier = pltpu.get_barrier_semaphore()

    def greet(where):
        pl.semaphore_signal(barrier, inc=1, device_id=where, device_id_type=MESH)

    loop(1, N_PAIR, lambda i: greet(place(class_far(i), me)))
    for half in range(2):
        loop(1, N_TILE, lambda i, half=half: greet(place(group_at(residue_far(i), half), residue_far(i))))

    pl.semaphore_wait(barrier, 2 * N_TILE + N_PAIR - 3)

    code = ck_ref[0:1, :] * 65536 + ck_ref[1:2, :]
    cg[group] = jnp.concatenate([code[:, i * 128:(i + 1) * 128] for i in range(PIX // 128)], axis=0)
    start_class(c_copy)

    load.wait()

    def pack(other, half, dst):
        blocks = []
        for a in range(N_PAIR):
            p, t = place(a, other)
            first = pl.multiple_of((p * N_TILE + t) * PIX + half * HALF, HALF)
            blocks.append(ph_ref[:, pl.ds(first, HALF)].astype(F32))
        for a in range(4):
            two = jnp.concatenate([blocks[2 * a][0:8], blocks[2 * a + 1][0:8]], axis=0)
            dst[a] = two.astype(BF16)
        for a in range(2):
            four = jnp.concatenate([blocks[4 * a + q][8:12] for q in range(4)], axis=0)
            dst[4 + a] = four.astype(BF16)

    def y_start(i, half):
        other = residue_peer(i)
        pack(other, half, sb.at[half, other])
        for part in range(PARTS):
            y_copy(other, me, half, part).start()

    for half in range(2):
        loop(1, N_TILE, lambda i, half=half: y_start(i, half))
    for half in range(2):
        pack(me, half, rb.at[half, me])

    rows = jnp.concatenate([pd_ref[...].astype(F32), w_ref[...], jnp.zeros((4, KP), F32)], axis=0)
    rows = by_group(rows)
    w = rows[2:4, :]
    at = incidence_rows(rows[0:2, :].astype(jnp.int32))
    at16 = at.astype(BF16)
    xt = design_rows(at16)
    normals, evens, fits = normal_parts(at, at16, xt, w)
    firsts, links, schurs = eliminate_even(normals, evens)
    lasts = newton_start(schurs + fits, [1.0, 1.0, 0.5, 0.5])
    lasts = newton_steps(schurs + fits, lasts, 8)
    last0, last1, f0, f1 = newton_end(schurs + fits, lasts)

    sel = near_dates(zh)
    fit0 = (p3(f0, xt) * w[0:1, :]).astype(BF16)
    fit1 = (p3(f1, xt) * w[1:2, :]).astype(BF16)
    d0 = date_solve(full_inverse(firsts[0], links[0], last0), at16, w[0:1, :])
    d1 = date_solve(p3(sel, full_inverse(firsts[1], links[1], last1)), at16, w[1:2, :])
    lhs[0:DATES] = d0
    lhs[DATES:F0_AT] = jnp.zeros((F0_AT - DATES, KP), BF16)
    lhs[F0_AT:D1_AT] = jnp.concatenate([fit0, fit1], axis=0)
    lhs[D1_AT:ROWS] = d1
    xhi, xlo = split2(xt)
    c0 = nt(d0, xhi) + nt(d0, xlo)
    c1 = nt(d1, xhi) + nt(d1, xlo)
    ends = jnp.concatenate([nt(fit1, at16), nt(d1, at16), sel], axis=0)
    fit_own = [nn(fit1, spread_own(functools.partial(group_at, half=half))).astype(BF16) for half in range(2)]

    wait_class(c_copy)
    centers = iota((KNOTS, 1), 0).astype(F32) - 1.0

    def knots(p, carry):
        g1, g2 = carry
        for i in range(PIX // 128):
            rows, cols = knot_rows(cg[p, i:i + 1, :], centers)
            lanes = pl.ds(i * 128, 128)
            for m in range(KNOTS):
                hi, lo = split2(rows[m:m + 1, :] * cols)
                bhi[p, m * KNOTS:(m + 1) * KNOTS, lanes] = hi
                blo_ref[m * KNOTS:(m + 1) * KNOTS, lanes] = lo
        hi = bhi[p]
        return g1 + nt(hi, hi), g2 + nt(hi, blo_ref[...])

    zero = jnp.zeros((SCREEN, SCREEN), F32)
    g1, g2 = lax.fori_loop(0, N_PAIR, knots, (zero, zero))
    gs[...] = (g1 + g2 + g2.T).reshape(N_TILE, KNOTS, SCREEN)
    start_residue(gs_copy)
    gr[me] = gs[me]


    def unpack(t, half):
        rest = [rb[half, t, 4 + a].astype(F32) for a in range(2)]
        for a in range(4):
            two = rb[half, t, a].astype(F32)
            for b in range(2):
                p = 2 * a + b
                low = rest[p // 4][4 * (p % 4):4 * (p % 4) + 4]
                block = jnp.concatenate([two[8 * b:8 * b + 8], low, jnp.zeros((4, HALF), F32)], axis=0)
                ybuf[half, p, pl.ds(pl.multiple_of(t * SLOTS, SLOTS), SLOTS), :] = block.astype(BF16)

    def y_arrive(i, half):
        other = residue_peer(i)
        for part in range(PARTS):
            y_copy(other, other, half, part).wait_recv()
        unpack(other, half)

    def z_body(p, acc, half):
        y = ybuf[half, p]
        cp[half, p] = nn(fit_own[half], y).astype(BF16)
        return acc + nt(bhi[p, :, half * HALF:(half + 1) * HALF], y)

    for half in range(2):
        unpack(me, half)
        loop(1, N_TILE, lambda i, half=half: y_arrive(N_TILE - i, half))
        zt = lax.fori_loop(0, N_PAIR, functools.partial(z_body, half=half), zero)
        zs[half] = zt.reshape(N_TILE, KNOTS, SCREEN)
        start_residue(zs_copy, half)
        zr[half, me] = zs[half, me]
        cr[half, group] = cp[half, group]
    sent_class(c_copy)
    sent_residue(gs_copy)
    for half in range(2):
        for part in range(PARTS):
            sent_residue(y_copy, half, part)
    wait_residue(gs_copy)
    gsum = gr[0]
    for t in range(1, N_TILE):
        gsum = gsum + gr[t]
    gg[me] = gsum
    start_residue(gg_copy)

    sums = []
    for half in range(2):
        wait_residue(zs_copy, half)
        zsum = zr[half, 0]
        for t in range(1, N_TILE):
            zsum = zsum + zr[half, t]
        sums.extend(split2(zsum))
    zg[group] = nn(jnp.concatenate(sums, axis=0), squeeze()).astype(BF16)
    start_class(zg_copy)
    for half in range(2):
        start_class(f_copy, half)
    wait_residue(gg_copy)
    gram = gg[...].reshape(SCREEN, SCREEN)
    gram = gram + jnp.where(iota((SCREEN, SCREEN), 0) == iota((SCREEN, SCREEN), 1), 1.0, 0.0)
    state = newton_start([gram], [1.0])
    state = newton_steps([gram], state, 5)
    sent_residue(gg_copy)
    for half in range(2):
        sent_residue(zs_copy, half)
    wait_class(zg_copy)
    octant = iota((1, SCREEN), 1)
    octant = jnp.where(octant < GROUP, (octant * 10923) >> 18, -1)
    across = []
    for a in range(N_PAIR):
        b = ((zl + a // 4) % 2) * 4 + ((yl + (a // 2) % 2) % 2) * 2 + (xl + a % 2) % 2
        both = zg[b].astype(F32)
        across.append(both[2 * KNOTS:3 * KNOTS] + both[3 * KNOTS:4 * KNOTS])
    zrow = []
    for a in range(N_PAIR):
        both = zg[a].astype(F32)
        here = both[0:KNOTS] + both[KNOTS:2 * KNOTS]
        for m in range(N_PAIR):
            here = here + jnp.where(octant == m, across[a ^ m], 0.0)
        zrow.append(here[:, 0:GROUP])
    zhi, zlo = split2(jnp.concatenate(zrow, axis=1))
    both = nt(jnp.concatenate([zhi, zlo], axis=0), lhs[...])
    wt = both[0:KNOTS] + both[KNOTS:2 * KNOTS]
    w0 = wt[:, 0:DATES] - p3t(wt[:, F0_AT:F1_AT], c0)
    q = p3t(w0, ends)
    for n in range(4):
        lo = n * OWN
        wq[n] = jnp.concatenate([
            q[:, 0:NB], q[:, NB + lo:NB + lo + OWN], q[:, NB + NEAR + lo:NB + NEAR + lo + OWN],
            jnp.zeros((KNOTS, 128 - NB - 2 * OWN), F32),
            wt[:, F1_AT:D1_AT], wt[:, D1_AT + lo:D1_AT + lo + OWN], jnp.zeros((KNOTS, 128 - NB - OWN), F32),
        ], axis=1)
    start_residue(w_copy)
    wg[me] = wq[me // 4]
    state = newton_steps([gram], state, 4)
    (h,) = newton_end([gram], state)
    sent_class(zg_copy)
    mine = zl * 2 + yl
    c1_own = c1[0:OWN]
    for n in range(1, 4):
        c1_own = jnp.where(mine == n, c1[n * OWN:(n + 1) * OWN], c1_own)
    totals = []
    for half in range(2):
        wait_class(f_copy, half)
        total = cr[half, 0].astype(F32)
        for p in range(1, N_PAIR):
            total = total + cr[half, p].astype(F32)
        totals.append(total)
    total = jnp.concatenate(totals, axis=1)
    wait_residue(w_copy)

    wt_ref[...] = wg[...].reshape(SCREEN, 2 * 128)
    h_ref[...] = h
    total_ref[...] = total
    kn_ref[...] = bhi[group]
    c1_ref[...] = c1_own

    sent_residue(w_copy)
    for half in range(2):
        sent_class(f_copy, half)


def tail_kernel(wt_ref, h_ref, total_ref, kn_ref, c1_ref, co_ref, sc_ref):
    wt, h = wt_ref[...], h_ref[...]
    q0 = wt[:, 0:128]
    q1 = p3(h, q0)
    ehi, elo = split2(q1[:, 0:NB].T)
    knots = kn_ref[...]
    co_ref[...] = total_ref[...] - (nn(ehi, knots) + nn(elo, knots))
    step = wt[:, 128:128 + NB + OWN] - (q0[:, 0:NB + OWN] - q1[:, 0:NB + OWN])
    change = step[:, NB:] - p3t(step[:, 0:NB], c1_ref[...])
    s2 = q1[:, NB + OWN:NB + 2 * OWN] + p3(h, change)
    sc_ref[...] = s2.T[0:38]


def local(phases, pair_dates, weights, coords):
    vmem = pl.BlockSpec(memory_space=pltpu.VMEM)
    shape = jax.ShapeDtypeStruct
    dma = pltpu.SemaphoreType.DMA
    tiles, pairs = dma((N_TILE,)), dma((N_PAIR,))
    twos, halves, parts = dma((2, N_PAIR)), dma((2, N_TILE)), dma((2, N_TILE, PARTS))
    parts_out = pl.pallas_call(
        mega_kernel,
        out_shape=[
            shape((SCREEN, 2 * 128), F32), shape((SCREEN, SCREEN), F32), shape((NB, PIX), F32),
            shape((SCREEN, PIX), BF16), shape((OWN, NB), F32),
        ],
        in_specs=[pl.BlockSpec(memory_space=pl.ANY)] + [vmem] * 3,
        out_specs=[vmem] * 5,
        scratch_shapes=[
            pltpu.VMEM((PAIRS, NPIX), BF16),
            dma,
            pltpu.VMEM((N_PAIR, PIX // 128, 128), jnp.int32),
            pltpu.VMEM((2, N_TILE, 6, SLOTS, HALF), BF16),
            pltpu.VMEM((2, N_TILE, 6, SLOTS, HALF), BF16),
            pltpu.VMEM((N_PAIR, SCREEN, PIX), BF16),
            pltpu.VMEM((SCREEN, PIX), BF16),
            pltpu.VMEM((2, N_PAIR, SCREEN, HALF), BF16),
            pltpu.VMEM((N_TILE, KNOTS, SCREEN), F32),
            pltpu.VMEM((N_TILE, KNOTS, SCREEN), F32),
            pltpu.VMEM((N_TILE, KNOTS, SCREEN), F32),
            pltpu.VMEM((2, N_TILE, KNOTS, SCREEN), F32),
            pltpu.VMEM((2, N_TILE, KNOTS, SCREEN), F32),
            pltpu.VMEM((N_PAIR, 4 * KNOTS, SCREEN), BF16),
            pltpu.VMEM((4, KNOTS, 2 * 128), F32),
            pltpu.VMEM((N_TILE, KNOTS, 2 * 128), F32),
            pltpu.VMEM((2, N_PAIR, NB, HALF), BF16),
            pltpu.VMEM((2, N_PAIR, NB, HALF), BF16),
            pltpu.VMEM((ROWS, KP), BF16),
            pairs, pairs, parts, parts, tiles, tiles, tiles, tiles,
            halves, halves, pairs, pairs, tiles, tiles, twos, twos,
        ],
        compiler_params=pltpu.CompilerParams(
            collective_id=0, has_side_effects=True, vmem_limit_bytes=VMEM_LIMIT
        ),
        name="mega",
    )(phases, coords, pair_dates.T, weights)
    return pl.pallas_call(
        tail_kernel,
        out_shape=[shape((NB, PIX), F32), shape((38, SCREEN), F32)],
        in_specs=[vmem] * 5,
        out_specs=[vmem] * 2,
        compiler_params=pltpu.CompilerParams(vmem_limit_bytes=VMEM_LIMIT),
        name="tail",
    )(*parts_out)


def solution(mesh):
    return jax.shard_map(
        local,
        mesh=mesh,
        in_specs=(P(("pair", "tile"), None), P(), P(), P(None, ("pair", "tile"))),
        out_specs=(P(None, ("pair", "tile")), P("pair", None)),
        check_vma=False,
    )
```

```python
import functools

import jax
import jax.numpy as jnp
from jax import lax
from jax.experimental import pallas as pl
from jax.experimental.pallas import tpu as pltpu
from jax.sharding import PartitionSpec as P

MESH = pl.DeviceIdType.MESH
HI = lax.Precision.HIGHEST
F32, BF16 = jnp.float32, jnp.bfloat16
DATES, NB, KNOTS, FRAME, SCREEN = 304, 32, 16, 4096, 256
PAIRS, SLOTS, DEVICES, PIX = 12, 16, 128, 1024
NPIX = DEVICES * PIX
N_TILE = 16
EVEN, ODD = 160, 144
KP = PAIRS * DEVICES
GROUP = PAIRS * N_TILE
OWN = 40
N_PAIR = 8
NEAR = 160
F0_AT, F1_AT, D1_AT, ROWS = 384, 416, 448, 608
HALF = PIX // 2
PARTS = 1
VMEM_LIMIT = 60 * 1024 * 1024

def nn(a, b, precision=None):
    return lax.dot_general(a, b, (((1,), (0,)), ((), ())), precision=precision, preferred_element_type=F32)

def nt(a, b, precision=None):
    return lax.dot_general(a, b, (((1,), (1,)), ((), ())), precision=precision, preferred_element_type=F32)

def tn(a, b, precision=None):
    return lax.dot_general(a, b, (((0,), (0,)), ((), ())), precision=precision, preferred_element_type=F32)

def split2(x):
    hi = x.astype(BF16)
    return hi, (x - hi.astype(F32)).astype(BF16)

def spline(s):
    a = jnp.abs(s)
    r = jnp.maximum(2.0 - a, 0.0)
    q = jnp.maximum(1.0 - a, 0.0)
    return (r * r * r - 4.0 * (q * q * q)) * (1.0 / 6.0)

def date_of(r):
    rr = jnp.where(r < EVEN, r, r - EVEN)
    base = ((rr >> 4) << 5) + (rr & 15)
    return jnp.where(r < EVEN, base, base + 16)

def iota(shape, dim):
    return lax.broadcasted_iota(jnp.int32, shape, dim)

def block_inverse(c):
    n = c.shape[1]
    row = iota((1, n, n), 1)
    col = iota((1, n, n), 2)
    for j in range(n):
        prow = c[:, j:j + 1, :]
        pcol = c[:, :, j:j + 1]
        d = 1.0 / c[:, j:j + 1, j:j + 1]
        newrow = jnp.where(col[:, :1, :] == j, 1.0, prow) * d
        base = jnp.where(col == j, 0.0, c)
        c = jnp.where(row == j, newrow, base - pcol * newrow)
    return c

def product3(a, b):
    (ah, al), (bh, bl) = a, b
    return nn(ah, bh) + (nn(ah, bl) + nn(al, bh))

def p3(a, b):
    return product3(split2(a), split2(b))

def p3t(a, b):
    (ah, al), (bh, bl) = split2(a), split2(b)
    return nt(ah, bh) + (nt(ah, bl) + nt(al, bh))

def newton_start(mats, floors):
    xs, lows = [], []
    for m, floor in zip(mats, floors):
        n = m.shape[0]
        top = jnp.max(jnp.sum(jnp.abs(m), axis=1, keepdims=True), axis=0, keepdims=True)
        c = 2.0 / (top + floor)
        low = c * floor
        ab = low * (2.0 - low)
        k = 2.0 / (1.0 + ab)
        diagonal = iota((n, n), 0) == iota((n, n), 1)
        xs.append((jnp.where(diagonal, 2.0, 0.0) - m * c) * (c * k))
        lows.append(ab * k)
    return xs, lows

def newton_steps(mats, state, steps):
    parts = [split2(m) for m in mats]
    def body(_, carry):
        xs, lows = carry
        nx, nl = [], []
        halves = [split2(x) for x in xs]
        ys = [product3(m, x) for m, x in zip(parts, halves)]
        for x, y, low in zip(halves, ys, lows):
            n = y.shape[0]
            ab = low * (2.0 - low)
            k = 2.0 / (1.0 + ab)
            eye = jnp.where(iota((n, n), 0) == iota((n, n), 1), 2.0, 0.0)
            nx.append(product3(x, split2(eye - y)) * k)
            nl.append(ab * k)
        return nx, nl
    return lax.fori_loop(0, steps, body, state)

def newton_end(mats, state):
    out = []
    for m, x in zip(mats, state[0]):
        n = m.shape[0]
        eye = jnp.where(iota((n, n), 0) == iota((n, n), 1), 2.0, 0.0)
        out.append(nn(x, eye - nn(m, x, HI), HI))
    return out

def near_dates(quarter):
    row, col = iota((NEAR, DATES), 0), iota((NEAR, DATES), 1)
    q = jnp.where(row >= 2 * OWN, jnp.where(row >= 3 * OWN, 3, 2), jnp.where(row >= OWN, 1, 0))
    i = row - OWN * q
    return jnp.where((38 * (4 * quarter + q) + i == date_of(col)) & (i < 38), 1.0, 0.0)

def by_group(x):
    lane = iota((8, KP), 1)
    t = (lane * 21846) >> 18
    delta = ((t >> 4) & 3) - ((t >> 2) & 3)
    out = x
    for d in (-3, -2, -1, 1, 2, 3):
        out = jnp.where(delta == d, pltpu.roll(x, (144 * d) % KP, 1), out)
    return out

def incidence_rows(pd):
    t = date_of(iota((DATES, KP), 0))
    later = jnp.where(t == pd[1:2, :], 1.0, 0.0)
    return later - jnp.where(t == pd[0:1, :], 1.0, 0.0)

def design_rows(at16):
    tt = date_of(iota((DATES, NB), 0)).astype(F32) * ((NB - 3.0) / (DATES - 1.0))
    t1 = spline(tt - (iota((DATES, NB), 1).astype(F32) - 1.0)).T
    a = t1.astype(BF16)
    r = t1 - a.astype(F32)
    b, c = split2(r)
    return nn(a, at16) + nn(b, at16) + nn(c, at16)

def normal_parts(at, at16, xt, w):
    eye = jnp.where(iota((DATES, DATES), 0) == iota((DATES, DATES), 1), 1.0, 0.0)
    fold = jnp.where((iota((EVEN, 16), 0) & 15) == iota((EVEN, 16), 1), 1.0, 0.0)
    mask = (iota((EVEN, EVEN), 0) >> 4) == (iota((EVEN, EVEN), 1) >> 4)
    ns, comps, fits = [], [], []
    for i in range(2):
        wi = w[i:i + 1, :]
        hi, lo = split2(wi)
        n = nt((at * hi.astype(F32)).astype(BF16), at16) + nt((at * lo.astype(F32)).astype(BF16), at16) + eye
        ns.append(n)
        comps.append(nn(jnp.where(mask, n[:EVEN, :EVEN], 0.0), fold, HI).reshape(10, 16, 16))
        fits.append(nt(xt * wi, xt, HI) + jnp.where(iota((NB, NB), 0) == iota((NB, NB), 1), 0.5, 0.0))
    return ns, comps, fits

def eliminate_even(ns, comps):
    fold = jnp.where((iota((EVEN, 16), 0) & 15) == iota((EVEN, 16), 1), 1.0, 0.0)
    mask = (iota((EVEN, EVEN), 0) >> 4) == (iota((EVEN, EVEN), 1) >> 4)
    inv = block_inverse(jnp.concatenate(comps, axis=0))
    firsts, links, schurs = [], [], []
    for i in range(2):
        compact = inv[10 * i:10 * i + 10].reshape(EVEN, 16)
        first = jnp.where(mask, nt(compact, fold, HI), 0.0)
        e = ns[i][:EVEN, EVEN:]
        y = nn(first, e, HI)
        schurs.append(ns[i][EVEN:, EVEN:] - tn(e, y, HI))
        firsts.append(first)
        links.append(y)
    return firsts, links, schurs

def full_inverse(first, link, last):
    right = p3(link, last)
    top = jnp.concatenate([first + p3t(right, link), -right], axis=1)
    bottom = jnp.concatenate([-right.T, last], axis=1)
    return jnp.concatenate([top, bottom], axis=0)

def date_solve(inverse, at16, wi):
    hi, lo = split2(inverse)
    return ((nn(hi, at16) + nn(lo, at16)) * wi).astype(BF16)

def spread_own(group_of_residue):
    row, col = iota((KP, SCREEN), 0), iota((KP, SCREEN), 1)
    group = group_of_residue(iota((1, SCREEN), 1) >> 4)
    inside = (col & 15) < PAIRS
    return jnp.where((row == GROUP * group + PAIRS * (col >> 4) + (col & 15)) & inside, 1.0, 0.0).astype(BF16)

def squeeze():
    row, col = iota((SCREEN, SCREEN), 0), iota((SCREEN, SCREEN), 1)
    inside = (row & 15) < PAIRS
    return jnp.where((col == PAIRS * (row >> 4) + (row & 15)) & inside, 1.0, 0.0).astype(BF16)

def knot_rows(code, centers):
    scale = (KNOTS - 3.0) / FRAME
    rows = spline((code >> 16).astype(F32) * scale - centers)
    cols = spline((code & 65535).astype(F32) * scale - centers)
    return rows, cols


def mega_kernel(
    ph_hbm, ck_ref, pd_ref, w_ref, wt_ref, h_ref, total_ref, kn_ref, c1_ref,
    ph_ref, ph_sem, cg, sb, rb, bhi, blo_ref, ybuf, gs, gr, gg, zs, zr, zg, wq, wg, cp, cr, lhs,
    c_send, c_recv, y_send, y_recv, gs_send, gs_recv, gg_send, gg_recv,
    zs_send, zs_recv, zg_send, zg_recv, w_send, w_recv, f_send, f_recv,
):
    pair, tile = lax.axis_index("pair"), lax.axis_index("tile")
    zh, zl, yl = pair >> 2, (pair >> 1) & 1, pair & 1
    yh, xh, xl, core = tile >> 3, (tile >> 2) & 1, (tile >> 1) & 1, tile & 1
    me = zl * 8 + yl * 4 + xl * 2 + core
    group = zh * 4 + yh * 2 + xh

    def place(a, r):
        return (a >> 2) * 4 + (r >> 2), ((a >> 1) & 1) * 8 + (a & 1) * 4 + (r & 3)

    def group_at(r, half):
        if half == 0:
            return group
        return (
            ((zh + zl + (r >> 3)) & 1) * 4 + ((yh + yl + (r >> 2)) & 1) * 2 + ((xh + xl + (r >> 1)) & 1)
        )

    def residue_peer(i):
        t = me + i
        return jnp.where(t >= N_TILE, t - N_TILE, t)

    def class_peer(i):
        t = group + i
        return jnp.where(t >= N_PAIR, t - N_PAIR, t)

    def residue_far(i):
        k = N_TILE - i
        return (
            ((zl + (k >> 3)) & 1) * 8 + ((yl + (k >> 2)) & 1) * 4 + ((xl + (k >> 1)) & 1) * 2 + ((core + k) & 1)
        )

    def class_far(i):
        k = N_PAIR - i
        return ((zh + (k >> 2)) & 1) * 4 + ((yh + (k >> 1)) & 1) * 2 + ((xh + k) & 1)

    def loop(lo, hi, f):
        def body(i, carry):
            f(i)
            return carry
        lax.fori_loop(lo, hi, body, 0)

    def to_residue(src, dst, send, recv, other, half=0):
        return pltpu.make_async_remote_copy(
            src_ref=src, dst_ref=dst, send_sem=send, recv_sem=recv,
            device_id=place(group_at(other, half), other), device_id_type=MESH,
        )

    def to_class(src, dst, send, recv, other, slot):
        return pltpu.make_async_remote_copy(
            src_ref=src, dst_ref=dst.at[slot], send_sem=send.at[other], recv_sem=recv.at[slot],
            device_id=place(other, me), device_id_type=MESH,
        )

    def c_copy(other, slot):
        return to_class(cg.at[group], cg, c_send, c_recv, other, slot)

    def y_copy(other, slot, half, part):
        rows = pl.ds(6 * part, 6)
        return to_residue(
            sb.at[half, other, rows], rb.at[half, slot, rows],
            y_send.at[half, other, part], y_recv.at[half, slot, part], other, half,
        )

    def gs_copy(other, slot):
        return to_residue(gs.at[other], gr.at[slot], gs_send.at[other], gs_recv.at[slot], other)

    def gg_copy(other, slot):
        return to_residue(gg.at[me], gg.at[slot], gg_send.at[other], gg_recv.at[slot], other)

    def zs_copy(other, slot, half):
        return to_residue(
            zs.at[half, other], zr.at[half, slot], zs_send.at[half, other], zs_recv.at[half, slot], other, half
        )

    def zg_copy(other, slot):
        return to_class(zg.at[group], zg, zg_send, zg_recv, other, slot)

    def w_copy(other, slot):
        return to_residue(wq.at[other // 4], wg.at[slot], w_send.at[other], w_recv.at[slot], other)

    def f_copy(other, slot, half):
        return to_class(cp.at[half, other], cr.at[half], f_send.at[half], f_recv.at[half], other, slot)

    def start_residue(copy, *more):
        loop(1, N_TILE, lambda i: copy(residue_far(i), me, *more).start())

    def wait_residue(copy, *more):
        loop(1, N_TILE, lambda i: copy(residue_peer(i), residue_peer(i), *more).wait_recv())

    def sent_residue(copy, *more):
        loop(1, N_TILE, lambda i: copy(residue_peer(i), me, *more).wait_send())

    def sent_class(copy, *more):
        loop(1, N_PAIR, lambda i: copy(class_peer(i), group, *more).wait_send())

    def start_class(copy, *more):
        loop(1, N_PAIR, lambda i: copy(class_far(i), group, *more).start())

    def wait_class(copy, *more):
        loop(1, N_PAIR, lambda i: copy(class_peer(i), class_peer(i), *more).wait_recv())

    load = pltpu.make_async_copy(ph_hbm, ph_ref, ph_sem)
    load.start()
    barrier = pltpu.get_barrier_semaphore()

    def greet(where):
        pl.semaphore_signal(barrier, inc=1, device_id=where, device_id_type=MESH)

    loop(1, N_PAIR, lambda i: greet(place(class_far(i), me)))
    for half in range(2):
        loop(1, N_TILE, lambda i, half=half: greet(place(group_at(residue_far(i), half), residue_far(i))))

    pl.semaphore_wait(barrier, 2 * N_TILE + N_PAIR - 3)

    code = ck_ref[0:1, :] * 65536 + ck_ref[1:2, :]
    cg[group] = jnp.concatenate([code[:, i * 128:(i + 1) * 128] for i in range(PIX // 128)], axis=0)
    start_class(c_copy)

    load.wait()

    def pack(other, half, dst):
        blocks = []
        for a in range(N_PAIR):
            p, t = place(a, other)
            first = pl.multiple_of((p * N_TILE + t) * PIX + half * HALF, HALF)
            blocks.append(ph_ref[:, pl.ds(first, HALF)].astype(F32))
        for a in range(4):
            two = jnp.concatenate([blocks[2 * a][0:8], blocks[2 * a + 1][0:8]], axis=0)
            dst[a] = two.astype(BF16)
        for a in range(2):
            four = jnp.concatenate([blocks[4 * a + q][8:12] for q in range(4)], axis=0)
            dst[4 + a] = four.astype(BF16)

    def y_start(i, half):
        other = residue_peer(i)
        pack(other, half, sb.at[half, other])
        for part in range(PARTS):
            y_copy(other, me, half, part).start()

    for half in range(2):
        loop(1, N_TILE, lambda i, half=half: y_start(i, half))
    for half in range(2):
        pack(me, half, rb.at[half, me])

    rows = jnp.concatenate([pd_ref[...].astype(F32), w_ref[...], jnp.zeros((4, KP), F32)], axis=0)
    rows = by_group(rows)
    w = rows[2:4, :]
    at = incidence_rows(rows[0:2, :].astype(jnp.int32))
    at16 = at.astype(BF16)
    xt = design_rows(at16)
    normals, evens, fits = normal_parts(at, at16, xt, w)
    firsts, links, schurs = eliminate_even(normals, evens)
    lasts = newton_start(schurs + fits, [1.0, 1.0, 0.5, 0.5])
    lasts = newton_steps(schurs + fits, lasts, 8)
    last0, last1, f0, f1 = newton_end(schurs + fits, lasts)

    sel = near_dates(zh)
    fit0 = (p3(f0, xt) * w[0:1, :]).astype(BF16)
    fit1 = (p3(f1, xt) * w[1:2, :]).astype(BF16)
    fit_own = [nn(fit1, spread_own(functools.partial(group_at, half=half))).astype(BF16) for half in range(2)]

    wait_class(c_copy)
    centers = iota((KNOTS, 1), 0).astype(F32) - 1.0

    def knots(p, carry):
        g1, g2 = carry
        for i in range(PIX // 128):
            rows, cols = knot_rows(cg[p, i:i + 1, :], centers)
            lanes = pl.ds(i * 128, 128)
            for m in range(KNOTS):
                hi, lo = split2(rows[m:m + 1, :] * cols)
                bhi[p, m * KNOTS:(m + 1) * KNOTS, lanes] = hi
                blo_ref[m * KNOTS:(m + 1) * KNOTS, lanes] = lo
        hi = bhi[p]
        return g1 + nt(hi, hi), g2 + nt(hi, blo_ref[...])

    zero = jnp.zeros((SCREEN, SCREEN), F32)
    g1, g2 = lax.fori_loop(0, N_PAIR, knots, (zero, zero))
    gs[...] = (g1 + g2 + g2.T).reshape(N_TILE, KNOTS, SCREEN)
    start_residue(gs_copy)
    gr[me] = gs[me]


    def unpack(t, half):
        rest = [rb[half, t, 4 + a].astype(F32) for a in range(2)]
        for a in range(4):
            two = rb[half, t, a].astype(F32)
            for b in range(2):
                p = 2 * a + b
                low = rest[p // 4][4 * (p % 4):4 * (p % 4) + 4]
                block = jnp.concatenate([two[8 * b:8 * b + 8], low, jnp.zeros((4, HALF), F32)], axis=0)
                ybuf[half, p, pl.ds(pl.multiple_of(t * SLOTS, SLOTS), SLOTS), :] = block.astype(BF16)

    def y_arrive(i, half):
        other = residue_peer(i)
        for part in range(PARTS):
            y_copy(other, other, half, part).wait_recv()
        unpack(other, half)

    def z_body(p, acc, half):
        y = ybuf[half, p]
        cp[half, p] = nn(fit_own[half], y).astype(BF16)
        return acc + nt(bhi[p, :, half * HALF:(half + 1) * HALF], y)

    for half in range(2):
        unpack(me, half)
        loop(1, N_TILE, lambda i, half=half: y_arrive(N_TILE - i, half))
        zt = lax.fori_loop(0, N_PAIR, functools.partial(z_body, half=half), zero)
        zs[half] = zt.reshape(N_TILE, KNOTS, SCREEN)
        start_residue(zs_copy, half)
        zr[half, me] = zs[half, me]
        cr[half, group] = cp[half, group]
    sent_class(c_copy)
    sent_residue(gs_copy)
    for half in range(2):
        for part in range(PARTS):
            sent_residue(y_copy, half, part)
    wait_residue(gs_copy)
    gsum = gr[0]
    for t in range(1, N_TILE):
        gsum = gsum + gr[t]
    gg[me] = gsum
    start_residue(gg_copy)

    d0 = date_solve(full_inverse(firsts[0], links[0], last0), at16, w[0:1, :])
    d1 = date_solve(p3(sel, full_inverse(firsts[1], links[1], last1)), at16, w[1:2, :])
    lhs[0:DATES] = d0
    lhs[DATES:F0_AT] = jnp.zeros((F0_AT - DATES, KP), BF16)
    lhs[F0_AT:D1_AT] = jnp.concatenate([fit0, fit1], axis=0)
    lhs[D1_AT:ROWS] = d1

    sums = []
    for half in range(2):
        wait_residue(zs_copy, half)
        zsum = zr[half, 0]
        for t in range(1, N_TILE):
            zsum = zsum + zr[half, t]
        sums.extend(split2(zsum))
    zg[group] = nn(jnp.concatenate(sums, axis=0), squeeze()).astype(BF16)
    start_class(zg_copy)
    for half in range(2):
        start_class(f_copy, half)
    xhi, xlo = split2(xt)
    c0 = nt(d0, xhi) + nt(d0, xlo)
    c1 = nt(d1, xhi) + nt(d1, xlo)
    ends = jnp.concatenate([nt(fit1, at16), nt(d1, at16), sel], axis=0)
    wait_residue(gg_copy)
    gram = gg[...].reshape(SCREEN, SCREEN)
    gram = gram + jnp.where(iota((SCREEN, SCREEN), 0) == iota((SCREEN, SCREEN), 1), 1.0, 0.0)
    state = newton_start([gram], [1.0])
    state = newton_steps([gram], state, 5)
    sent_residue(gg_copy)
    for half in range(2):
        sent_residue(zs_copy, half)
    wait_class(zg_copy)
    octant = iota((1, SCREEN), 1)
    octant = jnp.where(octant < GROUP, (octant * 10923) >> 18, -1)
    across = []
    for a in range(N_PAIR):
        b = ((zl + a // 4) % 2) * 4 + ((yl + (a // 2) % 2) % 2) * 2 + (xl + a % 2) % 2
        both = zg[b].astype(F32)
        across.append(both[2 * KNOTS:3 * KNOTS] + both[3 * KNOTS:4 * KNOTS])
    zrow = []
    for a in range(N_PAIR):
        both = zg[a].astype(F32)
        here = both[0:KNOTS] + both[KNOTS:2 * KNOTS]
        for m in range(N_PAIR):
            here = here + jnp.where(octant == m, across[a ^ m], 0.0)
        zrow.append(here[:, 0:GROUP])
    zhi, zlo = split2(jnp.concatenate(zrow, axis=1))
    both = nt(jnp.concatenate([zhi, zlo], axis=0), lhs[...])
    wt = both[0:KNOTS] + both[KNOTS:2 * KNOTS]
    w0 = wt[:, 0:DATES] - p3t(wt[:, F0_AT:F1_AT], c0)
    q = p3t(w0, ends)
    for n in range(4):
        lo = n * OWN
        wq[n] = jnp.concatenate([
            q[:, 0:NB], q[:, NB + lo:NB + lo + OWN], q[:, NB + NEAR + lo:NB + NEAR + lo + OWN],
            jnp.zeros((KNOTS, 128 - NB - 2 * OWN), F32),
            wt[:, F1_AT:D1_AT], wt[:, D1_AT + lo:D1_AT + lo + OWN], jnp.zeros((KNOTS, 128 - NB - OWN), F32),
        ], axis=1)
    start_residue(w_copy)
    wg[me] = wq[me // 4]
    state = newton_steps([gram], state, 4)
    (h,) = newton_end([gram], state)
    sent_class(zg_copy)
    mine = zl * 2 + yl
    c1_own = c1[0:OWN]
    for n in range(1, 4):
        c1_own = jnp.where(mine == n, c1[n * OWN:(n + 1) * OWN], c1_own)
    totals = []
    for half in range(2):
        wait_class(f_copy, half)
        total = cr[half, 0].astype(F32)
        for p in range(1, N_PAIR):
            total = total + cr[half, p].astype(F32)
        totals.append(total)
    total = jnp.concatenate(totals, axis=1)
    wait_residue(w_copy)

    wt_ref[...] = wg[...].reshape(SCREEN, 2 * 128)
    h_ref[...] = h
    total_ref[...] = total
    kn_ref[...] = bhi[group]
    c1_ref[...] = c1_own

    sent_residue(w_copy)
    for half in range(2):
        sent_class(f_copy, half)


def tail_kernel(wt_ref, h_ref, total_ref, kn_ref, c1_ref, co_ref, sc_ref):
    wt, h = wt_ref[...], h_ref[...]
    q0 = wt[:, 0:128]
    q1 = p3(h, q0)
    ehi, elo = split2(q1[:, 0:NB].T)
    knots = kn_ref[...]
    co_ref[...] = total_ref[...] - (nn(ehi, knots) + nn(elo, knots))
    step = wt[:, 128:128 + NB + OWN] - (q0[:, 0:NB + OWN] - q1[:, 0:NB + OWN])
    change = step[:, NB:] - p3t(step[:, 0:NB], c1_ref[...])
    s2 = q1[:, NB + OWN:NB + 2 * OWN] + p3(h, change)
    sc_ref[...] = s2.T[0:38]


def local(phases, pair_dates, weights, coords):
    vmem = pl.BlockSpec(memory_space=pltpu.VMEM)
    shape = jax.ShapeDtypeStruct
    dma = pltpu.SemaphoreType.DMA
    tiles, pairs = dma((N_TILE,)), dma((N_PAIR,))
    twos, halves, parts = dma((2, N_PAIR)), dma((2, N_TILE)), dma((2, N_TILE, PARTS))
    parts_out = pl.pallas_call(
        mega_kernel,
        out_shape=[
            shape((SCREEN, 2 * 128), F32), shape((SCREEN, SCREEN), F32), shape((NB, PIX), F32),
            shape((SCREEN, PIX), BF16), shape((OWN, NB), F32),
        ],
        in_specs=[pl.BlockSpec(memory_space=pl.ANY)] + [vmem] * 3,
        out_specs=[vmem] * 5,
        scratch_shapes=[
            pltpu.VMEM((PAIRS, NPIX), BF16),
            dma,
            pltpu.VMEM((N_PAIR, PIX // 128, 128), jnp.int32),
            pltpu.VMEM((2, N_TILE, 6, SLOTS, HALF), BF16),
            pltpu.VMEM((2, N_TILE, 6, SLOTS, HALF), BF16),
            pltpu.VMEM((N_PAIR, SCREEN, PIX), BF16),
            pltpu.VMEM((SCREEN, PIX), BF16),
            pltpu.VMEM((2, N_PAIR, SCREEN, HALF), BF16),
            pltpu.VMEM((N_TILE, KNOTS, SCREEN), F32),
            pltpu.VMEM((N_TILE, KNOTS, SCREEN), F32),
            pltpu.VMEM((N_TILE, KNOTS, SCREEN), F32),
            pltpu.VMEM((2, N_TILE, KNOTS, SCREEN), F32),
            pltpu.VMEM((2, N_TILE, KNOTS, SCREEN), F32),
            pltpu.VMEM((N_PAIR, 4 * KNOTS, SCREEN), BF16),
            pltpu.VMEM((4, KNOTS, 2 * 128), F32),
            pltpu.VMEM((N_TILE, KNOTS, 2 * 128), F32),
            pltpu.VMEM((2, N_PAIR, NB, HALF), BF16),
            pltpu.VMEM((2, N_PAIR, NB, HALF), BF16),
            pltpu.VMEM((ROWS, KP), BF16),
            pairs, pairs, parts, parts, tiles, tiles, tiles, tiles,
            halves, halves, pairs, pairs, tiles, tiles, twos, twos,
        ],
        compiler_params=pltpu.CompilerParams(
            collective_id=0, has_side_effects=True, vmem_limit_bytes=VMEM_LIMIT
        ),
        name="mega",
    )(phases, coords, pair_dates.T, weights)
    return pl.pallas_call(
        tail_kernel,
        out_shape=[shape((NB, PIX), F32), shape((38, SCREEN), F32)],
        in_specs=[vmem] * 5,
        out_specs=[vmem] * 2,
        compiler_params=pltpu.CompilerParams(vmem_limit_bytes=VMEM_LIMIT),
        name="tail",
    )(*parts_out)


def solution(mesh):
    return jax.shard_map(
        local,
        mesh=mesh,
        in_specs=(P(("pair", "tile"), None), P(), P(), P(None, ("pair", "tile"))),
        out_specs=(P(None, ("pair", "tile")), P("pair", None)),
        check_vma=False,
    )
```

```python
import functools

import jax
import jax.numpy as jnp
from jax import lax
from jax.experimental import pallas as pl
from jax.experimental.pallas import tpu as pltpu
from jax.sharding import PartitionSpec as P

MESH = pl.DeviceIdType.MESH
HI = lax.Precision.HIGHEST
F32, BF16 = jnp.float32, jnp.bfloat16
DATES, NB, KNOTS, FRAME, SCREEN = 304, 32, 16, 4096, 256
PAIRS, SLOTS, DEVICES, PIX = 12, 16, 128, 1024
NPIX = DEVICES * PIX
N_TILE = 16
EVEN, ODD = 160, 144
KP = PAIRS * DEVICES
GROUP = PAIRS * N_TILE
OWN = 40
N_PAIR = 8
NEAR = 160
F0_AT, F1_AT, D1_AT, ROWS = 384, 416, 448, 608
HALF = PIX // 2
PARTS = 1
VMEM_LIMIT = 60 * 1024 * 1024

def nn(a, b, precision=None):
    return lax.dot_general(a, b, (((1,), (0,)), ((), ())), precision=precision, preferred_element_type=F32)

def nt(a, b, precision=None):
    return lax.dot_general(a, b, (((1,), (1,)), ((), ())), precision=precision, preferred_element_type=F32)

def tn(a, b, precision=None):
    return lax.dot_general(a, b, (((0,), (0,)), ((), ())), precision=precision, preferred_element_type=F32)

def split2(x):
    hi = x.astype(BF16)
    return hi, (x - hi.astype(F32)).astype(BF16)

def spline(s):
    a = jnp.abs(s)
    r = jnp.maximum(2.0 - a, 0.0)
    q = jnp.maximum(1.0 - a, 0.0)
    return (r * r * r - 4.0 * (q * q * q)) * (1.0 / 6.0)

def date_of(r):
    rr = jnp.where(r < EVEN, r, r - EVEN)
    base = ((rr >> 4) << 5) + (rr & 15)
    return jnp.where(r < EVEN, base, base + 16)

def iota(shape, dim):
    return lax.broadcasted_iota(jnp.int32, shape, dim)

def block_inverse(c):
    n = c.shape[1]
    row = iota((1, n, n), 1)
    col = iota((1, n, n), 2)
    for j in range(n):
        prow = c[:, j:j + 1, :]
        pcol = c[:, :, j:j + 1]
        d = 1.0 / c[:, j:j + 1, j:j + 1]
        newrow = jnp.where(col[:, :1, :] == j, 1.0, prow) * d
        base = jnp.where(col == j, 0.0, c)
        c = jnp.where(row == j, newrow, base - pcol * newrow)
    return c

def product3(a, b):
    (ah, al), (bh, bl) = a, b
    return nn(ah, bh) + (nn(ah, bl) + nn(al, bh))

def p3(a, b):
    return product3(split2(a), split2(b))

def p3t(a, b):
    (ah, al), (bh, bl) = split2(a), split2(b)
    return nt(ah, bh) + (nt(ah, bl) + nt(al, bh))

def newton_start(mats, floors):
    xs, lows = [], []
    for m, floor in zip(mats, floors):
        n = m.shape[0]
        top = jnp.max(jnp.sum(jnp.abs(m), axis=1, keepdims=True), axis=0, keepdims=True)
        c = 2.0 / (top + floor)
        low = c * floor
        ab = low * (2.0 - low)
        k = 2.0 / (1.0 + ab)
        diagonal = iota((n, n), 0) == iota((n, n), 1)
        xs.append((jnp.where(diagonal, 2.0, 0.0) - m * c) * (c * k))
        lows.append(ab * k)
    return xs, lows

def newton_steps(mats, state, steps):
    parts = [split2(m) for m in mats]
    def body(_, carry):
        xs, lows = carry
        nx, nl = [], []
        halves = [split2(x) for x in xs]
        ys = [product3(m, x) for m, x in zip(parts, halves)]
        for x, y, low in zip(halves, ys, lows):
            n = y.shape[0]
            ab = low * (2.0 - low)
            k = 2.0 / (1.0 + ab)
            eye = jnp.where(iota((n, n), 0) == iota((n, n), 1), 2.0, 0.0)
            nx.append(product3(x, split2(eye - y)) * k)
            nl.append(ab * k)
        return nx, nl
    return lax.fori_loop(0, steps, body, state)

def newton_end(mats, state):
    out = []
    for m, x in zip(mats, state[0]):
        n = m.shape[0]
        eye = jnp.where(iota((n, n), 0) == iota((n, n), 1), 2.0, 0.0)
        out.append(nn(x, eye - nn(m, x, HI), HI))
    return out

def near_dates(quarter):
    row, col = iota((NEAR, DATES), 0), iota((NEAR, DATES), 1)
    q = jnp.where(row >= 2 * OWN, jnp.where(row >= 3 * OWN, 3, 2), jnp.where(row >= OWN, 1, 0))
    i = row - OWN * q
    return jnp.where((38 * (4 * quarter + q) + i == date_of(col)) & (i < 38), 1.0, 0.0)

def by_group(x):
    lane = iota((8, KP), 1)
    t = (lane * 21846) >> 18
    delta = ((t >> 4) & 3) - ((t >> 2) & 3)
    out = x
    for d in (-3, -2, -1, 1, 2, 3):
        out = jnp.where(delta == d, pltpu.roll(x, (144 * d) % KP, 1), out)
    return out

def incidence_rows(pd):
    t = date_of(iota((DATES, KP), 0))
    later = jnp.where(t == pd[1:2, :], 1.0, 0.0)
    return later - jnp.where(t == pd[0:1, :], 1.0, 0.0)

def design_rows(at16):
    tt = date_of(iota((DATES, NB), 0)).astype(F32) * ((NB - 3.0) / (DATES - 1.0))
    t1 = spline(tt - (iota((DATES, NB), 1).astype(F32) - 1.0)).T
    a = t1.astype(BF16)
    r = t1 - a.astype(F32)
    b, c = split2(r)
    return nn(a, at16) + nn(b, at16) + nn(c, at16)

def normal_parts(at, at16, xt, w):
    eye = jnp.where(iota((DATES, DATES), 0) == iota((DATES, DATES), 1), 1.0, 0.0)
    fold = jnp.where((iota((EVEN, 16), 0) & 15) == iota((EVEN, 16), 1), 1.0, 0.0)
    mask = (iota((EVEN, EVEN), 0) >> 4) == (iota((EVEN, EVEN), 1) >> 4)
    ns, comps, fits = [], [], []
    for i in range(2):
        wi = w[i:i + 1, :]
        hi, lo = split2(wi)
        n = nt((at * hi.astype(F32)).astype(BF16), at16) + nt((at * lo.astype(F32)).astype(BF16), at16) + eye
        ns.append(n)
        comps.append(nn(jnp.where(mask, n[:EVEN, :EVEN], 0.0), fold, HI).reshape(10, 16, 16))
        fits.append(nt(xt * wi, xt, HI) + jnp.where(iota((NB, NB), 0) == iota((NB, NB), 1), 0.5, 0.0))
    return ns, comps, fits

def eliminate_even(ns, comps):
    fold = jnp.where((iota((EVEN, 16), 0) & 15) == iota((EVEN, 16), 1), 1.0, 0.0)
    mask = (iota((EVEN, EVEN), 0) >> 4) == (iota((EVEN, EVEN), 1) >> 4)
    inv = block_inverse(jnp.concatenate(comps, axis=0))
    firsts, links, schurs = [], [], []
    for i in range(2):
        compact = inv[10 * i:10 * i + 10].reshape(EVEN, 16)
        first = jnp.where(mask, nt(compact, fold, HI), 0.0)
        e = ns[i][:EVEN, EVEN:]
        y = nn(first, e, HI)
        schurs.append(ns[i][EVEN:, EVEN:] - tn(e, y, HI))
        firsts.append(first)
        links.append(y)
    return firsts, links, schurs

def full_inverse(first, link, last):
    right = p3(link, last)
    top = jnp.concatenate([first + p3t(right, link), -right], axis=1)
    bottom = jnp.concatenate([-right.T, last], axis=1)
    return jnp.concatenate([top, bottom], axis=0)

def date_solve(inverse, at16, wi):
    hi, lo = split2(inverse)
    return ((nn(hi, at16) + nn(lo, at16)) * wi).astype(BF16)

def spread_own(group_of_residue):
    row, col = iota((KP, SCREEN), 0), iota((KP, SCREEN), 1)
    group = group_of_residue(iota((1, SCREEN), 1) >> 4)
    inside = (col & 15) < PAIRS
    return jnp.where((row == GROUP * group + PAIRS * (col >> 4) + (col & 15)) & inside, 1.0, 0.0).astype(BF16)

def squeeze():
    row, col = iota((SCREEN, SCREEN), 0), iota((SCREEN, SCREEN), 1)
    inside = (row & 15) < PAIRS
    return jnp.where((col == PAIRS * (row >> 4) + (row & 15)) & inside, 1.0, 0.0).astype(BF16)

def knot_rows(code, centers):
    scale = (KNOTS - 3.0) / FRAME
    rows = spline((code >> 16).astype(F32) * scale - centers)
    cols = spline((code & 65535).astype(F32) * scale - centers)
    return rows, cols


def mega_kernel(
    ph_hbm, ck_ref, pd_ref, w_ref, wt_ref, h_ref, total_ref, kn_ref, c1_ref,
    ph_ref, ph_sem, cg, sb, rb, bhi, blo_ref, ybuf, gs, gr, gg, zs, zr, zg, wq, wg, cp, cr, lhs,
    c_send, c_recv, y_send, y_recv, gs_send, gs_recv, gg_send, gg_recv,
    zs_send, zs_recv, zg_send, zg_recv, w_send, w_recv, f_send, f_recv,
):
    pair, tile = lax.axis_index("pair"), lax.axis_index("tile")
    zh, zl, yl = pair >> 2, (pair >> 1) & 1, pair & 1
    yh, xh, xl, core = tile >> 3, (tile >> 2) & 1, (tile >> 1) & 1, tile & 1
    me = zl * 8 + yl * 4 + xl * 2 + core
    group = zh * 4 + yh * 2 + xh

    def place(a, r):
        return (a >> 2) * 4 + (r >> 2), ((a >> 1) & 1) * 8 + (a & 1) * 4 + (r & 3)

    def group_at(r, half):
        if half == 0:
            return group
        return (
            ((zh + zl + (r >> 3)) & 1) * 4 + ((yh + yl + (r >> 2)) & 1) * 2 + ((xh + xl + (r >> 1)) & 1)
        )

    def residue_peer(i):
        t = me + i
        return jnp.where(t >= N_TILE, t - N_TILE, t)

    def class_peer(i):
        t = group + i
        return jnp.where(t >= N_PAIR, t - N_PAIR, t)

    def residue_far(i):
        k = N_TILE - i
        return (
            ((zl + (k >> 3)) & 1) * 8 + ((yl + (k >> 2)) & 1) * 4 + ((xl + (k >> 1)) & 1) * 2 + ((core + k) & 1)
        )

    def class_far(i):
        k = N_PAIR - i
        return ((zh + (k >> 2)) & 1) * 4 + ((yh + (k >> 1)) & 1) * 2 + ((xh + k) & 1)

    def loop(lo, hi, f):
        def body(i, carry):
            f(i)
            return carry
        lax.fori_loop(lo, hi, body, 0)

    def to_residue(src, dst, send, recv, other, half=0):
        return pltpu.make_async_remote_copy(
            src_ref=src, dst_ref=dst, send_sem=send, recv_sem=recv,
            device_id=place(group_at(other, half), other), device_id_type=MESH,
        )

    def to_class(src, dst, send, recv, other, slot):
        return pltpu.make_async_remote_copy(
            src_ref=src, dst_ref=dst.at[slot], send_sem=send.at[other], recv_sem=recv.at[slot],
            device_id=place(other, me), device_id_type=MESH,
        )

    def c_copy(other, slot):
        return to_class(cg.at[group], cg, c_send, c_recv, other, slot)

    def y_copy(other, slot, half, part):
        rows = pl.ds(6 * part, 6)
        return to_residue(
            sb.at[half, other, rows], rb.at[half, slot, rows],
            y_send.at[half, other, part], y_recv.at[half, slot, part], other, half,
        )

    def gs_copy(other, slot):
        return to_residue(gs.at[other], gr.at[slot], gs_send.at[other], gs_recv.at[slot], other)

    def gg_copy(other, slot):
        return to_residue(gg.at[me], gg.at[slot], gg_send.at[other], gg_recv.at[slot], other)

    def zs_copy(other, slot, half):
        return to_residue(
            zs.at[half, other], zr.at[half, slot], zs_send.at[half, other], zs_recv.at[half, slot], other, half
        )

    def zg_copy(other, slot):
        return to_class(zg.at[group], zg, zg_send, zg_recv, other, slot)

    def w_copy(other, slot):
        return to_residue(wq.at[other // 4], wg.at[slot], w_send.at[other], w_recv.at[slot], other)

    def f_copy(other, slot, half):
        return to_class(cp.at[half, other], cr.at[half], f_send.at[half], f_recv.at[half], other, slot)

    def start_residue(copy, *more):
        loop(1, N_TILE, lambda i: copy(residue_far(i), me, *more).start())

    def wait_residue(copy, *more):
        loop(1, N_TILE, lambda i: copy(residue_peer(i), residue_peer(i), *more).wait_recv())

    def sent_residue(copy, *more):
        loop(1, N_TILE, lambda i: copy(residue_peer(i), me, *more).wait_send())

    def sent_class(copy, *more):
        loop(1, N_PAIR, lambda i: copy(class_peer(i), group, *more).wait_send())

    def start_class(copy, *more):
        loop(1, N_PAIR, lambda i: copy(class_far(i), group, *more).start())

    def wait_class(copy, *more):
        loop(1, N_PAIR, lambda i: copy(class_peer(i), class_peer(i), *more).wait_recv())

    load = pltpu.make_async_copy(ph_hbm, ph_ref, ph_sem)
    load.start()
    barrier = pltpu.get_barrier_semaphore()

    def greet(where):
        pl.semaphore_signal(barrier, inc=1, device_id=where, device_id_type=MESH)

    loop(1, N_PAIR, lambda i: greet(place(class_far(i), me)))
    for half in range(2):
        loop(1, N_TILE, lambda i, half=half: greet(place(group_at(residue_far(i), half), residue_far(i))))

    pl.semaphore_wait(barrier, 2 * N_TILE + N_PAIR - 3)

    code = ck_ref[0:1, :] * 65536 + ck_ref[1:2, :]
    cg[group] = jnp.concatenate([code[:, i * 128:(i + 1) * 128] for i in range(PIX // 128)], axis=0)
    start_class(c_copy)

    load.wait()

    def pack(other, half, dst):
        blocks = []
        for a in range(N_PAIR):
            p, t = place(a, other)
            first = pl.multiple_of((p * N_TILE + t) * PIX + half * HALF, HALF)
            blocks.append(ph_ref[:, pl.ds(first, HALF)].astype(F32))
        for a in range(4):
            two = jnp.concatenate([blocks[2 * a][0:8], blocks[2 * a + 1][0:8]], axis=0)
            dst[a] = two.astype(BF16)
        for a in range(2):
            four = jnp.concatenate([blocks[4 * a + q][8:12] for q in range(4)], axis=0)
            dst[4 + a] = four.astype(BF16)

    def y_start(i, half):
        other = residue_peer(i)
        pack(other, half, sb.at[half, other])
        for part in range(PARTS):
            y_copy(other, me, half, part).start()

    for half in range(2):
        loop(1, N_TILE, lambda i, half=half: y_start(i, half))
    for half in range(2):
        pack(me, half, rb.at[half, me])

    rows = jnp.concatenate([pd_ref[...].astype(F32), w_ref[...], jnp.zeros((4, KP), F32)], axis=0)
    rows = by_group(rows)
    w = rows[2:4, :]
    at = incidence_rows(rows[0:2, :].astype(jnp.int32))
    at16 = at.astype(BF16)
    xt = design_rows(at16)
    normals, evens, fits = normal_parts(at, at16, xt, w)
    firsts, links, schurs = eliminate_even(normals, evens)
    lasts = newton_start(schurs + fits, [1.0, 1.0, 0.5, 0.5])
    lasts = newton_steps(schurs + fits, lasts, 8)
    last0, last1, f0, f1 = newton_end(schurs + fits, lasts)

    sel = near_dates(zh)
    fit0 = (p3(f0, xt) * w[0:1, :]).astype(BF16)
    fit1 = (p3(f1, xt) * w[1:2, :]).astype(BF16)
    fit_own = [nn(fit1, spread_own(functools.partial(group_at, half=half))).astype(BF16) for half in range(2)]

    wait_class(c_copy)
    centers = iota((KNOTS, 1), 0).astype(F32) - 1.0

    def knots(p, carry):
        g1, g2 = carry
        for i in range(PIX // 128):
            rows, cols = knot_rows(cg[p, i:i + 1, :], centers)
            lanes = pl.ds(i * 128, 128)
            for m in range(KNOTS):
                hi, lo = split2(rows[m:m + 1, :] * cols)
                bhi[p, m * KNOTS:(m + 1) * KNOTS, lanes] = hi
                blo_ref[m * KNOTS:(m + 1) * KNOTS, lanes] = lo
        hi = bhi[p]
        return g1 + nt(hi, hi), g2 + nt(hi, blo_ref[...])

    zero = jnp.zeros((SCREEN, SCREEN), F32)
    g1, g2 = lax.fori_loop(0, N_PAIR, knots, (zero, zero))
    gs[...] = (g1 + g2 + g2.T).reshape(N_TILE, KNOTS, SCREEN)
    start_residue(gs_copy)
    gr[me] = gs[me]


    def unpack(t, half):
        rest = [rb[half, t, 4 + a].astype(F32) for a in range(2)]
        for a in range(4):
            two = rb[half, t, a].astype(F32)
            for b in range(2):
                p = 2 * a + b
                low = rest[p // 4][4 * (p % 4):4 * (p % 4) + 4]
                block = jnp.concatenate([two[8 * b:8 * b + 8], low, jnp.zeros((4, HALF), F32)], axis=0)
                ybuf[half, p, pl.ds(pl.multiple_of(t * SLOTS, SLOTS), SLOTS), :] = block.astype(BF16)

    def y_arrive(i, half):
        other = residue_peer(i)
        for part in range(PARTS):
            y_copy(other, other, half, part).wait_recv()
        unpack(other, half)

    def z_body(p, acc, half):
        y = ybuf[half, p]
        return acc + nt(bhi[p, :, half * HALF:(half + 1) * HALF], y)

    for half in range(2):
        unpack(me, half)
        loop(1, N_TILE, lambda i, half=half: y_arrive(N_TILE - i, half))
        zt = lax.fori_loop(0, N_PAIR, functools.partial(z_body, half=half), zero)
        zs[half] = zt.reshape(N_TILE, KNOTS, SCREEN)
        start_residue(zs_copy, half)
        zr[half, me] = zs[half, me]
    sent_class(c_copy)
    sent_residue(gs_copy)
    for half in range(2):
        for part in range(PARTS):
            sent_residue(y_copy, half, part)
    wait_residue(gs_copy)
    gsum = gr[0]
    for t in range(1, N_TILE):
        gsum = gsum + gr[t]
    gg[me] = gsum
    start_residue(gg_copy)

    d0 = date_solve(full_inverse(firsts[0], links[0], last0), at16, w[0:1, :])
    d1 = date_solve(p3(sel, full_inverse(firsts[1], links[1], last1)), at16, w[1:2, :])
    lhs[0:DATES] = d0
    lhs[DATES:F0_AT] = jnp.zeros((F0_AT - DATES, KP), BF16)
    lhs[F0_AT:D1_AT] = jnp.concatenate([fit0, fit1], axis=0)
    lhs[D1_AT:ROWS] = d1

    sums = []
    for half in range(2):
        wait_residue(zs_copy, half)
        zsum = zr[half, 0]
        for t in range(1, N_TILE):
            zsum = zsum + zr[half, t]
        sums.extend(split2(zsum))
    zg[group] = nn(jnp.concatenate(sums, axis=0), squeeze()).astype(BF16)
    start_class(zg_copy)
    for half in range(2):
        def fit_body(p, half=half):
            cp[half, p] = nn(fit_own[half], ybuf[half, p]).astype(BF16)

        loop(0, N_PAIR, fit_body)
        start_class(f_copy, half)
        cr[half, group] = cp[half, group]
    xhi, xlo = split2(xt)
    c0 = nt(d0, xhi) + nt(d0, xlo)
    c1 = nt(d1, xhi) + nt(d1, xlo)
    ends = jnp.concatenate([nt(fit1, at16), nt(d1, at16), sel], axis=0)
    wait_residue(gg_copy)
    gram = gg[...].reshape(SCREEN, SCREEN)
    gram = gram + jnp.where(iota((SCREEN, SCREEN), 0) == iota((SCREEN, SCREEN), 1), 1.0, 0.0)
    state = newton_start([gram], [1.0])
    state = newton_steps([gram], state, 5)
    sent_residue(gg_copy)
    for half in range(2):
        sent_residue(zs_copy, half)
    wait_class(zg_copy)
    octant = iota((1, SCREEN), 1)
    octant = jnp.where(octant < GROUP, (octant * 10923) >> 18, -1)
    across = []
    for a in range(N_PAIR):
        b = ((zl + a // 4) % 2) * 4 + ((yl + (a // 2) % 2) % 2) * 2 + (xl + a % 2) % 2
        both = zg[b].astype(F32)
        across.append(both[2 * KNOTS:3 * KNOTS] + both[3 * KNOTS:4 * KNOTS])
    zrow = []
    for a in range(N_PAIR):
        both = zg[a].astype(F32)
        here = both[0:KNOTS] + both[KNOTS:2 * KNOTS]
        for m in range(N_PAIR):
            here = here + jnp.where(octant == m, across[a ^ m], 0.0)
        zrow.append(here[:, 0:GROUP])
    zhi, zlo = split2(jnp.concatenate(zrow, axis=1))
    both = nt(jnp.concatenate([zhi, zlo], axis=0), lhs[...])
    wt = both[0:KNOTS] + both[KNOTS:2 * KNOTS]
    w0 = wt[:, 0:DATES] - p3t(wt[:, F0_AT:F1_AT], c0)
    q = p3t(w0, ends)
    for n in range(4):
        lo = n * OWN
        wq[n] = jnp.concatenate([
            q[:, 0:NB], q[:, NB + lo:NB + lo + OWN], q[:, NB + NEAR + lo:NB + NEAR + lo + OWN],
            jnp.zeros((KNOTS, 128 - NB - 2 * OWN), F32),
            wt[:, F1_AT:D1_AT], wt[:, D1_AT + lo:D1_AT + lo + OWN], jnp.zeros((KNOTS, 128 - NB - OWN), F32),
        ], axis=1)
    start_residue(w_copy)
    wg[me] = wq[me // 4]
    state = newton_steps([gram], state, 4)
    (h,) = newton_end([gram], state)
    sent_class(zg_copy)
    mine = zl * 2 + yl
    c1_own = c1[0:OWN]
    for n in range(1, 4):
        c1_own = jnp.where(mine == n, c1[n * OWN:(n + 1) * OWN], c1_own)
    totals = []
    for half in range(2):
        wait_class(f_copy, half)
        total = cr[half, 0].astype(F32)
        for p in range(1, N_PAIR):
            total = total + cr[half, p].astype(F32)
        totals.append(total)
    total = jnp.concatenate(totals, axis=1)
    wait_residue(w_copy)

    wt_ref[...] = wg[...].reshape(SCREEN, 2 * 128)
    h_ref[...] = h
    total_ref[...] = total
    kn_ref[...] = bhi[group]
    c1_ref[...] = c1_own

    sent_residue(w_copy)
    for half in range(2):
        sent_class(f_copy, half)


def tail_kernel(wt_ref, h_ref, total_ref, kn_ref, c1_ref, co_ref, sc_ref):
    wt, h = wt_ref[...], h_ref[...]
    q0 = wt[:, 0:128]
    q1 = p3(h, q0)
    ehi, elo = split2(q1[:, 0:NB].T)
    knots = kn_ref[...]
    co_ref[...] = total_ref[...] - (nn(ehi, knots) + nn(elo, knots))
    step = wt[:, 128:128 + NB + OWN] - (q0[:, 0:NB + OWN] - q1[:, 0:NB + OWN])
    change = step[:, NB:] - p3t(step[:, 0:NB], c1_ref[...])
    s2 = q1[:, NB + OWN:NB + 2 * OWN] + p3(h, change)
    sc_ref[...] = s2.T[0:38]


def local(phases, pair_dates, weights, coords):
    vmem = pl.BlockSpec(memory_space=pltpu.VMEM)
    shape = jax.ShapeDtypeStruct
    dma = pltpu.SemaphoreType.DMA
    tiles, pairs = dma((N_TILE,)), dma((N_PAIR,))
    twos, halves, parts = dma((2, N_PAIR)), dma((2, N_TILE)), dma((2, N_TILE, PARTS))
    parts_out = pl.pallas_call(
        mega_kernel,
        out_shape=[
            shape((SCREEN, 2 * 128), F32), shape((SCREEN, SCREEN), F32), shape((NB, PIX), F32),
            shape((SCREEN, PIX), BF16), shape((OWN, NB), F32),
        ],
        in_specs=[pl.BlockSpec(memory_space=pl.ANY)] + [vmem] * 3,
        out_specs=[vmem] * 5,
        scratch_shapes=[
            pltpu.VMEM((PAIRS, NPIX), BF16),
            dma,
            pltpu.VMEM((N_PAIR, PIX // 128, 128), jnp.int32),
            pltpu.VMEM((2, N_TILE, 6, SLOTS, HALF), BF16),
            pltpu.VMEM((2, N_TILE, 6, SLOTS, HALF), BF16),
            pltpu.VMEM((N_PAIR, SCREEN, PIX), BF16),
            pltpu.VMEM((SCREEN, PIX), BF16),
            pltpu.VMEM((2, N_PAIR, SCREEN, HALF), BF16),
            pltpu.VMEM((N_TILE, KNOTS, SCREEN), F32),
            pltpu.VMEM((N_TILE, KNOTS, SCREEN), F32),
            pltpu.VMEM((N_TILE, KNOTS, SCREEN), F32),
            pltpu.VMEM((2, N_TILE, KNOTS, SCREEN), F32),
            pltpu.VMEM((2, N_TILE, KNOTS, SCREEN), F32),
            pltpu.VMEM((N_PAIR, 4 * KNOTS, SCREEN), BF16),
            pltpu.VMEM((4, KNOTS, 2 * 128), F32),
            pltpu.VMEM((N_TILE, KNOTS, 2 * 128), F32),
            pltpu.VMEM((2, N_PAIR, NB, HALF), BF16),
            pltpu.VMEM((2, N_PAIR, NB, HALF), BF16),
            pltpu.VMEM((ROWS, KP), BF16),
            pairs, pairs, parts, parts, tiles, tiles, tiles, tiles,
            halves, halves, pairs, pairs, tiles, tiles, twos, twos,
        ],
        compiler_params=pltpu.CompilerParams(
            collective_id=0, has_side_effects=True, vmem_limit_bytes=VMEM_LIMIT
        ),
        name="mega",
    )(phases, coords, pair_dates.T, weights)
    return pl.pallas_call(
        tail_kernel,
        out_shape=[shape((NB, PIX), F32), shape((38, SCREEN), F32)],
        in_specs=[vmem] * 5,
        out_specs=[vmem] * 2,
        compiler_params=pltpu.CompilerParams(vmem_limit_bytes=VMEM_LIMIT),
        name="tail",
    )(*parts_out)


def solution(mesh):
    return jax.shard_map(
        local,
        mesh=mesh,
        in_specs=(P(("pair", "tile"), None), P(), P(), P(None, ("pair", "tile"))),
        out_specs=(P(None, ("pair", "tile")), P("pair", None)),
        check_vma=False,
    )
```
